32 devices in a mesh: seq: 8 (over z, y), row: 4 (over x, core).
Axes of the slice: x: 2, y: 2, z: 4, core: 2. Of those that a mesh axis runs over, the one named last changes fastest.
Arguments:
- inputs: float32 [8, 1024, 1024], P('row', 'seq'), may hold values from -6 to 6
- cotangent: float32 [8, 1024, 1024], P('row', 'seq'), may hold values from -6 to 6
- segments: int32 [8, 1024], P('row', 'seq'), may hold values from 0 to 4, as said below
- norm1_gain: bfloat16 [1024], P(('seq', 'row')), may hold values from 0.5 to 1.5
- input_proj: bfloat16 [1024, 1536], P(('seq', 'row')), may hold values from -0.1875 to 0.1875
- branch_proj: bfloat16 [1024, 1536], P(('seq', 'row')), may hold values from -0.1875 to 0.1875
- conv_weight: bfloat16 [4, 1536], P(None, ('seq', 'row')), may hold values from -3 to 3
- conv_bias: bfloat16 [1536], P(('seq', 'row')), may hold values from -2 to 2
- recur_gate: bfloat16 [1536, 128], P(('seq', 'row')), may hold values from -0.5 to 0.5
- input_gate: bfloat16 [1536, 128], P(('seq', 'row')), may hold values from -0.5 to 0.5
- recur_bias: bfloat16 [1536], P(('seq', 'row')), may hold values from -2 to 2
- input_bias: bfloat16 [1536], P(('seq', 'row')), may hold values from -2 to 2
- decay_param: bfloat16 [1536], P(('seq', 'row')), may hold values from -16 to -3
- output_proj: bfloat16 [1536, 1024], P(('seq', 'row')), may hold values from -0.4375 to 0.4375
- norm2_gain: bfloat16 [1024], P(('seq', 'row')), may hold values from 0.5 to 1.5
- mlp_gate: bfloat16 [1024, 3072], P(('seq', 'row')), may hold values from -0.1875 to 0.1875
- mlp_up: bfloat16 [1024, 3072], P(('seq', 'row')), may hold values from -0.1875 to 0.1875
- mlp_down: bfloat16 [3072, 1024], P(('seq', 'row')), may hold values from -0.21875 to 0.21875
Outputs:
- result: float32 [8, 1024, 1024], P('row', 'seq')
- grad_inputs: float32 [8, 1024, 1024], P('row', 'seq')
- grad_norm1_gain: float32 [1024], P(('seq', 'row'))
- grad_input_proj: float32 [1024, 1536], P(('seq', 'row'))
- grad_branch_proj: float32 [1024, 1536], P(('seq', 'row'))
- grad_conv_weight: float32 [4, 1536], P(None, ('seq', 'row'))
- grad_conv_bias: float32 [1536], P(('seq', 'row'))
- grad_recur_gate: float32 [1536, 128], P(('seq', 'row'))
- grad_input_gate: float32 [1536, 128], P(('seq', 'row'))
- grad_recur_bias: float32 [1536], P(('seq', 'row'))
- grad_input_bias: float32 [1536], P(('seq', 'row'))
- grad_decay_param: float32 [1536], P(('seq', 'row'))
- grad_output_proj: float32 [1536, 1024], P(('seq', 'row'))
- grad_norm2_gain: float32 [1024], P(('seq', 'row'))
- grad_mlp_gate: float32 [1024, 3072], P(('seq', 'row'))
- grad_mlp_up: float32 [1024, 3072], P(('seq', 'row'))
- grad_mlp_down: float32 [3072, 1024], P(('seq', 'row'))
The draws below stay inside these ranges and needn't reach their ends.
Inputs may be any that keep to these rules, and one draw needn't show every extreme that they name: `segments`: within a row the numbers never fall and rise by one at each of four document starts. In even rows two documents start among the first 128 tokens and two among the last 128 tokens. In odd rows one starts among the first 128 tokens, one among the last 128, and the two others lie in the token ranges of the two middle indices of seq, each at least 3 tokens after the range's start.
All inputs are finite; a program needn't handle non-finite values.
Results may differ from the reference program's by a relative error of at most 0.014.
Values may be sent and summed in bfloat16 or wider, within the bound.
No kernel may reach another device: no remote copies, remote signals or barrier semaphores. Data moves between devices by JAX's collectives and lax.ppermute only.
A program may use at most 320 MiB of HBM per device.

```python
import math
import jax
import jax.numpy as jnp
from jax import lax

D = 1024
R = 1536
FF = 3072
BLK = 128
GROUP = 128
ROWS = 8
SEQ_LEN = 1024


def draw_segments(key, part):
    key = jax.random.fold_in(key, 11)
    keys = jax.random.split(key, 8)
    devices_along = SEQ_LEN // GROUP
    first_long = jax.random.randint(keys[0], (ROWS,), GROUP // 2, GROUP)
    early_start = jax.random.randint(keys[1], (ROWS,), 1, first_long)
    last_long = SEQ_LEN - GROUP + jax.random.randint(keys[2], (ROWS,), 1, GROUP // 2)
    late_start = jax.random.randint(keys[3], (ROWS,), last_long + 1, SEQ_LEN)
    odd_first = jax.random.randint(keys[4], (ROWS,), 1, GROUP)
    odd_second = (devices_along // 2 - 1) * GROUP + jax.random.randint(keys[5], (ROWS,), 3, GROUP)
    odd_third = devices_along // 2 * GROUP + jax.random.randint(keys[6], (ROWS,), 3, GROUP)
    odd_fourth = SEQ_LEN - GROUP + jax.random.randint(keys[7], (ROWS,), 1, GROUP)
    is_odd = jnp.arange(ROWS, dtype=jnp.int32) % 2 == 1
    start_one = jnp.where(is_odd, odd_first, early_start)
    start_two = jnp.where(is_odd, odd_second, first_long)
    start_three = jnp.where(is_odd, odd_third, last_long)
    start_four = jnp.where(is_odd, odd_fourth, late_start)
    position = jnp.arange(SEQ_LEN, dtype=jnp.int32)[None, :]
    total = (position >= start_one[:, None]).astype(jnp.int32)
    total = total + (position >= start_two[:, None]).astype(jnp.int32)
    total = total + (position >= start_three[:, None]).astype(jnp.int32)
    total = total + (position >= start_four[:, None]).astype(jnp.int32)
    return total


def draw_decay_param(key, part):
    key = jax.random.fold_in(key, 7)
    keys = jax.random.split(key, 3)
    share = 0.5
    slower = jax.random.uniform(keys[0], (R,), jnp.float32) < share
    slow_rate = jax.random.uniform(keys[1], (R,), jnp.float32, 0.02, 0.3) / SEQ_LEN
    fast_rate = jnp.exp(jax.random.uniform(keys[2], (R,), jnp.float32, math.log(0.005), math.log(0.02)))
    rate = jnp.where(slower, slow_rate, fast_rate)
    return jnp.log(jnp.expm1(rate)).astype(jnp.bfloat16)


def steps_of(key, extent, cuts, smallest, largest):
    def one(dim, parts):
        draws = jax.random.uniform(jax.random.fold_in(jax.random.fold_in(key, 6), dim), (parts,), jnp.float32, smallest / len(cuts), largest / len(cuts))
        return jnp.repeat(jnp.exp(draws), extent[dim] // parts).reshape((-1,) + (1,) * (len(extent) - dim - 1))

    factor_of = one(*cuts[0])
    for cut in cuts[1:]:
        factor_of = factor_of * one(*cut)
    return factor_of


def noise(rng, shape, spread, most, pieces=(), kind=jnp.bfloat16):
    factor_of = steps_of(rng, shape, pieces, -0.22, 0.18) if pieces else 1.0
    values = jax.random.normal(rng, shape, jnp.float32) * spread * factor_of
    return jnp.minimum(jnp.maximum(values, -most), most).astype(kind)


def setup_inputs(seed: int = 0) -> dict:
    arg_keys = jax.random.split(jax.random.key(seed), 19)
    return {
        "inputs": noise(arg_keys[0], (ROWS, SEQ_LEN, D), 1.0, 6.0, ((0, 4), (1, 8)), jnp.float32),
        "cotangent": noise(arg_keys[1], (ROWS, SEQ_LEN, D), 1.0, 6.0, ((0, 4), (1, 8)), jnp.float32),
        "segments": draw_segments(jax.random.fold_in(arg_keys[18], 71), 0),
        "norm1_gain": jnp.clip(1.0 + 0.1 * jax.random.normal(arg_keys[3], (D,), jnp.float32), 0.5, 1.5).astype(jnp.bfloat16),
        "input_proj": noise(arg_keys[4], (D, R), D ** -0.5, 0.1875, ((0, 32),)),
        "branch_proj": noise(arg_keys[5], (D, R), D ** -0.5, 0.1875, ((0, 32),)),
        "conv_weight": noise(arg_keys[6], (4, R), 0.5, 3.0, ((1, 32),)),
        "conv_bias": noise(arg_keys[7], (R,), 0.3, 2.0, ((0, 32),)),
        "recur_gate": noise(arg_keys[8], (R, BLK), BLK ** -0.5, 0.5, ((0, 32),)),
        "input_gate": noise(arg_keys[9], (R, BLK), BLK ** -0.5, 0.5, ((0, 32),)),
        "recur_bias": noise(arg_keys[10], (R,), 0.5, 2.0, ((0, 32),)),
        "input_bias": noise(arg_keys[11], (R,), 0.5, 2.0, ((0, 32),)),
        "decay_param": draw_decay_param(jax.random.fold_in(arg_keys[18], 71), 0),
        "output_proj": noise(arg_keys[13], (R, D), (R // 8) ** -0.5, 0.4375, ((0, 32),)),
        "norm2_gain": jnp.clip(1.0 + 0.1 * jax.random.normal(arg_keys[14], (D,), jnp.float32), 0.5, 1.5).astype(jnp.bfloat16),
        "mlp_gate": noise(arg_keys[15], (D, FF), D ** -0.5, 0.1875, ((0, 32),)),
        "mlp_up": noise(arg_keys[16], (D, FF), D ** -0.5, 0.1875, ((0, 32),)),
        "mlp_down": noise(arg_keys[17], (FF, D), (FF // 4) ** -0.5, 0.21875, ((0, 32),)),
    }


EPS = 1e-06
HIGH = lax.Precision.HIGHEST

@jax.custom_vjp
def low(v):
    return lax.optimization_barrier(v.astype(jnp.bfloat16)).astype(jnp.float32)

@jax.custom_vjp
def low_back(v):
    return v

def low_keep(v):
    return (low(v), None)

def low_pass(kept, grad):
    return (grad,)

def back_keep(v):
    return (v, None)

def back_low(kept, grad):
    return (low(grad),)
low.defvjp(low_keep, low_pass)
low_back.defvjp(back_keep, back_low)

def matmul(left, right):
    return jnp.dot(left, right, precision=HIGH, preferred_element_type=jnp.float32)

def normed(values, gain):
    return values * lax.rsqrt(lax.optimization_barrier(jnp.mean(values * values, axis=-1, keepdims=True)) + EPS) * gain

def block_mix(values, weight):
    block = weight.shape[1]
    heads = weight.shape[0] // block
    shaped = values.reshape(values.shape[0], heads, block)
    mixed = jnp.einsum('thi,hio->tho', shaped, weight.reshape(heads, block, block), precision=HIGH)
    return mixed.reshape(values.shape)

def gate_math(recur_pre, input_pre, conv_out, decay_param, reset):
    recur = jax.nn.sigmoid(recur_pre)
    admit = jax.nn.sigmoid(input_pre)
    log_decay = -8.0 * jax.nn.softplus(decay_param) * recur
    decay = jnp.exp(log_decay)
    scaled = jnp.where(reset[..., None], 1.0, jnp.sqrt(-jnp.expm1(2.0 * log_decay)))
    carried = jnp.where(reset[..., None], 0.0, decay)
    return (carried, scaled * admit * conv_out)

def affine(earlier, later):
    return (earlier[0] * later[0], later[0] * earlier[1] + later[1])

def row_forward(params, inputs, segments):
    norm1_gain, input_proj, branch_proj, conv_weight, conv_bias, recur_gate, input_gate, recur_bias, input_bias, decay_param, output_proj, norm2_gain, mlp_gate, mlp_up, mlp_down = params
    length = inputs.shape[0]
    first = low(normed(inputs, norm1_gain))
    mixer_in = low(low_back(matmul(first, input_proj)))
    branch = jax.nn.gelu(low_back(matmul(first, branch_proj)))
    padded = jnp.concatenate([jnp.zeros((3, mixer_in.shape[1]), mixer_in.dtype), mixer_in], axis=0)
    padded_ids = jnp.concatenate([jnp.full((3,), -1, jnp.int32), segments.astype(jnp.int32)])
    conv_sum = conv_bias
    for offset in range(4):
        same = (padded_ids[3 - offset:3 - offset + length] == segments).astype(inputs.dtype)
        conv_sum = conv_sum + conv_weight[offset] * padded[3 - offset:3 - offset + length] * same[:, None]
    conv_out = low(conv_sum)
    reset = padded_ids[2:2 + length] != segments
    recur_pre = low_back(block_mix(conv_out, recur_gate) + recur_bias)
    input_pre = low_back(block_mix(conv_out, input_gate) + input_bias)
    carried, driven = gate_math(recur_pre, input_pre, conv_out, decay_param, reset)
    through, state = lax.associative_scan(affine, (carried, driven), axis=0)
    mixed = low(state * branch)
    middle = inputs + low_back(matmul(mixed, output_proj))
    second = low(normed(middle, norm2_gain))
    gate_pre = low_back(matmul(second, mlp_gate))
    up_pre = low_back(matmul(second, mlp_up))
    hidden = low(jax.nn.gelu(gate_pre) * up_pre)
    return middle + low_back(matmul(hidden, mlp_down))

def reference(inputs, cotangent, segments, norm1_gain, input_proj, branch_proj, conv_weight, conv_bias, recur_gate, input_gate, recur_bias, input_bias, decay_param, output_proj, norm2_gain, mlp_gate, mlp_up, mlp_down):
    params = tuple((member.astype(jnp.float32) for member in (norm1_gain, input_proj, branch_proj, conv_weight, conv_bias, recur_gate, input_gate, recur_bias, input_bias, decay_param, output_proj, norm2_gain, mlp_gate, mlp_up, mlp_down)))

    def forward(values, weights):

        def one_row(paired):
            return row_forward(weights, paired[0], paired[1])
        return lax.map(jax.checkpoint(one_row), (values, segments))
    result, pullback = jax.vjp(forward, inputs, params)
    grad_inputs, grads = pullback(cotangent)
    return (result, grad_inputs, grads[0], grads[1], grads[2], grads[3], grads[4], grads[5], grads[6], grads[7], grads[8], grads[9], grads[10], grads[11], grads[12], grads[13], grads[14])
```

```python
import functools
import math

import jax
import jax.numpy as jnp
from jax import lax
from jax.experimental import pallas as pl
from jax.experimental.pallas import tpu as pltpu
from jax.sharding import PartitionSpec as P

EPS = 1e-06
BF = jnp.bfloat16
F32 = jnp.float32
AXES = ("seq", "row")
MIB = 1 << 20
TILE = 256
HALO = 8
GELU_C = math.sqrt(2.0 / math.pi)


class Place:
    def __init__(self):
        seq, row = lax.axis_size("seq"), lax.axis_size("row")
        ny = 1 << ((seq.bit_length() - 1) // 2)
        self.size = {"z": seq // ny, "y": ny, "x": row // 2, "c": 2}
        self.seq, self.row = seq, row
        s, r = lax.axis_index("seq"), lax.axis_index("row")
        self.s = s
        self.at = {"z": s // ny, "y": s % ny, "x": r // 2, "c": r % 2}
        self.stride = {"z": ny * row, "y": row, "x": 2, "c": 1}
        self.chips = seq * (row // 2)

    def swap(self, value, axis, distance):
        pairs = []
        for i in range(self.seq * self.row):
            place = (i // self.stride[axis]) % self.size[axis]
            pairs.append((i, i + ((place ^ distance) - place) * self.stride[axis]))
        return lax.ppermute(value, AXES, pairs)

    def along(self, value, distance):
        pairs = []
        for s in range(self.seq):
            if 0 <= s + distance < self.seq:
                for r in range(self.row):
                    pairs.append((s * self.row + r, (s + distance) * self.row + r))
        return lax.ppermute(value, AXES, pairs)

    def ordered(self, axis, bit, mine, other):
        high = (self.at[axis] & bit) != 0
        return jnp.where(high, other, mine), jnp.where(high, mine, other)

    def gather(self, value, axis, dim):
        distance = 1
        while distance < self.size[axis]:
            other = self.swap(value, axis, distance)
            value = jnp.concatenate(self.ordered(axis, distance, value, other), axis=dim)
            distance *= 2
        return value

    def scatter(self, value, axis, dim, dtype=BF, between=BF):
        distance = self.size[axis] // 2
        while distance:
            half = value.shape[dim] // 2
            high = (self.at[axis] // distance) % 2
            send = lax.dynamic_slice_in_dim(value, (1 - high) * half, half, dim)
            keep = lax.dynamic_slice_in_dim(value, high * half, half, dim)
            other = self.swap(send, axis, distance)
            distance //= 2
            value = (keep.astype(F32) + other.astype(F32)).astype(between if distance else dtype)
        return value


def gather_group(place, value, cut):
    value = place.gather(value[None, None, None], "z", 0)
    left, right = value[..., :cut], value[..., cut:]
    left = place.gather(left, "y", 1)
    right = place.gather(right, "x", 2)
    left = place.gather(left, "x", 2)
    right = place.gather(right, "y", 1)
    return left, right


def scatter_group(place, left, right, last=F32):
    lead = (place.size["z"], place.size["y"], place.size["x"])
    left = left.reshape(lead + left.shape[-2:])
    right = right.reshape(lead + right.shape[-2:])
    left = place.scatter(left, "x", 2)
    right = place.scatter(right, "y", 1)
    left = place.scatter(left, "y", 1)
    right = place.scatter(right, "x", 2)
    both = jnp.concatenate([left, right], axis=-1)
    return place.scatter(both, "z", 0, last)[0, 0, 0]


def compose(earlier, later):
    return jnp.concatenate(
        [earlier[:4] * later[:4], later[:4] * earlier[4:] + later[4:]], axis=0
    )


def carry_in(place, end_map, sign):
    n = place.seq
    unit = jnp.concatenate([jnp.ones_like(end_map[:4]), jnp.zeros_like(end_map[4:])], axis=0)

    def fetched(value, distance):
        got = place.along(value, sign * distance)
        inside = (place.s >= distance) if sign > 0 else (place.s < n - distance)
        return jnp.where(inside, got, unit)

    window, width, first = end_map, 1, True
    total = None
    reach = 0
    while reach < n - 1:
        if first:
            parts = [fetched(window, d) for d in range(1, min(4, n))]
            total = parts[0]
            for part in parts[1:]:
                total = compose(part, total)
            reach = len(parts)
            first = False
        else:
            shifts = []
            d = reach
            while d < n - 1 and len(shifts) < 3:
                shifts.append(d)
                d += reach
            parts = [fetched(total, d) for d in shifts]
            for part in parts:
                total = compose(part, total)
            reach = reach * (len(shifts) + 1)
    return total[4:]


def dot(a, b):
    return jnp.dot(a, b, preferred_element_type=F32)


def dot_nt(a, b):
    return lax.dot_general(a, b, (((1,), (1,)), ((), ())), preferred_element_type=F32)


def dot_tn(a, b):
    return lax.dot_general(a, b, (((0,), (0,)), ((), ())), preferred_element_type=F32)


def moved(value, distance, fill):
    n = value.shape[0]
    size = abs(distance)
    edge = jnp.full((size,) + value.shape[1:], fill, value.dtype)
    if size % 8 == 0:
        if distance > 0:
            return jnp.concatenate([edge, value[: n - size]], axis=0)
        return jnp.concatenate([value[size:], edge], axis=0)
    at = lax.broadcasted_iota(jnp.int32, value.shape, 0)
    turned = pltpu.roll(value, distance % n, 0)
    inside = at >= size if distance > 0 else at < n - size
    return jnp.where(inside, turned, fill)


def scan_tile(decay, drive, sign):
    n = decay.shape[0]
    distance = 1
    while distance < n:
        drive = decay * moved(drive, sign * distance, 0.0) + drive
        decay = decay * moved(decay, sign * distance, 1.0)
        distance *= 2
    return decay, drive


def one_less_exp(u):
    term = jnp.full_like(u, 1.0 / 3628800.0)
    for k in (362880, 40320, 5040, 720, 120, 24, 6, 2):
        term = 1.0 / k - u * term
    small = u * (1.0 - u * term)
    return jnp.where(u < 0.8, small, 1.0 - jnp.exp(-u))


def gelu_parts(value):
    square = value * value
    t = jnp.tanh(GELU_C * value * (1.0 + 0.044715 * square))
    half = 0.5 * (1.0 + t)
    slope = half + 0.5 * value * (1.0 - t * t) * GELU_C * (1.0 + 3.0 * 0.044715 * square)
    return value * half, slope


def full(shape):
    return pl.BlockSpec(shape, lambda j: (0,) * len(shape))


def columns(rows, width=TILE):
    return pl.BlockSpec((rows, width), lambda j: (0, j))


def lines(rows, width):
    return pl.BlockSpec((rows, width), lambda j: (j, 0))


def shape_of(shape, dtype):
    return jax.ShapeDtypeStruct(shape, dtype)


def params(limit):
    return pltpu.CompilerParams(vmem_limit_bytes=limit * MIB)


def forward_kernel(
    n_rows,
    group,
    block,
    first_ref,
    w_ref,
    vec_ref,
    mask_ref,
    gr_ref,
    gi_ref,
    mixer_ref,
    conv_ref,
    rpre_ref,
    ipre_ref,
    through_ref,
    local_ref,
    ends_ref,
    ext_ref,
):
    mixer = dot(first_ref[...], w_ref[...]).astype(BF)
    mixer_ref[...] = mixer
    wide = mixer.astype(F32)
    tokens = n_rows * group
    for r in range(n_rows):
        ext_ref[r, 0:HALO] = wide[tokens + HALO * r : tokens + HALO * (r + 1)]
        ext_ref[r, HALO : HALO + group] = wide[r * group : (r + 1) * group]
    for r in range(n_rows):
        span = slice(r * group, (r + 1) * group)
        conv = vec_ref[4:5] + vec_ref[0:1] * ext_ref[r, HALO : HALO + group]
        for k in range(1, 4):
            conv += (
                vec_ref[k : k + 1]
                * ext_ref[r, HALO - k : HALO - k + group]
                * mask_ref[span, k : k + 1]
            )
        conv_ref[span] = conv.astype(BF)
    for h in range(w_ref.shape[1] // block):
        cols = slice(h * block, (h + 1) * block)
        low = conv_ref[:, cols]
        rpre_ref[:, cols] = dot(low, gr_ref[cols]) + vec_ref[5:6, cols]
        ipre_ref[:, cols] = dot(low, gi_ref[cols]) + vec_ref[6:7, cols]
        for r in range(n_rows):
            span = slice(r * group, (r + 1) * group)
            recur = jax.nn.sigmoid(rpre_ref[span, cols])
            admit = jax.nn.sigmoid(ipre_ref[span, cols])
            rate = vec_ref[7:8, cols] * recur
            reset = mask_ref[span, 0:1]
            decay = jnp.exp(-rate) * (1.0 - reset)
            scale = jnp.where(reset > 0.5, 1.0, jnp.sqrt(one_less_exp(2.0 * rate)))
            drive = scale * admit * conv_ref[span, cols].astype(F32)
            decay, drive = scan_tile(decay, drive, 1)
            through_ref[span, cols] = decay
            local_ref[span, cols] = drive
            ends_ref[r : r + 1, cols] = decay[group - 1 : group]
            ends_ref[n_rows + r : n_rows + r + 1, cols] = drive[group - 1 : group]


def forward_call(first, w_in, vec, masks, gate_r, gate_i, n_rows, group):
    length, model = first.shape
    width, block = w_in.shape[1], gate_r.shape[1]
    tokens = n_rows * group
    tile = TILE
    return pl.pallas_call(
        functools.partial(forward_kernel, n_rows, group, block),
        grid=(width // tile,),
        in_specs=[
            full((length, model)),
            columns(model),
            columns(8),
            full(masks.shape),
            lines(tile, block),
            lines(tile, block),
        ],
        out_specs=[columns(length)] + [columns(tokens)] * 5 + [columns(2 * n_rows)],
        out_shape=[
            shape_of((length, width), BF),
            shape_of((tokens, width), BF),
            shape_of((tokens, width), F32),
            shape_of((tokens, width), F32),
            shape_of((tokens, width), F32),
            shape_of((tokens, width), F32),
            shape_of((2 * n_rows, width), F32),
        ],
        scratch_shapes=[pltpu.VMEM((n_rows, HALO + group, tile), F32)],
        compiler_params=params(24),
        name="recurrence_forward",
    )(first, w_in, vec, masks, gate_r, gate_i)


def mix_kernel(
    n_rows, group, local_ref, through_ref, enter_ref, bpre_ref, w_ref, state_ref, mixed_ref, part_ref
):
    for r in range(n_rows):
        span = slice(r * group, (r + 1) * group)
        state = local_ref[span] + through_ref[span] * enter_ref[r : r + 1]
        state_ref[span] = state
        branch, _ = gelu_parts(bpre_ref[span])
        mixed_ref[span] = (state * branch).astype(BF)
    part = dot(mixed_ref[...], w_ref[...])

    @pl.when(pl.program_id(0) == 0)
    def _():
        part_ref[...] = part

    @pl.when(pl.program_id(0) > 0)
    def _():
        part_ref[...] += part


def mix_call(local, through, enter, branch_pre, w_out, n_rows, group):
    tokens, width = local.shape
    model = w_out.shape[1]
    return pl.pallas_call(
        functools.partial(mix_kernel, n_rows, group),
        grid=(width // TILE,),
        in_specs=[
            columns(tokens),
            columns(tokens),
            columns(n_rows),
            columns(tokens),
            lines(TILE, model),
        ],
        out_specs=[columns(tokens), columns(tokens), full((tokens, model))],
        out_shape=[
            shape_of((tokens, width), F32),
            shape_of((tokens, width), BF),
            shape_of((tokens, model), F32),
        ],
        compiler_params=params(24),
        name="mix",
    )(local, through, enter, branch_pre, w_out)


def ffn_kernel(
    second_ref, low_ref, wg_ref, wu_ref, wd_ref, gg_ref, gu_ref, gd_ref, part_ref, back_ref, turned_ref
):
    step = pl.program_id(0)

    @pl.when(step == 0)
    def _():
        turned_ref[...] = second_ref[...].T

    second, low = second_ref[...], low_ref[...]
    gate = dot(second, wg_ref[...])
    up = dot(second, wu_ref[...])
    grad = dot_nt(low, wd_ref[...])
    active, slope = gelu_parts(gate)
    hidden = (active * up).astype(BF)
    gate_low = (grad * up * slope).astype(BF)
    up_low = (grad * active).astype(BF)
    gg_ref[...] = dot(turned_ref[...], gate_low).astype(BF)
    gu_ref[...] = dot(turned_ref[...], up_low).astype(BF)
    gd_ref[...] = dot_tn(hidden, low).astype(BF)
    part = dot(hidden, wd_ref[...])
    back = dot_nt(gate_low, wg_ref[...]) + dot_nt(up_low, wu_ref[...])

    @pl.when(step == 0)
    def _():
        part_ref[...] = part
        back_ref[...] = back

    @pl.when(step > 0)
    def _():
        part_ref[...] += part
        back_ref[...] += back


def ffn_call(second, low, w_gate, w_up, w_down):
    tokens, model = second.shape
    width = w_gate.shape[1]
    return pl.pallas_call(
        ffn_kernel,
        grid=(width // TILE,),
        in_specs=[
            full((tokens, model)),
            full((tokens, model)),
            columns(model),
            columns(model),
            lines(TILE, model),
        ],
        out_specs=[
            columns(model),
            columns(model),
            lines(TILE, model),
            full((tokens, model)),
            full((tokens, model)),
        ],
        out_shape=[
            shape_of((model, width), BF),
            shape_of((model, width), BF),
            shape_of((width, model), BF),
            shape_of((tokens, model), F32),
            shape_of((tokens, model), F32),
        ],
        scratch_shapes=[pltpu.VMEM((model, tokens), BF)],
        compiler_params=params(40),
        name="feed_forward",
    )(second, low, w_gate, w_up, w_down)


def decay_of(rpre, vec7, reset):
    recur = jax.nn.sigmoid(rpre)
    rate = vec7 * recur
    return recur, rate, jnp.exp(-rate) * (1.0 - reset)


def back_kernel(
    n_rows,
    group,
    low_ref,
    w_ref,
    bpre_ref,
    state_ref,
    rpre_ref,
    mixed_ref,
    vec_ref,
    mask_ref,
    first_ref,
    go_ref,
    gb_ref,
    gbl_ref,
    reach_ref,
    local_ref,
    ends_ref,
    turned_ref,
    grad_ref,
):
    @pl.when(pl.program_id(0) == 0)
    def _():
        turned_ref[...] = first_ref[...].T

    low = low_ref[...]
    grad_ref[...] = dot_nt(low, w_ref[...])
    go_ref[...] = dot_tn(mixed_ref[...], low).astype(BF)
    half = w_ref.shape[0] // 2
    for h in range(2):
        cols = slice(h * half, (h + 1) * half)
        for r in range(n_rows):
            span = slice(r * group, (r + 1) * group)
            branch, slope = gelu_parts(bpre_ref[span, cols])
            grad = grad_ref[span, cols]
            gbl_ref[span, cols] = (grad * state_ref[span, cols] * slope).astype(BF)
            _, _, decay = decay_of(rpre_ref[span, cols], vec_ref[7:8, cols], mask_ref[span, 0:1])
            ahead = moved(decay, -1, 1.0)
            reach, local = scan_tile(ahead, grad * branch, -1)
            reach_ref[span, cols] = reach
            local_ref[span, cols] = local
            ends_ref[r : r + 1, cols] = decay[0:1] * reach[0:1]
            ends_ref[n_rows + r : n_rows + r + 1, cols] = decay[0:1] * local[0:1]
    gb_ref[...] = dot(turned_ref[...], gbl_ref[...]).astype(BF)


def back_call(low, w_out, branch_pre, state, rpre, mixed, vec, masks, first, n_rows, group):
    tokens, model = low.shape
    width = w_out.shape[0]
    return pl.pallas_call(
        functools.partial(back_kernel, n_rows, group),
        grid=(width // TILE,),
        in_specs=[
            full((tokens, model)),
            lines(TILE, model),
            columns(tokens),
            columns(tokens),
            columns(tokens),
            columns(tokens),
            columns(8),
            full(masks.shape),
            full((tokens, model)),
        ],
        out_specs=[
            lines(TILE, model),
            columns(model),
            columns(tokens),
            columns(tokens),
            columns(tokens),
            columns(2 * n_rows),
        ],
        out_shape=[
            shape_of((width, model), BF),
            shape_of((model, width), BF),
            shape_of((tokens, width), BF),
            shape_of((tokens, width), F32),
            shape_of((tokens, width), F32),
            shape_of((2 * n_rows, width), F32),
        ],
        scratch_shapes=[pltpu.VMEM((model, tokens), BF), pltpu.VMEM((tokens, TILE), F32)],
        compiler_params=params(32),
        name="recurrence_back",
    )(low, w_out, branch_pre, state, rpre, mixed, vec, masks, first)


def gates_kernel(
    n_rows,
    group,
    block,
    reach_ref,
    local_ref,
    leave_ref,
    state_ref,
    enter_ref,
    rpre_ref,
    ipre_ref,
    conv_ref,
    mixer_ref,
    vec_ref,
    mask_ref,
    gr_ref,
    gi_ref,
    first_ref,
    win_ref,
    wbr_ref,
    gbl_ref,
    gin_ref,
    ggr_ref,
    ggi_ref,
    gvec_ref,
    gfirst_ref,
    turned_ref,
    rlow_ref,
    ilow_ref,
    gconv_ref,
    ext_ref,
    spread_ref,
    gm_ref,
):
    step = pl.program_id(0)
    tokens = n_rows * group

    @pl.when(step == 0)
    def _():
        turned_ref[...] = first_ref[...].T

    gvec_ref[...] = jnp.zeros_like(gvec_ref)
    for h in range(win_ref.shape[1] // block):
        cols = slice(h * block, (h + 1) * block)
        for r in range(n_rows):
            span = slice(r * group, (r + 1) * group)
            adjoint = local_ref[span, cols] + reach_ref[span, cols] * leave_ref[r : r + 1, cols]
            state = state_ref[span, cols]
            at = lax.broadcasted_iota(jnp.int32, state.shape, 0)
            before = jnp.where(at == 0, enter_ref[r : r + 1, cols], pltpu.roll(state, 1, 0))
            reset = mask_ref[span, 0:1]
            live = 1.0 - reset
            recur, rate, decay = decay_of(rpre_ref[span, cols], vec_ref[7:8, cols], reset)
            admit = jax.nn.sigmoid(ipre_ref[span, cols])
            full_decay = jnp.exp(-rate)
            root = jnp.sqrt(one_less_exp(2.0 * rate))
            scale = jnp.where(reset > 0.5, 1.0, root)
            conv = conv_ref[span, cols].astype(F32)
            direct = adjoint * scale
            gadmit = direct * conv
            gconv_ref[span, cols] = direct * admit
            gscale = adjoint * admit * conv
            glog = live * full_decay * (adjoint * before - gscale * full_decay / root)
            gvec_ref[7:8, cols] += jnp.sum(glog * recur, axis=0, keepdims=True)
            grecur = -(vec_ref[7:8, cols] * glog) * recur * (1.0 - recur)
            ginput = gadmit * admit * (1.0 - admit)
            rlow, ilow = grecur.astype(BF), ginput.astype(BF)
            rlow_ref[span, cols] = rlow
            ilow_ref[span, cols] = ilow
            gvec_ref[5:6, cols] += jnp.sum(rlow.astype(F32), axis=0, keepdims=True)
            gvec_ref[6:7, cols] += jnp.sum(ilow.astype(F32), axis=0, keepdims=True)
        rlow, ilow = rlow_ref[:, cols], ilow_ref[:, cols]
        low = conv_ref[:, cols]
        ggr_ref[cols] = dot_tn(low, rlow)
        ggi_ref[cols] = dot_tn(low, ilow)
        gconv_ref[:, cols] += dot_nt(rlow, gr_ref[cols]) + dot_nt(ilow, gi_ref[cols])
        for r in range(n_rows):
            span = slice(r * group, (r + 1) * group)
            head = slice(tokens + HALO * r, tokens + HALO * (r + 1))
            ext_ref[0:HALO] = mixer_ref[head, cols].astype(F32)
            ext_ref[HALO : HALO + group] = mixer_ref[span, cols].astype(F32)
            gconv = gconv_ref[span, cols]
            gvec_ref[4:5, cols] += jnp.sum(gconv, axis=0, keepdims=True)
            gvec_ref[0:1, cols] += jnp.sum(
                gconv * ext_ref[HALO : HALO + group], axis=0, keepdims=True
            )
            spread_ref[0:HALO] = jnp.zeros((HALO, block), F32)
            spread_ref[HALO : HALO + group] = vec_ref[0:1, cols] * gconv
            for k in range(1, 4):
                masked = gconv * mask_ref[span, k : k + 1]
                there = slice(HALO - k, HALO - k + group)
                gvec_ref[k : k + 1, cols] += jnp.sum(
                    masked * ext_ref[there], axis=0, keepdims=True
                )
                spread_ref[there] += vec_ref[k : k + 1, cols] * masked
            gm_ref[head, cols] = spread_ref[0:HALO].astype(BF)
            gm_ref[span, cols] = spread_ref[HALO : HALO + group].astype(BF)
    gm = gm_ref[...]
    gin_ref[...] = dot(turned_ref[...], gm).astype(BF)
    part = dot_nt(gm, win_ref[...])
    part_branch = dot_nt(gbl_ref[...], wbr_ref[...])

    @pl.when(step == 0)
    def _():
        gfirst_ref[...] = part

    @pl.when(step > 0)
    def _():
        gfirst_ref[...] += part

    gfirst_ref[0:tokens] += part_branch


def gates_call(
    reach, local, leave, state, enter, rpre, ipre, conv, mixer, vec, masks, gate_r, gate_i, first, w_in, w_branch, gbl, n_rows, group
):
    length, model = first.shape
    tokens, width = state.shape
    block = gate_r.shape[1]
    tile = TILE
    return pl.pallas_call(
        functools.partial(gates_kernel, n_rows, group, block),
        grid=(width // tile,),
        in_specs=[
            columns(tokens),
            columns(tokens),
            columns(n_rows),
            columns(tokens),
            columns(n_rows),
            columns(tokens),
            columns(tokens),
            columns(tokens),
            columns(length),
            columns(8),
            full(masks.shape),
            lines(tile, block),
            lines(tile, block),
            full((length, model)),
            columns(model),
            columns(model),
            columns(tokens),
        ],
        out_specs=[
            columns(model),
            lines(tile, block),
            lines(tile, block),
            columns(8),
            full((length, model)),
        ],
        out_shape=[
            shape_of((model, width), BF),
            shape_of((width, block), F32),
            shape_of((width, block), F32),
            shape_of((8, width), F32),
            shape_of((length, model), F32),
        ],
        scratch_shapes=[
            pltpu.VMEM((model, length), BF),
            pltpu.VMEM((tokens, tile), BF),
            pltpu.VMEM((tokens, tile), BF),
            pltpu.VMEM((tokens, tile), F32),
            pltpu.VMEM((HALO + group, block), F32),
            pltpu.VMEM((HALO + group, block), F32),
            pltpu.VMEM((length, tile), BF),
        ],
        compiler_params=params(40),
        name="recurrence_gates",
    )(reach, local, leave, state, enter, rpre, ipre, conv, mixer, vec, masks, gate_r, gate_i, first, w_in, w_branch, gbl)


def normed(values, gain):
    return values * lax.rsqrt(jnp.mean(values * values, axis=-1, keepdims=True) + EPS) * gain


def halves(value, place, dim):
    half = value.shape[dim] // 2
    mine = lax.dynamic_slice_in_dim(value, place.at["c"] * half, half, dim)
    other = lax.dynamic_slice_in_dim(value, (1 - place.at["c"]) * half, half, dim)
    return mine, other


def own_channels(place, value):
    mine, other = halves(value, place, 0)
    got = place.swap(other, "c", 1)
    pair = place.ordered("c", 1, mine, got)
    both = jnp.stack(pair, axis=1)
    return both.reshape(-1, both.shape[-1])


def own_devices(place, value, rows):
    shaped = value.reshape(place.chips // 2, 2, rows, value.shape[-1])
    mine = lax.dynamic_index_in_dim(shaped, place.at["c"], 1, keepdims=False)
    other = lax.dynamic_index_in_dim(shaped, 1 - place.at["c"], 1, keepdims=False)
    got = place.swap(other, "c", 1)
    return jnp.concatenate(place.ordered("c", 1, mine, got), axis=0)


def on_device(
    inputs,
    cotangent,
    segments,
    norm1_gain,
    input_proj,
    branch_proj,
    conv_weight,
    conv_bias,
    recur_gate,
    input_gate,
    recur_bias,
    input_bias,
    decay_param,
    output_proj,
    norm2_gain,
    mlp_gate,
    mlp_up,
    mlp_down,
):
    place = Place()
    core = place.at["c"]
    chips = place.chips
    rows_dev, group, model = inputs.shape
    n_rows = 2 * rows_dev
    tokens_dev = rows_dev * group
    tokens = 2 * tokens_dev
    d_rows, lru = input_proj.shape
    ffn = mlp_gate.shape[1]
    r_rows, block = recur_gate.shape
    f_rows = mlp_down.shape[0]
    lru_half, ffn_half = lru // 2, ffn // 2
    pair = lambda value: place.swap(value, "c", 1)

    vectors = jnp.concatenate(
        [
            norm1_gain,
            norm2_gain,
            conv_weight.reshape(-1),
            conv_bias,
            recur_bias,
            input_bias,
            decay_param,
        ]
    )
    small = vectors[None, None, None, None]
    for axis, dim in (("c", 3), ("x", 2), ("y", 1), ("z", 0)):
        small = place.gather(small, axis, dim)
    small = small.reshape(2 * chips, -1).astype(F32)
    gain_one = small[:, :d_rows].reshape(-1)
    gain_two = small[:, d_rows : 2 * d_rows].reshape(-1)
    vec = small[:, 2 * d_rows :].reshape(2 * chips, 8, r_rows)
    vec = jnp.transpose(vec, (1, 0, 2)).reshape(8, lru)
    vec = lax.dynamic_slice_in_dim(vec, core * lru_half, lru_half, 1)
    decay_raw = vec[7]
    vec = jnp.concatenate([vec[:7], 8.0 * jax.nn.softplus(decay_raw)[None]], axis=0)

    wide = [halves(w, place, 1) for w in (input_proj, branch_proj, mlp_gate, mlp_up)]
    mine = jnp.concatenate([w[0] for w in wide], axis=1)
    got = pair(jnp.concatenate([w[1] for w in wide], axis=1))
    chip_rows = jnp.concatenate(place.ordered("c", 1, mine, got), axis=0)
    gates = jnp.stack([recur_gate, input_gate]).reshape(-1, lru)
    gate_lines = gates.shape[0]
    group_a = jnp.concatenate([chip_rows[:, :lru], gates], axis=0)
    group_b = jnp.concatenate([output_proj, mlp_down], axis=0)
    group_c = chip_rows[:, lru:]

    a_left, a_right = gather_group(place, group_a, lru_half)
    chip_d = 2 * d_rows
    w_in = a_left[..., :chip_d, :].reshape(model, lru_half)
    w_branch = a_right[..., :chip_d, :].reshape(model, lru_half)
    packed = jnp.concatenate([a_left[..., chip_d:, :], a_right[..., chip_d:, :]], axis=-1)
    packed = packed.reshape(chips, 2, r_rows, block)
    packed = jnp.concatenate([packed[:, 0], packed[:, 1]], axis=-1)
    packed = own_channels(place, packed)
    gate_r, gate_i = packed[:, :block], packed[:, block:]

    b_left, b_right = gather_group(place, group_b, model // 2)
    outs = jnp.concatenate([b_left, b_right], axis=-1).reshape(chips, r_rows + f_rows, model)
    mine, other = halves(outs, place, 0)
    low_half, high_half = place.ordered("c", 1, mine, pair(other))
    w_out = jnp.stack([low_half[:, :r_rows], high_half[:, :r_rows]], axis=1).reshape(-1, model)
    w_down = jnp.stack([low_half[:, r_rows:], high_half[:, r_rows:]], axis=1).reshape(-1, model)

    c_left, c_right = gather_group(place, group_c, ffn_half)
    w_gate = c_left.reshape(model, ffn_half)
    w_up = c_right.reshape(model, ffn_half)

    flat = inputs.reshape(tokens_dev, model)
    first = normed(flat, gain_one).astype(BF)
    first = jnp.concatenate([first, pair(first)], axis=0)
    grad_out = cotangent.reshape(tokens_dev, model)
    grad_low = grad_out.astype(BF)
    grad_low = jnp.concatenate([grad_low, pair(grad_low)], axis=0)
    ids = jnp.concatenate([segments, pair(segments)], axis=0)
    prior_ids = place.along(ids[:, group - 3 :], 1)
    tail = first.reshape(n_rows, group, model)[:, group - 3 :]
    halo = place.along(tail, 1)
    halo = jnp.pad(halo, ((0, 0), (HALO - 3, 0), (0, 0))).reshape(n_rows * HALO, model)
    first_ext = jnp.concatenate([first, halo], axis=0)

    position = place.s * group + jnp.arange(group, dtype=jnp.int32)
    joined_ids = jnp.concatenate([prior_ids, ids], axis=1)
    marks = [(joined_ids[:, 2 : 2 + group] != ids) | (position == 0)[None, :]]
    for k in range(1, 4):
        marks.append(
            (joined_ids[:, 3 - k : 3 - k + group] == ids) & (position >= k)[None, :]
        )
    masks = jnp.stack(marks, axis=-1).astype(F32).reshape(tokens, 4)
    masks = jnp.pad(masks, ((0, 0), (0, 4)))

    mixer, conv, rpre, ipre, through, local, ends = forward_call(
        first_ext, w_in, vec, masks, gate_r, gate_i, n_rows, group
    )
    branch_pre = dot(first, w_branch)
    enter = carry_in(place, ends, 1)
    state, mixed, part = mix_call(local, through, enter, branch_pre, w_out, n_rows, group)
    middle = flat + (part[:tokens_dev] + pair(part[tokens_dev:]))
    second = normed(middle, gain_two).astype(BF)
    second = jnp.concatenate([second, pair(second)], axis=0)

    g_gate, g_up, g_down, part, back = ffn_call(second, grad_low, w_gate, w_up, w_down)
    result = middle + (part[:tokens_dev] + pair(part[tokens_dev:]))
    grad_second = back[:tokens_dev] + pair(back[tokens_dev:])
    grad_norm, grad_gain_two = jax.vjp(normed, middle, gain_two)[1](grad_second)
    grad_middle = grad_out + grad_norm
    mid_low = grad_middle.astype(BF)
    mid_low = jnp.concatenate([mid_low, pair(mid_low)], axis=0)

    g_out, g_branch, gbl, reach, local_back, ends_back = back_call(
        mid_low, w_out, branch_pre, state, rpre, mixed, vec, masks, first, n_rows, group
    )
    leave = carry_in(place, ends_back, -1)
    g_in, g_gate_r, g_gate_i, g_vec, grad_first = gates_call(
        reach, local_back, leave, state, enter, rpre, ipre, conv, mixer, vec, masks, gate_r, gate_i, first_ext, w_in, w_branch, gbl, n_rows, group
    )
    spill = grad_first[tokens:].reshape(n_rows, HALO, model)[:, HALO - 3 :]
    spill = place.along(spill, -1)
    spill = jnp.pad(spill, ((0, 0), (group - 3, 0), (0, 0))).reshape(tokens, model)
    grad_first = grad_first[:tokens] + spill
    grad_first = grad_first[:tokens_dev] + pair(grad_first[tokens_dev:])
    grad_norm, grad_gain_one = jax.vjp(normed, flat, gain_one)[1](grad_first)
    grad_inputs = grad_middle + grad_norm

    sum_c = scatter_group(
        place,
        g_gate.reshape(chips, chip_d, ffn_half),
        g_up.reshape(chips, chip_d, ffn_half),
    )
    outs = jnp.concatenate(
        [
            g_out.reshape(-1, r_rows, model),
            g_down.reshape(-1, f_rows, model),
        ],
        axis=1,
    )
    outs = own_devices(place, outs.reshape(-1, model), r_rows + f_rows)
    sum_b = scatter_group(place, outs[..., : model // 2], outs[..., model // 2 :])

    g_vec = g_vec * jnp.concatenate(
        [jnp.ones((7, lru_half), F32), -8.0 * jax.nn.sigmoid(decay_raw)[None]], axis=0
    )
    lines_r = jnp.concatenate([g_gate_r, g_gate_i], axis=1).astype(BF)
    lines_r = lines_r.reshape(chips, r_rows * 2 * block)
    lines_v = jnp.transpose(g_vec.reshape(8, chips, r_rows), (1, 0, 2)).astype(BF)
    lines_v = lines_v.reshape(chips, 8 * r_rows)
    packed = jnp.concatenate([lines_r, lines_v], axis=1)
    used = packed.shape[1]
    extra = -used % lru
    packed = jnp.pad(packed, ((0, 0), (0, extra)))
    packed = own_devices(place, packed, 1)
    packed = packed.reshape(chips, -1, lru)
    joined = jnp.concatenate(
        [
            jnp.concatenate([g_in, g_branch], axis=1).reshape(chips, chip_d, lru),
            packed,
        ],
        axis=1,
    )
    sum_a = scatter_group(place, joined[..., :lru_half], joined[..., lru_half:])

    gains = jnp.stack([grad_gain_one, grad_gain_two], axis=0)
    gains = jnp.transpose(gains.reshape(2, chips, 2, d_rows), (1, 2, 0, 3))
    gains = gains.reshape(
        place.size["z"], place.size["y"], place.size["x"], 2, 2 * d_rows
    )
    for axis, dim in (("c", 3), ("x", 2), ("y", 1), ("z", 0)):
        gains = place.scatter(gains, axis, dim, F32, F32)
    gains = gains.reshape(2, d_rows)

    summed = jnp.concatenate([sum_a[:chip_d], sum_c], axis=1)
    mine, other = halves(summed, place, 0)
    got = pair(other)
    low_half, high_half = place.ordered("c", 1, mine, got)

    def columns_of(start, width):
        span = slice(start, start + width)
        return jnp.concatenate([low_half[:, span], high_half[:, span]], axis=1)

    grad_input_proj = columns_of(0, lru_half)
    grad_branch_proj = columns_of(lru_half, lru_half)
    grad_gate = columns_of(lru, ffn_half)
    grad_up = columns_of(lru + ffn_half, ffn_half)
    own = sum_a[chip_d:].reshape(-1)[:used]
    own_gates = own[: r_rows * 2 * block].reshape(r_rows, 2 * block)
    own_vec = own[r_rows * 2 * block :].reshape(8, r_rows)
    return (
        result.reshape(inputs.shape),
        grad_inputs.reshape(inputs.shape),
        gains[0],
        grad_input_proj,
        grad_branch_proj,
        own_vec[:4],
        own_vec[4],
        own_gates[:, :block],
        own_gates[:, block:],
        own_vec[5],
        own_vec[6],
        own_vec[7],
        sum_b[:r_rows],
        gains[1],
        grad_gate,
        grad_up,
        sum_b[r_rows:],
    )


def solution(mesh):
    every = ("seq", "row")
    tokens, line, flat, taps = P("row", "seq", None), P(every, None), P(every), P(None, every)
    in_specs = (
        tokens,
        tokens,
        P("row", "seq"),
        flat,
        line,
        line,
        taps,
        flat,
        line,
        line,
        flat,
        flat,
        flat,
        line,
        flat,
        line,
        line,
        line,
    )
    out_specs = (
        tokens,
        tokens,
        flat,
        line,
        line,
        taps,
        flat,
        line,
        line,
        flat,
        flat,
        flat,
        line,
        flat,
        line,
        line,
        line,
    )
    return jax.shard_map(
        on_device, mesh=mesh, in_specs=in_specs, out_specs=out_specs, check_vma=False
    )
```

```python
import functools
import math

import jax
import jax.numpy as jnp
import numpy as np
from jax import lax
from jax.experimental import pallas as pl
from jax.experimental.pallas import tpu as pltpu
from jax.sharding import Mesh, PartitionSpec as P

EPS = 1e-06
BF = jnp.bfloat16
F32 = jnp.float32
AXES = ("z", "y", "x", "c")
MIB = 1 << 20
TILE = 256
HALO = 8
GELU_C = math.sqrt(2.0 / math.pi)


class Place:
    def __init__(self):
        self.size = {axis: lax.axis_size(axis) for axis in AXES}
        self.at = {axis: lax.axis_index(axis) for axis in AXES}
        nz, ny, nx, _ = self.size.values()
        self.seq, self.row = nz * ny, nx * 2
        self.s = self.at["z"] * ny + self.at["y"]
        self.stride = {"z": ny * self.row, "y": self.row, "x": 2, "c": 1}
        self.chips = nz * ny * nx
        self.sizes = (nz, ny, nx)
        self.where = jnp.stack([self.at[axis] for axis in AXES]).astype(jnp.int32)


    def ring(self, value, axis, shift):
        pairs = []
        for i in range(self.seq * self.row):
            at = (i // self.stride[axis]) % self.size[axis]
            to = (at + shift) % self.size[axis]
            pairs.append((i, i + (to - at) * self.stride[axis]))
        return lax.ppermute(value, AXES, pairs)

    def along(self, value, distance):
        pairs = []
        for s in range(self.seq):
            if 0 <= s + distance < self.seq:
                for r in range(self.row):
                    pairs.append((s * self.row + r, (s + distance) * self.row + r))
        return lax.ppermute(value, AXES, pairs)

    def ordered(self, mine, other):
        high = self.at["c"] != 0
        return jnp.where(high, other, mine), jnp.where(high, mine, other)


class Order:
    def __init__(self, place):
        self.place = place
        self.last = ()
        self.sent = ()

    def tie(self, value):
        if not self.last:
            return value
        return lax.optimization_barrier((value,) + self.last)[0]

    def must(self, *values):
        self.sent += values

    def ring(self, value, axis, shift=1):
        value = self.tie(value)
        self.sent += (value,)
        return self.place.ring(value, axis, shift)

    def along(self, value, distance):
        value = self.tie(value)
        self.sent += (value,)
        return self.place.along(value, distance)

    def wait(self, *values):
        n = len(values)
        held = values + self.last + self.sent
        if len(held) > n:
            values = lax.optimization_barrier(held)[:n]
        self.last = tuple(values)
        self.sent = ()
        return values[0] if n == 1 else values


class Gather:
    def __init__(self, order, value, axis, dim, direct=False, both=False):
        self.order, self.axis, self.dim = order, axis, dim
        self.n = order.place.size[axis]
        self.pieces = [value]
        self.direct = direct
        self.both = both and self.n == 4
        if self.both:
            self.flying = [order.ring(value, axis, 1), order.ring(value, axis, 3)]
            return
        shifts = range(1, self.n) if direct else range(1, min(2, self.n))
        self.flying = [order.ring(value, axis, k) for k in shifts]

    def next(self):
        if self.direct:
            if self.flying:
                got = self.order.wait(*self.flying)
                self.pieces += [got] if len(self.flying) == 1 else list(got)
            self.flying = []
            return
        if self.both:
            if len(self.flying) == 2:
                one, three = self.order.wait(*self.flying)
                self.pieces += [one, None, three]
                self.flying = [self.order.ring(one, self.axis)]
            elif self.flying:
                self.pieces[2] = self.order.wait(self.flying.pop())
            return
        got = self.order.wait(self.flying.pop())
        self.pieces.append(got)
        if len(self.pieces) < self.n:
            self.flying = [self.order.ring(got, self.axis)]

    def done(self):
        while len(self.pieces) < self.n or (self.both and self.flying):
            self.next()
        at = self.order.place.at[self.axis]
        if self.n == 2:
            high = at != 0
            mine, other = self.pieces
            parts = [jnp.where(high, other, mine), jnp.where(high, mine, other)]
            return jnp.concatenate(parts, axis=self.dim)
        parts = [
            lax.select_n(lax.rem(at - j + self.n, self.n), *self.pieces) for j in range(self.n)
        ]
        return jnp.concatenate(parts, axis=self.dim)


class Scatter:
    def __init__(self, order, blocks, axis, direct=False, between=BF, both=False):
        self.order, self.axis, self.blocks = order, axis, list(blocks)
        self.n = order.place.size[axis]
        self.both = both and self.n == 4
        self.direct, self.between = direct, between
        self.hop = 0
        if self.both:
            self.flying = [order.ring(self.blocks[1], axis, 3), order.ring(self.blocks[2], axis, 1)]
        elif direct:
            self.flying = [
                order.ring(self.blocks[i], axis, self.n - 1 - i) for i in range(self.n - 1)
            ]
        elif self.n > 1:
            self.flying = order.ring(self.blocks[0], axis)

    def next(self):
        if self.both:
            if self.hop == 0:
                far, near = self.order.wait(*self.flying)
                total = far.astype(F32) + self.blocks[0].astype(F32)
                self.got = [near]
                self.flying = self.order.ring(total.astype(self.between), self.axis, 3)
                self.hop = 1
            elif self.hop == 1:
                self.got.append(self.order.wait(self.flying))
                self.hop = self.n - 1
            return
        if self.direct:
            if self.n > 1:
                got = self.order.wait(*self.flying)
                self.got = [got] if self.n == 2 else list(got)
            self.hop = self.n - 1
            return
        self.got = [self.order.wait(self.flying)]
        self.hop += 1
        if self.hop < self.n - 1:
            total = self.got[0].astype(F32) + self.blocks[self.hop].astype(F32)
            self.flying = self.order.ring(total.astype(self.between), self.axis)

    def done(self, parts=0, dtype=BF):
        while self.hop < self.n - 1:
            self.next()
        terms = [self.blocks[-1]] + (self.got if self.n > 1 else [])

        def total(pick):
            values = [pick(t).astype(F32) for t in terms]
            return functools.reduce(jnp.add, values).astype(dtype)

        if not parts:
            return total(lambda t: t)
        return [total(lambda t, i=i: t[i]) for i in range(parts)]


def behind(place, order_of_axes, value):
    for dim, axis in enumerate(("z", "y", "x")):
        n, at = place.size[axis], place.at[axis]
        picks = [
            lax.dynamic_index_in_dim(value, lax.rem(at - i - 1 + 2 * n, n), dim)
            for i in range(n)
        ]
        value = jnp.concatenate(picks, axis=dim)
    dims = ["zyx".index(axis) for axis in order_of_axes]
    return jnp.transpose(value, tuple(dims) + tuple(range(3, value.ndim)))


def sources(place, order_of_axes, rows):
    lead = tuple(place.size[a] for a in "zyx")
    at = jnp.arange(math.prod(lead) * rows, dtype=jnp.int32).reshape(lead + (rows,))
    return behind(place, order_of_axes, at).reshape(-1)


def compose(earlier, later):
    return jnp.concatenate(
        [earlier[:4] * later[:4], later[:4] * earlier[4:] + later[4:]], axis=0
    )


class Carry:
    def __init__(self, order, end_map, sign, most=3):
        self.order, self.sign, self.most = order, sign, most
        self.n = order.place.seq
        self.unit = jnp.concatenate(
            [jnp.ones_like(end_map[:4]), jnp.zeros_like(end_map[4:])], axis=0
        )
        self.total = None
        self.reach = 0
        self.send(end_map, 1)

    def send(self, value, width):
        self.shifts = []
        distance = max(self.reach, 1)
        while distance < self.n and len(self.shifts) < self.most:
            self.shifts.append(distance)
            distance += width
        self.width = width
        self.flying = [self.order.along(value, self.sign * d) for d in self.shifts]

    def next(self):
        got = self.order.wait(*self.flying)
        got = [got] if len(self.flying) == 1 else list(got)
        s, n = self.order.place.s, self.n
        for value, d in zip(got, self.shifts):
            inside = (s >= d) if self.sign > 0 else (s < n - d)
            part = jnp.where(inside, value, self.unit)
            self.total = part if self.total is None else compose(part, self.total)
        self.reach += self.width * len(self.shifts)
        if self.reach < self.n - 1:
            self.send(self.total, self.reach)
            return True
        return False

    def done(self):
        while self.next():
            pass
        return self.total[4:]


def dot(a, b):
    return jnp.dot(a, b, preferred_element_type=F32)


def dot_nt(a, b):
    return lax.dot_general(a, b, (((1,), (1,)), ((), ())), preferred_element_type=F32)


def dot_tn(a, b):
    return lax.dot_general(a, b, (((0,), (0,)), ((), ())), preferred_element_type=F32)


def moved(value, distance, fill):
    n = value.shape[0]
    size = abs(distance)
    edge = jnp.full((size,) + value.shape[1:], fill, value.dtype)
    if size % 8 == 0:
        if distance > 0:
            return jnp.concatenate([edge, value[: n - size]], axis=0)
        return jnp.concatenate([value[size:], edge], axis=0)
    at = lax.broadcasted_iota(jnp.int32, value.shape, 0)
    turned = pltpu.roll(value, distance % n, 0)
    inside = at >= size if distance > 0 else at < n - size
    return jnp.where(inside, turned, fill)


def scan_tile(decay, drive, sign):
    n = decay.shape[0]
    distance = 1
    while distance < n:
        drive = decay * moved(drive, sign * distance, 0.0) + drive
        decay = decay * moved(decay, sign * distance, 1.0)
        distance *= 2
    return decay, drive


def one_less_exp(u):
    term = jnp.full_like(u, 1.0 / 3628800.0)
    for k in (362880, 40320, 5040, 720, 120, 24, 6, 2):
        term = 1.0 / k - u * term
    small = u * (1.0 - u * term)
    return jnp.where(u < 0.8, small, 1.0 - jnp.exp(-u))


def log2(n):
    return n.bit_length() - 1


def source_rows(order, sizes, at_ref, rows, first, count):
    spot = {"z": at_ref[0], "y": at_ref[1], "x": at_ref[2]}
    size = dict(zip("zyx", sizes))
    line = first + lax.broadcasted_iota(jnp.int32, (count, 1), 0)
    inside = line & (rows - 1)
    line = line >> log2(rows)
    where = {}
    for axis in reversed(order):
        n = size[axis]
        where[axis] = (spot[axis] + (n - 1) - (line & (n - 1))) & (n - 1)
        line = line >> log2(n)
    chip = (where["z"] * size["y"] + where["y"]) * size["x"] + where["x"]
    return chip * rows + inside


def turn_rows(order, sizes, at_ref, value, rows, out_ref):
    total = value.shape[1]
    step = min(total, 256)
    for first in range(0, total, step):
        source = source_rows(order, sizes, at_ref, rows, first, step)
        lane = lax.broadcasted_iota(jnp.int32, (step, total), 1)
        pick = jnp.where(source == lane, 1.0, 0.0).astype(BF)
        out_ref[first : first + step] = dot_nt(pick, value).astype(BF)


def gelu_parts(value):
    square = value * value
    t = jnp.tanh(GELU_C * value * (1.0 + 0.044715 * square))
    half = 0.5 * (1.0 + t)
    slope = half + 0.5 * value * (1.0 - t * t) * GELU_C * (1.0 + 3.0 * 0.044715 * square)
    return value * half, slope


def full(shape):
    return pl.BlockSpec(shape, lambda j: (0,) * len(shape))


def columns(rows, width=TILE):
    return pl.BlockSpec((rows, width), lambda j: (0, j))


def lines(rows, width):
    return pl.BlockSpec((rows, width), lambda j: (j, 0))


def in_hbm(shape, dtype):
    return pltpu.HBM(shape, dtype)


def shape_of(shape, dtype):
    return jax.ShapeDtypeStruct(shape, dtype)


def params(limit):
    return pltpu.CompilerParams(vmem_limit_bytes=limit * MIB)


LIGHT = pl.CostEstimate(flops=1, bytes_accessed=1, transcendentals=0)


def turn_kernel(sizes, rows, at_ref, first_ref, left_ref, right_ref):
    turn_rows("xyz", sizes, at_ref, first_ref[...], rows, left_ref)
    turn_rows("yxz", sizes, at_ref, first_ref[...], rows, right_ref)


def turn_call(place, first, rows):
    length, model = first.shape
    whole = pl.BlockSpec(memory_space=pltpu.VMEM)
    return pl.pallas_call(
        functools.partial(turn_kernel, place.sizes, rows),
        in_specs=[pl.BlockSpec(memory_space=pltpu.SMEM), whole],
        out_specs=[whole] * 2,
        out_shape=[shape_of((model, length), BF)] * 2,
        compiler_params=params(24),
        cost_estimate=LIGHT,
        name="turn",
    )(place.where, first)


def small_kernel(d_rows, r_rows, at_ref, small_ref, qd_ref, md_ref, qr_ref, mr_ref, gain_ref, vec_ref):
    def spread(row, q_ref, m_ref):
        value = dot(small_ref[:, row, :], q_ref[...])
        return jnp.sum(value * m_ref[...], axis=0, keepdims=True)

    for k in range(2):
        gain_ref[k : k + 1] = spread(k, qd_ref, md_ref)
    half = vec_ref.shape[1]
    for k in range(8):
        value = spread(2 + k, qr_ref, mr_ref)
        value = jnp.where(at_ref[3] == 0, value[:, :half], value[:, half:])
        if k == 7:
            soft = jnp.maximum(value, 0.0) + jnp.log1p(jnp.exp(-jnp.abs(value)))
            vec_ref[8:9] = -8.0 * jax.nn.sigmoid(value)
            value = 8.0 * soft
        vec_ref[k : k + 1] = value


def small_call(place, small, d_rows, r_rows):
    devices, _, span = small.shape
    operands = []
    for rows in (d_rows, r_rows):
        lane = np.arange(devices * rows)
        operands.append(jnp.asarray(lane[None] % rows == np.arange(span)[:, None], BF))
        operands.append(jnp.asarray(lane[None] // rows == np.arange(devices)[:, None], F32))
    whole = pl.BlockSpec(memory_space=pltpu.VMEM)
    return pl.pallas_call(
        functools.partial(small_kernel, d_rows, r_rows),
        in_specs=[pl.BlockSpec(memory_space=pltpu.SMEM)] + [whole] * 5,
        out_specs=[whole] * 2,
        out_shape=[shape_of((2, devices * d_rows), F32), shape_of((16, devices * r_rows // 2), F32)],
        compiler_params=params(24),
        cost_estimate=LIGHT,
        name="small_weights",
    )(place.where, small, *operands)


def norm_kernel(n_terms, row, *refs):
    terms, gain_ref, outs = refs[:n_terms], refs[n_terms], refs[n_terms + 1 :]
    value = functools.reduce(jnp.add, [t[...] for t in terms])
    scale = lax.rsqrt(jnp.mean(value * value, axis=-1, keepdims=True) + EPS)
    outs[0][...] = (value * scale * gain_ref[row : row + 1]).astype(BF)
    if n_terms > 1:
        outs[1][...] = value


def norm_call(terms, gains, row):
    tokens, model = terms[0].shape
    step = tokens // 4
    block = pl.BlockSpec((step, model), lambda j: (j, 0))
    shapes = [in_hbm((tokens, model), BF), shape_of((tokens, model), F32)]
    shapes = shapes[: 1 if len(terms) == 1 else 2]
    return pl.pallas_call(
        functools.partial(norm_kernel, len(terms), row),
        grid=(4,),
        in_specs=[block] * len(terms) + [full(gains.shape)],
        out_specs=[block] * len(shapes),
        out_shape=shapes,
        compiler_params=params(16),
        cost_estimate=LIGHT,
        name="norm",
    )(*terms, gains)


def norm_back_kernel(n_terms, row, low, *refs):
    terms = refs[:n_terms]
    value_ref, gain_ref, add_ref, out_ref = refs[n_terms : n_terms + 4]
    gain_out = refs[-1]
    grad = functools.reduce(jnp.add, [t[...] for t in terms])
    value = value_ref[...]
    scale = lax.rsqrt(jnp.mean(value * value, axis=-1, keepdims=True) + EPS)
    unit = value * scale
    inner = grad * gain_ref[row : row + 1]
    total = add_ref[...] + scale * (inner - unit * jnp.mean(inner * unit, axis=-1, keepdims=True))
    out_ref[...] = total
    if low:
        refs[n_terms + 4][...] = total.astype(BF)
    part = jnp.sum(grad * unit, axis=0, keepdims=True)

    @pl.when(pl.program_id(0) == 0)
    def _():
        gain_out[...] = part

    @pl.when(pl.program_id(0) > 0)
    def _():
        gain_out[...] += part


def norm_back_call(terms, value, gains, row, add, low):
    tokens, model = value.shape
    step = tokens // 4
    block = pl.BlockSpec((step, model), lambda j: (j, 0))
    shapes = [shape_of((tokens, model), F32)] + [in_hbm((tokens, model), BF)] * low
    return pl.pallas_call(
        functools.partial(norm_back_kernel, len(terms), row, low),
        grid=(4,),
        in_specs=[block] * len(terms) + [block, full(gains.shape), block],
        out_specs=[block] * len(shapes) + [full((1, model))],
        out_shape=shapes + [shape_of((1, model), F32)],
        compiler_params=params(16),
        cost_estimate=LIGHT,
        name="norm_back",
    )(*terms, value, gains, add)


def pack_kernel(at_ref, go_ref, gr_ref, gi_ref, gvec_ref, vec_ref, mine_ref, other_ref):
    pairs, rows, _ = mine_ref.shape
    model, block = go_ref.shape[1], gr_ref.shape[1]
    line = lax.broadcasted_iota(jnp.int32, gvec_ref.shape, 0)
    gvec = jnp.where(line == 7, gvec_ref[...] * vec_ref[8:9], gvec_ref[...]).astype(BF)
    slot = lax.broadcasted_iota(jnp.int32, (8, block), 0)
    lane = lax.broadcasted_iota(jnp.int32, (8, block), 1)
    turned = dot_tn(gvec, jnp.where(slot == lane, 1.0, 0.0).astype(BF)).astype(BF)
    gr, gi = gr_ref[...].astype(BF), gi_ref[...].astype(BF)
    for k in range(2):

        @pl.when(at_ref[3] == k)
        def _():
            for q in range(pairs):
                for ref, which in ((mine_ref, k), (other_ref, 1 - k)):
                    span = slice((2 * q + which) * rows, (2 * q + which + 1) * rows)
                    ref[q, :, 0:model] = go_ref[span]
                    ref[q, :, model : model + block] = gr[span]
                    ref[q, :, model + block : model + 2 * block] = gi[span]
                    ref[q, :, model + 2 * block :] = turned[span]


def pack_call(place, g_out, g_gate_r, g_gate_i, g_vec, vec, rows):
    width, model = g_out.shape
    block = g_gate_r.shape[1]
    shape = (width // (2 * rows), rows, model + 3 * block)
    whole = pl.BlockSpec(memory_space=pltpu.VMEM)
    return pl.pallas_call(
        pack_kernel,
        in_specs=[pl.BlockSpec(memory_space=pltpu.SMEM)] + [whole] * 5,
        out_specs=[whole] * 2,
        out_shape=[shape_of(shape, BF), shape_of(shape, BF)],
        compiler_params=params(24),
        cost_estimate=LIGHT,
        name="pack",
    )(place.where, g_out, g_gate_r, g_gate_i, g_vec, vec)


def forward_kernel(
    n_rows,
    group,
    block,
    mine_ref,
    other_ref,
    halo_ref,
    w_ref,
    wb_ref,
    vec_ref,
    mask_ref,
    gr_ref,
    gi_ref,
    first_ref,
    bpre_ref,
    mixer_ref,
    conv_ref,
    rpre_ref,
    ipre_ref,
    through_ref,
    local_ref,
    ends_ref,
    ext_ref,
):
    half = mine_ref.shape[0]

    @pl.when(pl.program_id(0) == 0)
    def _():
        first_ref[0:half] = mine_ref[...]
        first_ref[half : 2 * half] = other_ref[...]
        first_ref[2 * half :] = halo_ref[...]

    mixer = dot(first_ref[...], w_ref[...]).astype(BF)
    bpre_ref[...] = dot(first_ref[0 : 2 * half], wb_ref[...])
    mixer_ref[...] = mixer
    wide = mixer.astype(F32)
    tokens = n_rows * group
    for r in range(n_rows):
        ext_ref[r, 0:HALO] = wide[tokens + HALO * r : tokens + HALO * (r + 1)]
        ext_ref[r, HALO : HALO + group] = wide[r * group : (r + 1) * group]
    for r in range(n_rows):
        span = slice(r * group, (r + 1) * group)
        conv = vec_ref[4:5] + vec_ref[0:1] * ext_ref[r, HALO : HALO + group]
        for k in range(1, 4):
            conv += (
                vec_ref[k : k + 1]
                * ext_ref[r, HALO - k : HALO - k + group]
                * mask_ref[span, k : k + 1]
            )
        conv_ref[span] = conv.astype(BF)
    for h in range(w_ref.shape[1] // block):
        cols = slice(h * block, (h + 1) * block)
        low = conv_ref[:, cols]
        rpre_ref[:, cols] = dot(low, gr_ref[cols]) + vec_ref[5:6, cols]
        ipre_ref[:, cols] = dot(low, gi_ref[cols]) + vec_ref[6:7, cols]
        for r in range(n_rows):
            span = slice(r * group, (r + 1) * group)
            recur = jax.nn.sigmoid(rpre_ref[span, cols])
            admit = jax.nn.sigmoid(ipre_ref[span, cols])
            rate = vec_ref[7:8, cols] * recur
            reset = mask_ref[span, 0:1]
            decay = jnp.exp(-rate) * (1.0 - reset)
            scale = jnp.where(reset > 0.5, 1.0, jnp.sqrt(one_less_exp(2.0 * rate)))
            drive = scale * admit * conv_ref[span, cols].astype(F32)
            decay, drive = scan_tile(decay, drive, 1)
            through_ref[span, cols] = decay
            local_ref[span, cols] = drive
            ends_ref[r : r + 1, cols] = decay[group - 1 : group]
            ends_ref[n_rows + r : n_rows + r + 1, cols] = drive[group - 1 : group]


def forward_call(mine, other, halo, w_in, w_branch, vec, masks, gate_r, gate_i, n_rows, group):
    model = mine.shape[1]
    length = 2 * mine.shape[0] + halo.shape[0]
    width, block = w_in.shape[1], gate_r.shape[1]
    tokens = n_rows * group
    tile = TILE
    return pl.pallas_call(
        functools.partial(forward_kernel, n_rows, group, block),
        grid=(width // tile,),
        in_specs=[
            full(mine.shape),
            full(mine.shape),
            full(halo.shape),
            columns(model),
            columns(model),
            columns(16),
            full(masks.shape),
            lines(tile, block),
            lines(tile, block),
        ],
        out_specs=[full((length, model)), columns(tokens), columns(length)] + [columns(tokens)] * 5 + [columns(2 * n_rows)],
        out_shape=[
            shape_of((length, model), BF),
            shape_of((tokens, width), F32),
            shape_of((length, width), BF),
            shape_of((tokens, width), BF),
            shape_of((tokens, width), F32),
            shape_of((tokens, width), F32),
            shape_of((tokens, width), F32),
            shape_of((tokens, width), F32),
            shape_of((2 * n_rows, width), F32),
        ],
        scratch_shapes=[pltpu.VMEM((n_rows, HALO + group, tile), F32)],
        compiler_params=params(24),
        cost_estimate=LIGHT,
        name="recurrence_forward",
    )(mine, other, halo, w_in, w_branch, vec, masks, gate_r, gate_i)


def mix_kernel(
    n_rows, group, local_ref, through_ref, enter_ref, bpre_ref, w_ref, state_ref, mixed_ref, part_ref, part_other_ref
):
    for r in range(n_rows):
        span = slice(r * group, (r + 1) * group)
        state = local_ref[span] + through_ref[span] * enter_ref[r : r + 1]
        state_ref[span] = state
        branch, _ = gelu_parts(bpre_ref[span])
        mixed_ref[span] = (state * branch).astype(BF)
    part = dot(mixed_ref[...], w_ref[...])
    half = part_ref.shape[0]

    @pl.when(pl.program_id(0) == 0)
    def _():
        part_ref[...] = part[:half]
        part_other_ref[...] = part[half:]

    @pl.when(pl.program_id(0) > 0)
    def _():
        part_ref[...] += part[:half]
        part_other_ref[...] += part[half:]


def mix_call(local, through, enter, branch_pre, w_out, n_rows, group):
    tokens, width = local.shape
    model = w_out.shape[1]
    return pl.pallas_call(
        functools.partial(mix_kernel, n_rows, group),
        grid=(width // TILE,),
        in_specs=[
            columns(tokens),
            columns(tokens),
            columns(n_rows),
            columns(tokens),
            lines(TILE, model),
        ],
        out_specs=[columns(tokens), columns(tokens)] + [full((tokens // 2, model))] * 2,
        out_shape=[
            shape_of((tokens, width), F32),
            shape_of((tokens, width), BF),
            shape_of((tokens // 2, model), F32),
            in_hbm((tokens // 2, model), F32),
        ],
        compiler_params=params(24),
        cost_estimate=LIGHT,
        name="mix",
    )(local, through, enter, branch_pre, w_out)


def ffn_kernel(
    sizes,
    rows,
    at_ref,
    mine_ref,
    other_ref,
    low_mine_ref,
    low_other_ref,
    wg_ref,
    wu_ref,
    wd_ref,
    gg_send_ref,
    gg_ref,
    gu_send_ref,
    gu_ref,
    gd_ref,
    gd_other_ref,
    part_ref,
    part_other_ref,
    back_ref,
    back_other_ref,
    second_ref,
    low_ref,
    left_ref,
    right_ref,
    down_ref,
):
    step = pl.program_id(0)
    half = mine_ref.shape[0]

    @pl.when(step == 0)
    def _():
        second_ref[0:half] = mine_ref[...]
        second_ref[half:] = other_ref[...]
        low_ref[0:half] = low_mine_ref[...]
        low_ref[half:] = low_other_ref[...]
        turn_rows("xyz", sizes, at_ref, second_ref[...], rows, left_ref)
        turn_rows("yxz", sizes, at_ref, second_ref[...], rows, right_ref)

    second, low = second_ref[...], low_ref[...]
    gate = dot(second, wg_ref[...])
    up = dot(second, wu_ref[...])
    grad = dot_nt(low, wd_ref[...])
    active, slope = gelu_parts(gate)
    hidden = (active * up).astype(BF)
    gate_low = (grad * up * slope).astype(BF)
    up_low = (grad * active).astype(BF)
    sent = gg_send_ref.shape[0]
    gg = dot(left_ref[...], gate_low).astype(BF)
    gg_send_ref[...] = gg[:sent]
    gg_ref[...] = gg[sent:]
    sent = gu_send_ref.shape[0]
    gu = dot(right_ref[...], up_low).astype(BF)
    gu_send_ref[...] = gu[:sent]
    gu_ref[...] = gu[sent:]
    width = hidden.shape[1]
    down_ref[pl.ds(step * width, width)] = dot_tn(hidden, low).astype(BF)
    part = dot(hidden, wd_ref[...])
    back = dot_nt(gate_low, wg_ref[...]) + dot_nt(up_low, wu_ref[...])

    @pl.when(step == 0)
    def _():
        part_ref[...] = part[:half]
        part_other_ref[...] = part[half:]
        back_ref[...] = back[:half]
        back_other_ref[...] = back[half:]

    @pl.when(step > 0)
    def _():
        part_ref[...] += part[:half]
        part_other_ref[...] += part[half:]
        back_ref[...] += back[:half]
        back_other_ref[...] += back[half:]

    pairs, lines_down, _ = gd_ref.shape
    for k in range(2):

        @pl.when((step == pl.num_programs(0) - 1) & (at_ref[3] == k))
        def _():
            for q in range(pairs):
                at = 2 * q * lines_down
                near, far = at + k * lines_down, at + (1 - k) * lines_down
                gd_ref[q] = down_ref[near : near + lines_down]
                gd_other_ref[q] = down_ref[far : far + lines_down]


def ffn_call(place, mine, other, low_mine, low_other, w_gate, w_up, w_down, chip_d, f_rows):
    tokens, model = 2 * mine.shape[0], mine.shape[1]
    width = w_gate.shape[1]
    sent_l, sent_r = model // place.size["x"], model // place.size["y"]
    rows = [sent_l, model - sent_l, sent_r, model - sent_r]
    down = (width // (2 * f_rows), f_rows, model)
    return pl.pallas_call(
        functools.partial(ffn_kernel, place.sizes, chip_d),
        grid=(width // TILE,),
        in_specs=[
            pl.BlockSpec(memory_space=pltpu.SMEM),
            full((tokens // 2, model)),
            full((tokens // 2, model)),
            full((tokens // 2, model)),
            full((tokens // 2, model)),
            columns(model),
            columns(model),
            lines(TILE, model),
        ],
        out_specs=[columns(n) for n in rows]
        + [full(down)] * 2
        + [full((tokens // 2, model))] * 4,
        out_shape=[in_hbm((n, width), BF) for n in rows]
        + [shape_of(down, BF), in_hbm(down, BF)]
        + [shape_of((tokens // 2, model), F32), in_hbm((tokens // 2, model), F32)] * 2,
        scratch_shapes=[
            pltpu.VMEM((tokens, model), BF),
            pltpu.VMEM((tokens, model), BF),
            pltpu.VMEM((model, tokens), BF),
            pltpu.VMEM((model, tokens), BF),
            pltpu.VMEM((width, model), BF),
        ],
        compiler_params=params(52),
        cost_estimate=LIGHT,
        name="feed_forward",
    )(place.where, mine, other, low_mine, low_other, w_gate, w_up, w_down)


def split_kernel(cuts, at_ref, whole_ref, *outs):
    count = outs[0].shape[0]
    for q in range(count):
        for out, (low, high) in zip(outs, cuts):
            out[q] = whole_ref[at_ref[3] * count + q, low:high]


def split_call(place, whole, cuts):
    count, _, width = whole.shape
    shapes = [(count // 2, high - low, width) for low, high in cuts]
    spec = pl.BlockSpec(memory_space=pltpu.VMEM)
    outs = pl.pallas_call(
        functools.partial(split_kernel, cuts),
        in_specs=[pl.BlockSpec(memory_space=pltpu.SMEM), spec],
        out_specs=[spec] * len(cuts),
        out_shape=[shape_of(shape, BF) for shape in shapes],
        compiler_params=params(32),
        cost_estimate=LIGHT,
        name="split",
    )(place.where, whole)
    return [out.reshape(-1, width) for out in outs]


def regroup_kernel(sizes, order_of, cuts, at_ref, mine_ref, got_ref, *outs):
    nz, ny, nx = sizes
    size = {"z": nz, "y": ny, "x": nx}
    spot = {"z": at_ref[0], "y": at_ref[1], "x": at_ref[2]}
    half = mine_ref.shape[0]
    for index, order in enumerate(order_of):
        send_ref, rest_ref = outs[2 * index], outs[2 * index + 1]
        span = slice(*cuts[index])
        for i0 in range(size[order[0]]):
            for i1 in range(size[order[1]]):
                for i2 in range(size[order[2]]):
                    place = {}
                    for axis, i in zip(order, (i0, i1, i2)):
                        n = size[axis]
                        place[axis] = lax.rem(spot[axis] + (n - 1 - i), n)
                    chip = (place["z"] * ny + place["y"]) * nx + place["x"]
                    here = lax.rem(chip, half)
                    own = lax.div(chip, half) == at_ref[3]
                    value = jnp.where(own, mine_ref[here][:, span], got_ref[here][:, span])
                    if i0 == 0:
                        send_ref[i1, i2] = value
                    else:
                        rest_ref[i0 - 1, i1, i2] = value


def regroup_call(place, mine, got, order_of, cuts):
    sizes = tuple(place.size[a] for a in "zyx")
    rows = mine.shape[1]
    shapes = []
    for order, (low, high) in zip(order_of, cuts):
        n0, n1, n2 = (place.size[a] for a in order)
        shapes.append((n1, n2, rows, high - low))
        shapes.append((n0 - 1, n1, n2, rows, high - low))
    whole = pl.BlockSpec(memory_space=pltpu.VMEM)
    outs = pl.pallas_call(
        functools.partial(regroup_kernel, sizes, order_of, cuts),
        in_specs=[pl.BlockSpec(memory_space=pltpu.SMEM), whole, whole],
        out_specs=[whole] * len(shapes),
        out_shape=[shape_of(shape, BF) for shape in shapes],
        compiler_params=params(24),
        cost_estimate=LIGHT,
        name="regroup",
    )(place.where, mine, got)
    return [
        [outs[2 * i]] + [outs[2 * i + 1][j] for j in range(shapes[2 * i + 1][0])]
        for i in range(len(order_of))
    ]


def decay_of(rpre, vec7, reset):
    recur = jax.nn.sigmoid(rpre)
    rate = vec7 * recur
    return recur, rate, jnp.exp(-rate) * (1.0 - reset)


def back_kernel(
    n_rows,
    group,
    mine_ref,
    other_ref,
    w_ref,
    bpre_ref,
    state_ref,
    rpre_ref,
    mixed_ref,
    vec_ref,
    mask_ref,
    right_ref,
    go_ref,
    gb_send_ref,
    gb_ref,
    gbl_ref,
    reach_ref,
    local_ref,
    ends_ref,
    low_ref,
    grad_ref,
):
    @pl.when(pl.program_id(0) == 0)
    def _():
        half = mine_ref.shape[0]
        low_ref[0:half] = mine_ref[...]
        low_ref[half:] = other_ref[...]

    low = low_ref[...]
    grad_ref[...] = dot_nt(low, w_ref[...])
    go_ref[...] = dot_tn(mixed_ref[...], low).astype(BF)
    half = w_ref.shape[0] // 2
    for h in range(2):
        cols = slice(h * half, (h + 1) * half)
        for r in range(n_rows):
            span = slice(r * group, (r + 1) * group)
            branch, slope = gelu_parts(bpre_ref[span, cols])
            grad = grad_ref[span, cols]
            gbl_ref[span, cols] = (grad * state_ref[span, cols] * slope).astype(BF)
            _, _, decay = decay_of(rpre_ref[span, cols], vec_ref[7:8, cols], mask_ref[span, 0:1])
            ahead = moved(decay, -1, 1.0)
            reach, local = scan_tile(ahead, grad * branch, -1)
            reach_ref[span, cols] = reach
            local_ref[span, cols] = local
            ends_ref[r : r + 1, cols] = decay[0:1] * reach[0:1]
            ends_ref[n_rows + r : n_rows + r + 1, cols] = decay[0:1] * local[0:1]
    sent = gb_send_ref.shape[0]
    gb = dot(right_ref[:, 0 : gbl_ref.shape[0]], gbl_ref[...]).astype(BF)
    gb_send_ref[...] = gb[:sent]
    gb_ref[...] = gb[sent:]


def back_call(place, mine, other, w_out, branch_pre, state, rpre, mixed, vec, masks, right, n_rows, group):
    model, length = right.shape
    tokens = state.shape[0]
    sent = model // place.size["y"]
    width = w_out.shape[0]
    return pl.pallas_call(
        functools.partial(back_kernel, n_rows, group),
        grid=(width // TILE,),
        in_specs=[
            full((tokens // 2, model)),
            full((tokens // 2, model)),
            lines(TILE, model),
            columns(tokens),
            columns(tokens),
            columns(tokens),
            columns(tokens),
            columns(16),
            full(masks.shape),
            full((model, length)),
        ],
        out_specs=[
            lines(TILE, model),
            columns(sent),
            columns(model - sent),
            columns(tokens),
            columns(tokens),
            columns(tokens),
            columns(2 * n_rows),
        ],
        out_shape=[
            shape_of((width, model), BF),
            in_hbm((sent, width), BF),
            in_hbm((model - sent, width), BF),
            shape_of((tokens, width), BF),
            shape_of((tokens, width), F32),
            shape_of((tokens, width), F32),
            shape_of((2 * n_rows, width), F32),
        ],
        scratch_shapes=[pltpu.VMEM((tokens, model), BF), pltpu.VMEM((tokens, TILE), F32)],
        compiler_params=params(32),
        cost_estimate=LIGHT,
        name="recurrence_back",
    )(mine, other, w_out, branch_pre, state, rpre, mixed, vec, masks, right)


def gates_kernel(
    n_rows,
    group,
    block,
    reach_ref,
    local_ref,
    leave_ref,
    state_ref,
    enter_ref,
    rpre_ref,
    ipre_ref,
    conv_ref,
    mixer_ref,
    vec_ref,
    mask_ref,
    gr_ref,
    gi_ref,
    left_ref,
    win_ref,
    wbr_ref,
    gbl_ref,
    gin_send_ref,
    gin_ref,
    ggr_ref,
    ggi_ref,
    gvec_ref,
    gfirst_ref,
    rlow_ref,
    ilow_ref,
    gconv_ref,
    ext_ref,
    spread_ref,
    gm_ref,
):
    step = pl.program_id(0)
    tokens = n_rows * group

    gvec_ref[...] = jnp.zeros_like(gvec_ref)
    for h in range(win_ref.shape[1] // block):
        cols = slice(h * block, (h + 1) * block)
        for r in range(n_rows):
            span = slice(r * group, (r + 1) * group)
            adjoint = local_ref[span, cols] + reach_ref[span, cols] * leave_ref[r : r + 1, cols]
            state = state_ref[span, cols]
            at = lax.broadcasted_iota(jnp.int32, state.shape, 0)
            before = jnp.where(at == 0, enter_ref[r : r + 1, cols], pltpu.roll(state, 1, 0))
            reset = mask_ref[span, 0:1]
            live = 1.0 - reset
            recur, rate, decay = decay_of(rpre_ref[span, cols], vec_ref[7:8, cols], reset)
            admit = jax.nn.sigmoid(ipre_ref[span, cols])
            full_decay = jnp.exp(-rate)
            root = jnp.sqrt(one_less_exp(2.0 * rate))
            scale = jnp.where(reset > 0.5, 1.0, root)
            conv = conv_ref[span, cols].astype(F32)
            direct = adjoint * scale
            gadmit = direct * conv
            gconv_ref[span, cols] = direct * admit
            gscale = adjoint * admit * conv
            glog = live * full_decay * (adjoint * before - gscale * full_decay / root)
            gvec_ref[7:8, cols] += jnp.sum(glog * recur, axis=0, keepdims=True)
            grecur = -(vec_ref[7:8, cols] * glog) * recur * (1.0 - recur)
            ginput = gadmit * admit * (1.0 - admit)
            rlow, ilow = grecur.astype(BF), ginput.astype(BF)
            rlow_ref[span, cols] = rlow
            ilow_ref[span, cols] = ilow
            gvec_ref[5:6, cols] += jnp.sum(rlow.astype(F32), axis=0, keepdims=True)
            gvec_ref[6:7, cols] += jnp.sum(ilow.astype(F32), axis=0, keepdims=True)
        rlow, ilow = rlow_ref[:, cols], ilow_ref[:, cols]
        low = conv_ref[:, cols]
        ggr_ref[cols] = dot_tn(low, rlow)
        ggi_ref[cols] = dot_tn(low, ilow)
        gconv_ref[:, cols] += dot_nt(rlow, gr_ref[cols]) + dot_nt(ilow, gi_ref[cols])
        for r in range(n_rows):
            span = slice(r * group, (r + 1) * group)
            head = slice(tokens + HALO * r, tokens + HALO * (r + 1))
            ext_ref[0:HALO] = mixer_ref[head, cols].astype(F32)
            ext_ref[HALO : HALO + group] = mixer_ref[span, cols].astype(F32)
            gconv = gconv_ref[span, cols]
            gvec_ref[4:5, cols] += jnp.sum(gconv, axis=0, keepdims=True)
            gvec_ref[0:1, cols] += jnp.sum(
                gconv * ext_ref[HALO : HALO + group], axis=0, keepdims=True
            )
            spread_ref[0:HALO] = jnp.zeros((HALO, block), F32)
            spread_ref[HALO : HALO + group] = vec_ref[0:1, cols] * gconv
            for k in range(1, 4):
                masked = gconv * mask_ref[span, k : k + 1]
                there = slice(HALO - k, HALO - k + group)
                gvec_ref[k : k + 1, cols] += jnp.sum(
                    masked * ext_ref[there], axis=0, keepdims=True
                )
                spread_ref[there] += vec_ref[k : k + 1, cols] * masked
            gm_ref[head, cols] = spread_ref[0:HALO].astype(BF)
            gm_ref[span, cols] = spread_ref[HALO : HALO + group].astype(BF)
    gm = gm_ref[...]
    sent = gin_send_ref.shape[0]
    gin = dot(left_ref[...], gm).astype(BF)
    gin_send_ref[...] = gin[:sent]
    gin_ref[...] = gin[sent:]
    part = dot_nt(gm, win_ref[...])
    part_branch = dot_nt(gbl_ref[...], wbr_ref[...])

    @pl.when(step == 0)
    def _():
        gfirst_ref[...] = part

    @pl.when(step > 0)
    def _():
        gfirst_ref[...] += part

    gfirst_ref[0:tokens] += part_branch


def gates_call(
    place, reach, local, leave, state, enter, rpre, ipre, conv, mixer, vec, masks, gate_r, gate_i, left, w_in, w_branch, gbl, n_rows, group
):
    model, length = left.shape
    sent = model // place.size["x"]
    tokens, width = state.shape
    block = gate_r.shape[1]
    tile = TILE
    return pl.pallas_call(
        functools.partial(gates_kernel, n_rows, group, block),
        grid=(width // tile,),
        in_specs=[
            columns(tokens),
            columns(tokens),
            columns(n_rows),
            columns(tokens),
            columns(n_rows),
            columns(tokens),
            columns(tokens),
            columns(tokens),
            columns(length),
            columns(16),
            full(masks.shape),
            lines(tile, block),
            lines(tile, block),
            full((model, length)),
            columns(model),
            columns(model),
            columns(tokens),
        ],
        out_specs=[
            columns(sent),
            columns(model - sent),
            lines(tile, block),
            lines(tile, block),
            columns(8),
            full((length, model)),
        ],
        out_shape=[
            in_hbm((sent, width), BF),
            in_hbm((model - sent, width), BF),
            shape_of((width, block), F32),
            shape_of((width, block), F32),
            shape_of((8, width), F32),
            shape_of((length, model), F32),
        ],
        scratch_shapes=[
            pltpu.VMEM((tokens, tile), BF),
            pltpu.VMEM((tokens, tile), BF),
            pltpu.VMEM((tokens, tile), F32),
            pltpu.VMEM((HALO + group, block), F32),
            pltpu.VMEM((HALO + group, block), F32),
            pltpu.VMEM((length, tile), BF),
        ],
        compiler_params=params(40),
        cost_estimate=LIGHT,
        name="recurrence_gates",
    )(reach, local, leave, state, enter, rpre, ipre, conv, mixer, vec, masks, gate_r, gate_i, left, w_in, w_branch, gbl)


def normed(values, gain):
    return values * lax.rsqrt(jnp.mean(values * values, axis=-1, keepdims=True) + EPS) * gain


def halves(value, place, dim):
    half = value.shape[dim] // 2
    mine = lax.dynamic_slice_in_dim(value, place.at["c"] * half, half, dim)
    other = lax.dynamic_slice_in_dim(value, (1 - place.at["c"]) * half, half, dim)
    return mine, other


def own_channels(place, value):
    mine, other = halves(value, place, 0)
    got = place.ring(other, "c", 1)
    pair = place.ordered(mine, got)
    both = jnp.stack(pair, axis=1)
    return both.reshape(-1, both.shape[-1])


def own_devices(place, value, rows):
    shaped = value.reshape(place.chips // 2, 2, rows, value.shape[-1])
    mine = lax.dynamic_index_in_dim(shaped, place.at["c"], 1, keepdims=False)
    other = lax.dynamic_index_in_dim(shaped, 1 - place.at["c"], 1, keepdims=False)
    got = place.ring(other, "c", 1)
    return jnp.concatenate(place.ordered(mine, got), axis=0)


def on_device(
    inputs,
    cotangent,
    segments,
    norm1_gain,
    input_proj,
    branch_proj,
    conv_weight,
    conv_bias,
    recur_gate,
    input_gate,
    recur_bias,
    input_bias,
    decay_param,
    output_proj,
    norm2_gain,
    mlp_gate,
    mlp_up,
    mlp_down,
):
    place = Place()
    core = place.at["c"]
    chips = place.chips
    rows_dev, group, model = inputs.shape
    n_rows = 2 * rows_dev
    tokens_dev = rows_dev * group
    tokens = 2 * tokens_dev
    d_rows, lru = input_proj.shape
    ffn = mlp_gate.shape[1]
    r_rows, block = recur_gate.shape
    f_rows = mlp_down.shape[0]
    lru_half, ffn_half = lru // 2, ffn // 2
    pair = lambda value: place.ring(value, "c", 1)

    order = Order(place)
    lead = (place.size["z"], place.size["y"], place.size["x"])

    wide = [halves(w, place, 1) for w in (input_proj, branch_proj, mlp_gate, mlp_up)]
    got_a = order.ring(jnp.concatenate([w[1] for w in wide[:2]], axis=1), "c")
    got_c = order.ring(jnp.concatenate([w[1] for w in wide[2:]], axis=1), "c")
    span = max(d_rows, r_rows)
    lines_one = [
        jnp.pad(v, (0, span - v.shape[0]))[None]
        for v in (norm1_gain, norm2_gain, conv_bias, recur_bias, input_bias, decay_param)
    ]
    taps = jnp.pad(conv_weight, ((0, 0), (0, span - r_rows)))
    vectors = jnp.concatenate(lines_one[:2] + [taps] + lines_one[2:], axis=0)
    small = Gather(order, vectors[None, None, None, None], "y", 1)
    ids_pair = order.ring(segments, "c")
    mine_a = jnp.concatenate([w[0] for w in wide[:2]], axis=1)
    mine_c = jnp.concatenate([w[0] for w in wide[2:]], axis=1)
    gates = jnp.concatenate([recur_gate, input_gate], axis=0)
    gate_lines = 2 * r_rows * block // lru
    gates = gates.reshape(-1, gate_lines, block).transpose(1, 0, 2).reshape(gate_lines, lru)
    order.must(gates, mine_a)
    small = Gather(order, small.done(), "x", 2)
    got_a = order.wait(got_a)
    rows_a = jnp.concatenate(place.ordered(mine_a, got_a), axis=0)
    group_a = jnp.concatenate([rows_a, gates], axis=0)[None, None, None]
    order.must(group_a)
    both_whole = jnp.concatenate([output_proj, mlp_down], axis=0)
    both_whole = lax.all_gather(both_whole, AXES, axis=0)
    small = Gather(order, small.done(), "c", 3)
    small = Gather(order, small.done(), "z", 0, direct=True)

    a_z = Gather(order, group_a, "z", 0, direct=True)
    grad_out = cotangent.reshape(tokens_dev, model)
    low = grad_out.astype(BF)
    low_other = order.ring(low, "c")
    ids_pair, got_c = order.wait(ids_pair, got_c)
    ids = jnp.concatenate([segments, ids_pair], axis=0)
    prior_ids = order.along(ids[:, group - 3 :], 1)
    gains, vec = small_call(
        place, small.done().reshape(2 * chips, -1, span), d_rows, r_rows
    )
    flat = inputs.reshape(tokens_dev, model)
    (first,) = norm_call([flat], gains, 0)
    first_other = order.ring(first, "c")
    group_c = jnp.concatenate(place.ordered(mine_c, got_c), axis=0)[None, None, None]
    first_other, low_other = order.wait(first_other, low_other)
    tail = jnp.concatenate(
        [v.reshape(rows_dev, group, model)[:, group - 3 :] for v in (first, first_other)], axis=0
    )
    halo = order.along(tail, 1)
    c_z = Gather(order, group_c, "z", 0, both=True)
    a_z = a_z.done()
    halo, prior_ids = order.wait(halo, prior_ids)

    a_left = Gather(order, a_z[..., :lru_half], "y", 1)
    a_right = Gather(order, a_z[..., lru_half:], "x", 2)
    a_left, a_right = a_left.done(), a_right.done()

    a_left = Gather(order, a_left, "x", 2)
    a_right = Gather(order, a_right, "y", 1)
    c_z.next()
    a_left, a_right = a_left.done(), a_right.done()

    chip_d = 2 * d_rows
    packed = jnp.concatenate([a_left[..., chip_d:, :], a_right[..., chip_d:, :]], axis=-1)
    packed = packed.reshape(chips, gate_lines, -1, block)
    packed = packed.transpose(0, 2, 1, 3).reshape(chips, 2, r_rows, block)
    packed = jnp.concatenate([packed[:, 0], packed[:, 1]], axis=-1)
    gate_mine, gate_other = halves(packed, place, 0)
    gate_got = order.ring(gate_other, "c")
    c_z = c_z.done()
    c_left = Gather(order, c_z[..., :ffn_half], "y", 1)
    c_right = Gather(order, c_z[..., ffn_half:], "x", 2)
    w_in = a_left[..., :chip_d, :].reshape(model, lru_half)
    w_branch = a_right[..., :chip_d, :].reshape(model, lru_half)
    halo = jnp.pad(halo, ((0, 0), (HALO - 3, 0), (0, 0))).reshape(n_rows * HALO, model)
    position = place.s * group + jnp.arange(group, dtype=jnp.int32)
    joined_ids = jnp.concatenate([prior_ids, ids], axis=1)
    marks = [(joined_ids[:, 2 : 2 + group] != ids) | (position == 0)[None, :]]
    for k in range(1, 4):
        marks.append(
            (joined_ids[:, 3 - k : 3 - k + group] == ids) & (position >= k)[None, :]
        )
    masks = jnp.stack(marks, axis=-1).astype(F32).reshape(tokens, 4)
    masks = jnp.pad(masks, ((0, 0), (0, 4)))
    gate_got = order.wait(gate_got)
    packed = jnp.stack(place.ordered(gate_mine, gate_got), axis=1).reshape(-1, 2 * block)
    gate_r, gate_i = packed[:, :block], packed[:, block:]
    first_ext, branch_pre, mixer, conv, rpre, ipre, through, local, ends = forward_call(
        first, first_other, halo, w_in, w_branch, vec, masks, gate_r, gate_i, n_rows, group
    )
    enter = Carry(order, ends, 1)
    more = enter.next()
    c_left, c_right = c_left.done(), c_right.done()

    c_left = Gather(order, c_left, "x", 2)
    c_right = Gather(order, c_right, "y", 1)
    enter = enter.done() if more else enter.total[4:]
    both_whole = order.wait(both_whole)
    w_out, w_down = split_call(
        place, both_whole, ((0, r_rows), (r_rows, r_rows + f_rows))
    )
    state, mixed, part, part_other = mix_call(
        local, through, enter, branch_pre, w_out, n_rows, group
    )
    part_pair = order.ring(part_other, "c")
    first_l, first_r = turn_call(place, order.tie(first_ext), chip_d)
    order.must(first_l, first_r)
    w_gate = c_left.done().reshape(model, ffn_half)
    w_up = c_right.done().reshape(model, ffn_half)
    part_pair = order.wait(part_pair)
    second, middle = norm_call([flat, part, part_pair], gains, 1)
    second_other = order.ring(second, "c")
    order.must(w_gate, w_up)
    second_other = order.wait(second_other)

    nz, ny, nx = lead

    def blocks_of(send, rest, axis, other):
        shape = (place.size[other], nz, chip_d, -1)
        rest = rest.reshape((place.size[axis] - 1,) + shape)
        return [send.reshape(shape)] + [rest[i] for i in range(rest.shape[0])]

    def joined(left, right):
        return [jnp.concatenate(p, axis=-1) for p in zip(left.done(nz), right.done(nz))]

    g_send, g_rest, u_send, u_rest, down_mine, down_other, part, part_other, back, back_other = ffn_call(
        place, second, second_other, low, low_other, w_gate, w_up, w_down, chip_d, f_rows
    )

    back_pair = order.ring(back_other, "c")
    g_left = Scatter(order, blocks_of(g_send, g_rest, "x", "y"), "x")
    g_right = Scatter(order, blocks_of(u_send, u_rest, "y", "x"), "y")
    down_got = order.ring(down_other, "c")
    back_pair = order.wait(back_pair)
    grad_middle, mid_low, grad_gain_two = norm_back_call(
        [back, back_pair], middle, gains, 1, grad_out, 1
    )
    mid_pair = order.ring(mid_low, "c")
    mid_other = order.wait(mid_pair)
    g_out, b_send, b_rest, gbl, reach, local_back, ends_back = back_call(
        place, mid_low, mid_other, w_out, branch_pre, state, rpre, mixed, vec, masks, first_r, n_rows, group
    )
    leave = Carry(order, ends_back, -1)
    down_got = order.wait(down_got)
    (d_z,) = regroup_call(place, down_mine, down_got, ("zyx",), ((0, model),))
    order.must(d_z[0])
    g_left.next()
    g_right.next()
    more = leave.next()

    g_left = Scatter(order, g_left.done(ny), "y")
    g_right = Scatter(order, g_right.done(nx), "x")
    leave = leave.done() if more else leave.total[4:]
    d_z = Scatter(order, d_z, "z")
    in_send, in_rest, g_gate_r, g_gate_i, g_vec, grad_first = gates_call(
        place, reach, local_back, leave, state, enter, rpre, ipre, conv, mixer, vec, masks, gate_r, gate_i, first_l, w_in, w_branch, gbl, n_rows, group
    )
    order.must(in_send)
    g_left.next()
    g_right.next()
    d_z.next()

    a_left = Scatter(order, blocks_of(in_send, in_rest, "x", "y"), "x")
    a_right = Scatter(order, blocks_of(b_send, b_rest, "y", "x"), "y")
    g_both = Scatter(order, joined(g_left, g_right), "z", both=True)
    out_mine, out_other = pack_call(place, g_out, g_gate_r, g_gate_i, g_vec, vec, r_rows)
    out_got = order.ring(out_other, "c")
    out_got = order.wait(out_got)
    wide_r = out_mine.shape[-1]
    cut = (wide_r // (2 * block)) * block
    o_left, o_right = regroup_call(
        place, out_mine, out_got, ("xyz", "yxz"), ((0, cut), (cut, wide_r))
    )
    order.must(o_left[0], o_right[0])
    a_left.next()
    a_right.next()
    g_both.next()

    a_left = Scatter(order, a_left.done(ny), "y")
    a_right = Scatter(order, a_right.done(nx), "x")
    o_left = Scatter(order, o_left, "x")
    o_right = Scatter(order, o_right, "y")
    d_z.next()
    spill = grad_first[tokens:].reshape(n_rows, HALO, model)[:, HALO - 3 :]
    spill = order.along(spill, -1)
    a_left.next()
    a_right.next()
    o_left.next()
    o_right.next()

    a_both = Scatter(order, joined(a_left, a_right), "z", both=True)
    o_left = Scatter(order, o_left.done(ny), "y")
    o_right = Scatter(order, o_right.done(nx), "x")
    spill = order.wait(spill)
    spill = jnp.pad(spill, ((0, 0), (group - 3, 0), (0, 0))).reshape(tokens, model)
    grad_first = grad_first[:tokens] + spill
    first_pair = order.ring(grad_first[tokens_dev:], "c")
    g_both.next()
    first_pair = order.wait(first_pair)
    grad_inputs, grad_gain_one = norm_back_call(
        [grad_first[:tokens_dev], first_pair], flat, gains, 0, grad_middle, 0
    )
    order.must(grad_inputs)
    d_x = Scatter(order, d_z.done(ny), "y")
    a_both.next()
    o_left.next()
    o_right.next()
    d_x.next()

    o_both = Scatter(order, joined(o_left, o_right), "z", both=True)
    d_y = Scatter(order, d_x.done(nx), "x")
    g_gains = jnp.concatenate([grad_gain_one, grad_gain_two], axis=0)
    g_gains = jnp.transpose(g_gains.reshape(2, chips, 2, d_rows), (1, 2, 0, 3))
    g_gains = g_gains.reshape(lead + (2, 2 * d_rows))
    g_gains = jnp.moveaxis(behind(place, "yxz", g_gains), 3, 0)
    gains_mine = lax.dynamic_index_in_dim(g_gains, core, 0, False)
    gains_got = order.ring(lax.dynamic_index_in_dim(g_gains, 1 - core, 0, False), "c")
    part_pair = order.ring(part_other, "c")

    def whole_columns(value):
        mine, other = halves(value, place, 0)
        return mine, order.ring(other, "c")

    gains_got, part_pair = order.wait(gains_got, part_pair)
    result = middle + (part + part_pair)
    order.must(result)
    g_gains = gains_mine + gains_got
    g_gains = Scatter(order, [g_gains[i] for i in range(ny)], "y", between=F32)
    a_both.next()
    sum_c = whole_columns(g_both.done(dtype=F32))
    g_gains = Scatter(order, g_gains.done(nx, F32), "x", between=F32)
    o_both.next()
    sum_down = d_y.done(dtype=F32)
    order.must(sum_down)
    g_gains = Scatter(order, g_gains.done(nz, F32), "z", direct=True, between=F32)
    low_c, high_c = place.ordered(sum_c[0], order.wait(sum_c[1]))
    grad_gate = jnp.concatenate([low_c[:, :ffn_half], high_c[:, :ffn_half]], axis=1)
    grad_up = jnp.concatenate([low_c[:, ffn_half:], high_c[:, ffn_half:]], axis=1)
    order.must(grad_gate, grad_up)
    sum_a = whole_columns(a_both.done(dtype=F32))
    o_both.next()
    low_a, high_a = place.ordered(sum_a[0], order.wait(sum_a[1]))
    grad_input_proj = jnp.concatenate([low_a[:, :lru_half], high_a[:, :lru_half]], axis=1)
    grad_branch_proj = jnp.concatenate([low_a[:, lru_half:], high_a[:, lru_half:]], axis=1)
    order.must(grad_input_proj, grad_branch_proj)
    own = o_both.done(dtype=F32)
    g_gains = g_gains.done(dtype=F32).reshape(2, d_rows)
    own_gates = own[:, model : model + 2 * block]
    own_vec = own[:, model + 2 * block : model + 2 * block + 8].T
    return (
        result.reshape(inputs.shape),
        grad_inputs.reshape(inputs.shape),
        g_gains[0],
        grad_input_proj,
        grad_branch_proj,
        own_vec[:4],
        own_vec[4],
        own_gates[:, :block],
        own_gates[:, block:],
        own_vec[5],
        own_vec[6],
        own_vec[7],
        own[:, :model],
        g_gains[1],
        grad_gate,
        grad_up,
        sum_down,
    )


def solution(mesh):
    seq, row = mesh.shape["seq"], mesh.shape["row"]
    ny = 1 << ((seq.bit_length() - 1) // 2)
    grid = Mesh(mesh.devices.reshape(seq // ny, ny, row // 2, 2), AXES)
    tokens, line, flat, taps = P(("x", "c"), ("z", "y"), None), P(AXES, None), P(AXES), P(None, AXES)
    in_specs = (
        tokens,
        tokens,
        P(("x", "c"), ("z", "y")),
        flat,
        line,
        line,
        taps,
        flat,
        line,
        line,
        flat,
        flat,
        flat,
        line,
        flat,
        line,
        line,
        line,
    )
    out_specs = (
        tokens,
        tokens,
        flat,
        line,
        line,
        taps,
        flat,
        line,
        line,
        flat,
        flat,
        flat,
        line,
        flat,
        line,
        line,
        line,
    )
    return jax.shard_map(
        on_device, mesh=grid, in_specs=in_specs, out_specs=out_specs, check_vma=False
    )
```

```python
import functools
import math

import jax
import jax.numpy as jnp
import numpy as np
from jax import lax
from jax.experimental import pallas as pl
from jax.experimental.pallas import tpu as pltpu
from jax.sharding import Mesh, PartitionSpec as P

EPS = 1e-06
BF = jnp.bfloat16
F32 = jnp.float32
AXES = ("z", "y", "x", "c")
MIB = 1 << 20
TILE = 256
HALO = 8
GELU_C = math.sqrt(2.0 / math.pi)


class Place:
    def __init__(self):
        self.size = {axis: lax.axis_size(axis) for axis in AXES}
        self.at = {axis: lax.axis_index(axis) for axis in AXES}
        nz, ny, nx, _ = self.size.values()
        self.seq, self.row = nz * ny, nx * 2
        self.s = self.at["z"] * ny + self.at["y"]
        self.stride = {"z": ny * self.row, "y": self.row, "x": 2, "c": 1}
        self.chips = nz * ny * nx
        self.sizes = (nz, ny, nx)
        self.where = jnp.stack([self.at[axis] for axis in AXES]).astype(jnp.int32)


    def ring(self, value, axis, shift):
        pairs = []
        for i in range(self.seq * self.row):
            at = (i // self.stride[axis]) % self.size[axis]
            to = (at + shift) % self.size[axis]
            pairs.append((i, i + (to - at) * self.stride[axis]))
        return lax.ppermute(value, AXES, pairs)

    def along(self, value, distance):
        pairs = []
        for s in range(self.seq):
            if 0 <= s + distance < self.seq:
                for r in range(self.row):
                    pairs.append((s * self.row + r, (s + distance) * self.row + r))
        return lax.ppermute(value, AXES, pairs)

    def ordered(self, mine, other):
        high = self.at["c"] != 0
        return jnp.where(high, other, mine), jnp.where(high, mine, other)


class Order:
    def __init__(self, place):
        self.place = place
        self.last = ()
        self.sent = ()

    def tie(self, value):
        if not self.last:
            return value
        return lax.optimization_barrier((value,) + self.last)[0]

    def must(self, *values):
        self.sent += values

    def ring(self, value, axis, shift=1):
        value = self.tie(value)
        self.sent += (value,)
        return self.place.ring(value, axis, shift)

    def along(self, value, distance):
        value = self.tie(value)
        self.sent += (value,)
        return self.place.along(value, distance)

    def wait(self, *values):
        n = len(values)
        held = values + self.last + self.sent
        if len(held) > n:
            values = lax.optimization_barrier(held)[:n]
        self.last = tuple(values)
        self.sent = ()
        return values[0] if n == 1 else values


class Gather:
    def __init__(self, order, value, axis, dim, direct=False, both=False):
        self.order, self.axis, self.dim = order, axis, dim
        self.n = order.place.size[axis]
        self.pieces = [value]
        self.direct = direct
        self.both = both and self.n == 4
        if self.both:
            self.flying = [order.ring(value, axis, 1), order.ring(value, axis, 3)]
            return
        shifts = range(1, self.n) if direct else range(1, min(2, self.n))
        self.flying = [order.ring(value, axis, k) for k in shifts]

    def next(self):
        if self.direct:
            if self.flying:
                got = self.order.wait(*self.flying)
                self.pieces += [got] if len(self.flying) == 1 else list(got)
            self.flying = []
            return
        if self.both:
            if len(self.flying) == 2:
                one, three = self.order.wait(*self.flying)
                self.pieces += [one, None, three]
                self.flying = [self.order.ring(one, self.axis)]
            elif self.flying:
                self.pieces[2] = self.order.wait(self.flying.pop())
            return
        got = self.order.wait(self.flying.pop())
        self.pieces.append(got)
        if len(self.pieces) < self.n:
            self.flying = [self.order.ring(got, self.axis)]

    def arrived(self):
        while len(self.pieces) < self.n or (self.both and self.flying):
            self.next()
        return self.pieces

    def done(self):
        return self.whole(self.arrived())

    def whole(self, pieces):
        at = self.order.place.at[self.axis]
        if self.n == 2:
            high = at != 0
            mine, other = pieces
            parts = [jnp.where(high, other, mine), jnp.where(high, mine, other)]
            return jnp.concatenate(parts, axis=self.dim)
        parts = [
            lax.select_n(lax.rem(at - j + self.n, self.n), *pieces) for j in range(self.n)
        ]
        return jnp.concatenate(parts, axis=self.dim)

    def weight(self, rows):
        if rows % 16 == 0:
            return self.arrived()
        whole = self.done()[..., :rows, :]
        return [whole.reshape(-1, whole.shape[-1])]


class Scatter:
    def __init__(self, order, blocks, axis, direct=False, between=BF, both=False):
        self.order, self.axis, self.blocks = order, axis, list(blocks)
        self.n = order.place.size[axis]
        self.both = both and self.n == 4
        self.direct, self.between = direct, between
        self.hop = 0
        self.held = False
        if self.both:
            self.flying = [order.ring(self.blocks[1], axis, 3), order.ring(self.blocks[2], axis, 1)]
        elif direct:
            self.flying = [
                order.ring(self.blocks[i], axis, self.n - 1 - i) for i in range(self.n - 1)
            ]
        elif self.n > 1:
            self.flying = order.ring(self.blocks[0], axis)

    def next(self):
        if self.both:
            if self.hop == 0:
                far, near = self.order.wait(*self.flying)
                total = far.astype(F32) + self.blocks[0].astype(F32)
                self.got = [near]
                self.flying = self.order.ring(total.astype(self.between), self.axis, 3)
                self.hop = 1
            elif self.hop == 1:
                self.got.append(self.order.wait(self.flying))
                self.hop = self.n - 1
            return
        if self.direct:
            if self.n > 1:
                got = self.order.wait(*self.flying)
                self.got = [got] if self.n == 2 else list(got)
            self.hop = self.n - 1
            return
        if not self.held:
            self.take()
        self.held = False
        if self.hop < self.n - 1:
            total = self.got[0].astype(F32) + self.blocks[self.hop].astype(F32)
            self.flying = self.order.ring(total.astype(self.between), self.axis)

    def take(self):
        self.got = [self.order.wait(self.flying)]
        self.hop += 1
        self.held = True

    def done(self, parts=0, dtype=BF):
        if self.held:
            self.next()
        while self.hop < self.n - 1:
            self.next()
        terms = [self.blocks[-1]] + (self.got if self.n > 1 else [])

        def total(pick):
            values = [pick(t).astype(F32) for t in terms]
            return functools.reduce(jnp.add, values).astype(dtype)

        if not parts:
            return total(lambda t: t)
        return [total(lambda t, i=i: t[i]) for i in range(parts)]


def behind(place, order_of_axes, value):
    for dim, axis in enumerate(("z", "y", "x")):
        n, at = place.size[axis], place.at[axis]
        picks = [
            lax.dynamic_index_in_dim(value, lax.rem(at - i - 1 + 2 * n, n), dim)
            for i in range(n)
        ]
        value = jnp.concatenate(picks, axis=dim)
    dims = ["zyx".index(axis) for axis in order_of_axes]
    return jnp.transpose(value, tuple(dims) + tuple(range(3, value.ndim)))


def sources(place, order_of_axes, rows):
    lead = tuple(place.size[a] for a in "zyx")
    at = jnp.arange(math.prod(lead) * rows, dtype=jnp.int32).reshape(lead + (rows,))
    return behind(place, order_of_axes, at).reshape(-1)


def compose(earlier, later):
    return jnp.concatenate(
        [earlier[:4] * later[:4], later[:4] * earlier[4:] + later[4:]], axis=0
    )


class Carry:
    def __init__(self, order, end_map, sign, most=3):
        self.order, self.sign, self.most = order, sign, most
        self.n = order.place.seq
        self.unit = jnp.concatenate(
            [jnp.ones_like(end_map[:4]), jnp.zeros_like(end_map[4:])], axis=0
        )
        self.total = None
        self.reach = 0
        self.send(end_map, 1)

    def send(self, value, width):
        self.shifts = []
        distance = max(self.reach, 1)
        while distance < self.n and len(self.shifts) < self.most:
            self.shifts.append(distance)
            distance += width
        self.width = width
        self.flying = [self.order.along(value, self.sign * d) for d in self.shifts]

    def next(self):
        got = self.order.wait(*self.flying)
        got = [got] if len(self.flying) == 1 else list(got)
        s, n = self.order.place.s, self.n
        for value, d in zip(got, self.shifts):
            inside = (s >= d) if self.sign > 0 else (s < n - d)
            part = jnp.where(inside, value, self.unit)
            self.total = part if self.total is None else compose(part, self.total)
        self.reach += self.width * len(self.shifts)
        if self.reach < self.n - 1:
            self.send(self.total, self.reach)
            return True
        return False

    def done(self):
        while self.next():
            pass
        return self.total[4:]


def dot(a, b):
    return jnp.dot(a, b, preferred_element_type=F32)


def dot_nt(a, b):
    return lax.dot_general(a, b, (((1,), (1,)), ((), ())), preferred_element_type=F32)


def dot_tn(a, b):
    return lax.dot_general(a, b, (((0,), (0,)), ((), ())), preferred_element_type=F32)


def moved(value, distance, fill):
    n = value.shape[0]
    size = abs(distance)
    edge = jnp.full((size,) + value.shape[1:], fill, value.dtype)
    if size % 8 == 0:
        if distance > 0:
            return jnp.concatenate([edge, value[: n - size]], axis=0)
        return jnp.concatenate([value[size:], edge], axis=0)
    at = lax.broadcasted_iota(jnp.int32, value.shape, 0)
    turned = pltpu.roll(value, distance % n, 0)
    inside = at >= size if distance > 0 else at < n - size
    return jnp.where(inside, turned, fill)


def scan_tile(decay, drive, sign):
    n = decay.shape[0]
    distance = 1
    while distance < n:
        drive = decay * moved(drive, sign * distance, 0.0) + drive
        decay = decay * moved(decay, sign * distance, 1.0)
        distance *= 2
    return decay, drive


def one_less_exp(u):
    term = jnp.full_like(u, 1.0 / 3628800.0)
    for k in (362880, 40320, 5040, 720, 120, 24, 6, 2):
        term = 1.0 / k - u * term
    small = u * (1.0 - u * term)
    return jnp.where(u < 0.8, small, 1.0 - jnp.exp(-u))


def log2(n):
    return n.bit_length() - 1


def source_rows(order, sizes, at_ref, rows, first, count):
    spot = {"z": at_ref[0], "y": at_ref[1], "x": at_ref[2]}
    size = dict(zip("zyx", sizes))
    line = first + lax.broadcasted_iota(jnp.int32, (count, 1), 0)
    inside = line & (rows - 1)
    line = line >> log2(rows)
    where = {}
    for axis in reversed(order):
        n = size[axis]
        where[axis] = (spot[axis] + (n - 1) - (line & (n - 1))) & (n - 1)
        line = line >> log2(n)
    chip = (where["z"] * size["y"] + where["y"]) * size["x"] + where["x"]
    return chip * rows + inside


def turn_rows(order, sizes, at_ref, value, rows, out_ref):
    total = value.shape[1]
    step = min(total, 256)
    for first in range(0, total, step):
        source = source_rows(order, sizes, at_ref, rows, first, step)
        lane = lax.broadcasted_iota(jnp.int32, (step, total), 1)
        pick = jnp.where(source == lane, 1.0, 0.0).astype(BF)
        out_ref[first : first + step] = dot_nt(pick, value).astype(BF)


def gelu_parts(value):
    square = value * value
    t = jnp.tanh(GELU_C * value * (1.0 + 0.044715 * square))
    half = 0.5 * (1.0 + t)
    slope = half + 0.5 * value * (1.0 - t * t) * GELU_C * (1.0 + 3.0 * 0.044715 * square)
    return value * half, slope


def full(shape):
    return pl.BlockSpec(shape, lambda j: (0,) * len(shape))


def columns(rows, width=TILE):
    return pl.BlockSpec((rows, width), lambda j: (0, j))


def lines(rows, width):
    return pl.BlockSpec((rows, width), lambda j: (j, 0))


def in_hbm(shape, dtype):
    return pltpu.HBM(shape, dtype)


def piece_specs(pieces, rows, tile=TILE):
    if len(pieces) == 1:
        return [columns(pieces[0].shape[0], tile)]
    block = pieces[0].shape[:3] + (rows, tile)
    return [pl.BlockSpec(block, lambda j: (0, 0, 0, 0, j)) for _ in pieces]


def piece_scratch(place, pieces, rows, tile=TILE):
    if len(pieces) == 1:
        return pltpu.VMEM((16, 128), BF)
    return pltpu.VMEM(place.sizes + (rows, tile), BF)


def from_pieces(at, dim, refs, out_ref):
    n = len(refs)
    if n == 1:
        return refs[0][...]
    for k, ref in enumerate(refs):
        where = pl.ds((at - k + n) & (n - 1), 1)
        out_ref[(slice(None),) * dim + (where,)] = ref[...]
    whole = out_ref[...]
    return whole.reshape(-1, whole.shape[-1])


def shape_of(shape, dtype):
    return jax.ShapeDtypeStruct(shape, dtype)


def params(limit):
    return pltpu.CompilerParams(vmem_limit_bytes=limit * MIB)


LIGHT = pl.CostEstimate(flops=1, bytes_accessed=1, transcendentals=0)


def turn_kernel(sizes, rows, at_ref, first_ref, left_ref, right_ref):
    turn_rows("xyz", sizes, at_ref, first_ref[...], rows, left_ref)
    turn_rows("yxz", sizes, at_ref, first_ref[...], rows, right_ref)


def turn_call(place, first, rows):
    length, model = first.shape
    whole = pl.BlockSpec(memory_space=pltpu.VMEM)
    return pl.pallas_call(
        functools.partial(turn_kernel, place.sizes, rows),
        in_specs=[pl.BlockSpec(memory_space=pltpu.SMEM), whole],
        out_specs=[whole] * 2,
        out_shape=[shape_of((model, length), BF)] * 2,
        compiler_params=params(24),
        cost_estimate=LIGHT,
        name="turn",
    )(place.where, first)


def small_kernel(d_rows, r_rows, at_ref, small_ref, qd_ref, md_ref, qr_ref, mr_ref, gain_ref, vec_ref):
    def spread(row, q_ref, m_ref):
        value = dot(small_ref[:, row, :], q_ref[...])
        return jnp.sum(value * m_ref[...], axis=0, keepdims=True)

    for k in range(2):
        gain_ref[k : k + 1] = spread(k, qd_ref, md_ref)
    half = vec_ref.shape[1]
    for k in range(8):
        value = spread(2 + k, qr_ref, mr_ref)
        value = jnp.where(at_ref[3] == 0, value[:, :half], value[:, half:])
        if k == 7:
            soft = jnp.maximum(value, 0.0) + jnp.log1p(jnp.exp(-jnp.abs(value)))
            vec_ref[8:9] = -8.0 * jax.nn.sigmoid(value)
            value = 8.0 * soft
        vec_ref[k : k + 1] = value


def small_call(place, small, d_rows, r_rows):
    devices, _, span = small.shape
    operands = []
    for rows in (d_rows, r_rows):
        lane = np.arange(devices * rows)
        operands.append(jnp.asarray(lane[None] % rows == np.arange(span)[:, None], BF))
        operands.append(jnp.asarray(lane[None] // rows == np.arange(devices)[:, None], F32))
    whole = pl.BlockSpec(memory_space=pltpu.VMEM)
    return pl.pallas_call(
        functools.partial(small_kernel, d_rows, r_rows),
        in_specs=[pl.BlockSpec(memory_space=pltpu.SMEM)] + [whole] * 5,
        out_specs=[whole] * 2,
        out_shape=[shape_of((2, devices * d_rows), F32), shape_of((16, devices * r_rows // 2), F32)],
        compiler_params=params(24),
        cost_estimate=LIGHT,
        name="small_weights",
    )(place.where, small, *operands)


def norm_kernel(n_terms, row, *refs):
    terms, gain_ref, outs = refs[:n_terms], refs[n_terms], refs[n_terms + 1 :]
    value = functools.reduce(jnp.add, [t[...] for t in terms])
    scale = lax.rsqrt(jnp.mean(value * value, axis=-1, keepdims=True) + EPS)
    outs[0][...] = (value * scale * gain_ref[row : row + 1]).astype(BF)
    if n_terms > 1:
        outs[1][...] = value


def norm_call(terms, gains, row):
    tokens, model = terms[0].shape
    step = tokens // 4
    block = pl.BlockSpec((step, model), lambda j: (j, 0))
    shapes = [in_hbm((tokens, model), BF), shape_of((tokens, model), F32)]
    shapes = shapes[: 1 if len(terms) == 1 else 2]
    return pl.pallas_call(
        functools.partial(norm_kernel, len(terms), row),
        grid=(4,),
        in_specs=[block] * len(terms) + [full(gains.shape)],
        out_specs=[block] * len(shapes),
        out_shape=shapes,
        compiler_params=params(16),
        cost_estimate=LIGHT,
        name="norm",
    )(*terms, gains)


def norm_back_kernel(n_terms, row, low, *refs):
    terms = refs[:n_terms]
    value_ref, gain_ref, add_ref, out_ref = refs[n_terms : n_terms + 4]
    gain_out = refs[-1]
    grad = functools.reduce(jnp.add, [t[...] for t in terms])
    value = value_ref[...]
    scale = lax.rsqrt(jnp.mean(value * value, axis=-1, keepdims=True) + EPS)
    unit = value * scale
    inner = grad * gain_ref[row : row + 1]
    total = add_ref[...] + scale * (inner - unit * jnp.mean(inner * unit, axis=-1, keepdims=True))
    out_ref[...] = total
    if low:
        refs[n_terms + 4][...] = total.astype(BF)
    part = jnp.sum(grad * unit, axis=0, keepdims=True)

    @pl.when(pl.program_id(0) == 0)
    def _():
        gain_out[...] = part

    @pl.when(pl.program_id(0) > 0)
    def _():
        gain_out[...] += part


def norm_back_call(terms, value, gains, row, add, low):
    tokens, model = value.shape
    step = tokens // 4
    block = pl.BlockSpec((step, model), lambda j: (j, 0))
    shapes = [shape_of((tokens, model), F32)] + [in_hbm((tokens, model), BF)] * low
    return pl.pallas_call(
        functools.partial(norm_back_kernel, len(terms), row, low),
        grid=(4,),
        in_specs=[block] * len(terms) + [block, full(gains.shape), block],
        out_specs=[block] * len(shapes) + [full((1, model))],
        out_shape=shapes + [shape_of((1, model), F32)],
        compiler_params=params(16),
        cost_estimate=LIGHT,
        name="norm_back",
    )(*terms, value, gains, add)


def pack_kernel(at_ref, go_ref, gr_ref, gi_ref, gvec_ref, vec_ref, mine_ref, other_ref):
    pairs, rows, _ = mine_ref.shape
    model, block = go_ref.shape[1], gr_ref.shape[1]
    line = lax.broadcasted_iota(jnp.int32, gvec_ref.shape, 0)
    gvec = jnp.where(line == 7, gvec_ref[...] * vec_ref[8:9], gvec_ref[...]).astype(BF)
    slot = lax.broadcasted_iota(jnp.int32, (8, block), 0)
    lane = lax.broadcasted_iota(jnp.int32, (8, block), 1)
    turned = dot_tn(gvec, jnp.where(slot == lane, 1.0, 0.0).astype(BF)).astype(BF)
    gr, gi = gr_ref[...].astype(BF), gi_ref[...].astype(BF)
    for k in range(2):

        @pl.when(at_ref[3] == k)
        def _():
            for q in range(pairs):
                for ref, which in ((mine_ref, k), (other_ref, 1 - k)):
                    span = slice((2 * q + which) * rows, (2 * q + which + 1) * rows)
                    ref[q, :, 0:model] = go_ref[span]
                    ref[q, :, model : model + block] = gr[span]
                    ref[q, :, model + block : model + 2 * block] = gi[span]
                    ref[q, :, model + 2 * block :] = turned[span]


def pack_call(place, g_out, g_gate_r, g_gate_i, g_vec, vec, rows):
    width, model = g_out.shape
    block = g_gate_r.shape[1]
    shape = (width // (2 * rows), rows, model + 3 * block)
    whole = pl.BlockSpec(memory_space=pltpu.VMEM)
    return pl.pallas_call(
        pack_kernel,
        in_specs=[pl.BlockSpec(memory_space=pltpu.SMEM)] + [whole] * 5,
        out_specs=[whole] * 2,
        out_shape=[shape_of(shape, BF), shape_of(shape, BF)],
        compiler_params=params(24),
        cost_estimate=LIGHT,
        name="pack",
    )(place.where, g_out, g_gate_r, g_gate_i, g_vec, vec)


def forward_kernel(
    n_rows,
    group,
    block,
    n_in,
    n_branch,
    at_ref,
    mine_ref,
    other_ref,
    halo_ref,
    *refs,
):
    w_refs, wb_refs, refs = refs[:n_in], refs[n_in : n_in + n_branch], refs[n_in + n_branch :]
    vec_ref, mask_ref, gr_ref, gi_ref, first_ref, bpre_ref, mixer_ref, conv_ref = refs[:8]
    rpre_ref, ipre_ref, through_ref, local_ref, ends_ref, w_ref, wb_ref = refs[8:15]
    ext_ref, in_ref, branch_ref = refs[15:]
    half = mine_ref.shape[0]
    w_ref[...] = from_pieces(at_ref[2], 2, w_refs, in_ref)
    wb_ref[...] = from_pieces(at_ref[1], 1, wb_refs, branch_ref)

    @pl.when(pl.program_id(0) == 0)
    def _():
        first_ref[0:half] = mine_ref[...]
        first_ref[half : 2 * half] = other_ref[...]
        first_ref[2 * half :] = halo_ref[...]

    mixer = dot(first_ref[...], w_ref[...]).astype(BF)
    bpre_ref[...] = dot(first_ref[0 : 2 * half], wb_ref[...])
    mixer_ref[...] = mixer
    wide = mixer.astype(F32)
    tokens = n_rows * group
    for r in range(n_rows):
        ext_ref[r, 0:HALO] = wide[tokens + HALO * r : tokens + HALO * (r + 1)]
        ext_ref[r, HALO : HALO + group] = wide[r * group : (r + 1) * group]
    for r in range(n_rows):
        span = slice(r * group, (r + 1) * group)
        conv = vec_ref[4:5] + vec_ref[0:1] * ext_ref[r, HALO : HALO + group]
        for k in range(1, 4):
            conv += (
                vec_ref[k : k + 1]
                * ext_ref[r, HALO - k : HALO - k + group]
                * mask_ref[span, k : k + 1]
            )
        conv_ref[span] = conv.astype(BF)
    for h in range(w_ref.shape[1] // block):
        cols = slice(h * block, (h + 1) * block)
        low = conv_ref[:, cols]
        rpre_ref[:, cols] = dot(low, gr_ref[cols]) + vec_ref[5:6, cols]
        ipre_ref[:, cols] = dot(low, gi_ref[cols]) + vec_ref[6:7, cols]
        for r in range(n_rows):
            span = slice(r * group, (r + 1) * group)
            recur = jax.nn.sigmoid(rpre_ref[span, cols])
            admit = jax.nn.sigmoid(ipre_ref[span, cols])
            rate = vec_ref[7:8, cols] * recur
            reset = mask_ref[span, 0:1]
            decay = jnp.exp(-rate) * (1.0 - reset)
            scale = jnp.where(reset > 0.5, 1.0, jnp.sqrt(one_less_exp(2.0 * rate)))
            drive = scale * admit * conv_ref[span, cols].astype(F32)
            decay, drive = scan_tile(decay, drive, 1)
            through_ref[span, cols] = decay
            local_ref[span, cols] = drive
            ends_ref[r : r + 1, cols] = decay[group - 1 : group]
            ends_ref[n_rows + r : n_rows + r + 1, cols] = drive[group - 1 : group]


def forward_call(place, mine, other, halo, w_in, w_branch, vec, masks, gate_r, gate_i, n_rows, group, chip_d):
    model = mine.shape[1]
    length = 2 * mine.shape[0] + halo.shape[0]
    width, block = w_in[0].shape[-1], gate_r.shape[1]
    tokens = n_rows * group
    tile = TILE
    return pl.pallas_call(
        functools.partial(
            forward_kernel, n_rows, group, block, len(w_in), len(w_branch)
        ),
        grid=(width // tile,),
        in_specs=[
            pl.BlockSpec(memory_space=pltpu.SMEM),
            full(mine.shape),
            full(mine.shape),
            full(halo.shape),
            *piece_specs(w_in, chip_d),
            *piece_specs(w_branch, chip_d),
            columns(16),
            full(masks.shape),
            lines(tile, block),
            lines(tile, block),
        ],
        out_specs=[full((length, model)), columns(tokens), columns(length)]
        + [columns(tokens)] * 5
        + [columns(2 * n_rows), columns(model), columns(model)],
        out_shape=[
            in_hbm((length, model), BF),
            in_hbm((tokens, width), F32),
            in_hbm((length, width), BF),
            in_hbm((tokens, width), BF),
            in_hbm((tokens, width), F32),
            in_hbm((tokens, width), F32),
            in_hbm((tokens, width), F32),
            in_hbm((tokens, width), F32),
            in_hbm((2 * n_rows, width), F32),
            in_hbm((model, width), BF),
            in_hbm((model, width), BF),
        ],
        scratch_shapes=[
            pltpu.VMEM((n_rows, HALO + group, tile), F32),
            piece_scratch(place, w_in, chip_d),
            piece_scratch(place, w_branch, chip_d),
        ],
        compiler_params=params(24),
        cost_estimate=LIGHT,
        name="recurrence_forward",
    )(place.where, mine, other, halo, *w_in, *w_branch, vec, masks, gate_r, gate_i)


def mix_kernel(
    n_rows, group, local_ref, through_ref, enter_ref, bpre_ref, w_ref, state_ref, mixed_ref, part_ref, part_other_ref
):
    for r in range(n_rows):
        span = slice(r * group, (r + 1) * group)
        state = local_ref[span] + through_ref[span] * enter_ref[r : r + 1]
        state_ref[span] = state
        branch, _ = gelu_parts(bpre_ref[span])
        mixed_ref[span] = (state * branch).astype(BF)
    part = dot(mixed_ref[...], w_ref[...])
    half = part_ref.shape[0]

    @pl.when(pl.program_id(0) == 0)
    def _():
        part_ref[...] = part[:half]
        part_other_ref[...] = part[half:]

    @pl.when(pl.program_id(0) > 0)
    def _():
        part_ref[...] += part[:half]
        part_other_ref[...] += part[half:]


def mix_call(local, through, enter, branch_pre, w_out, n_rows, group):
    tokens, width = local.shape
    model = w_out.shape[1]
    return pl.pallas_call(
        functools.partial(mix_kernel, n_rows, group),
        grid=(width // TILE,),
        in_specs=[
            columns(tokens),
            columns(tokens),
            columns(n_rows),
            columns(tokens),
            lines(TILE, model),
        ],
        out_specs=[columns(tokens), columns(tokens)] + [full((tokens // 2, model))] * 2,
        out_shape=[
            in_hbm((tokens, width), F32),
            in_hbm((tokens, width), BF),
            shape_of((tokens // 2, model), F32),
            in_hbm((tokens // 2, model), F32),
        ],
        compiler_params=params(58),
        cost_estimate=LIGHT,
        name="mix",
    )(local, through, enter, branch_pre, w_out)


def ffn_kernel(
    sizes,
    rows,
    n_gate,
    n_up,
    at_ref,
    mine_ref,
    other_ref,
    low_mine_ref,
    low_other_ref,
    *refs,
):
    wg_refs, wu_refs, refs = refs[:n_gate], refs[n_gate : n_gate + n_up], refs[n_gate + n_up :]
    wd_ref, gg_send_ref, gg_ref, gu_send_ref, gu_ref, gd_ref, gd_other_ref = refs[:7]
    part_ref, part_other_ref, back_ref, back_other_ref = refs[7:11]
    second_ref, low_ref, left_ref, right_ref, gate_ref, up_ref, down_ref = refs[11:]
    step = pl.program_id(0)
    half = mine_ref.shape[0]

    @pl.when(step == 0)
    def _():
        second_ref[0:half] = mine_ref[...]
        second_ref[half:] = other_ref[...]
        low_ref[0:half] = low_mine_ref[...]
        low_ref[half:] = low_other_ref[...]
        turn_rows("xyz", sizes, at_ref, second_ref[...], rows, left_ref)
        turn_rows("yxz", sizes, at_ref, second_ref[...], rows, right_ref)

    second, low = second_ref[...], low_ref[...]
    w_gate = from_pieces(at_ref[2], 2, wg_refs, gate_ref)
    w_up = from_pieces(at_ref[1], 1, wu_refs, up_ref)
    gate = dot(second, w_gate)
    up = dot(second, w_up)
    grad = dot_nt(low, wd_ref[...])
    active, slope = gelu_parts(gate)
    hidden = (active * up).astype(BF)
    gate_low = (grad * up * slope).astype(BF)
    up_low = (grad * active).astype(BF)
    sent = gg_send_ref.shape[0]
    gg = dot(left_ref[...], gate_low).astype(BF)
    gg_send_ref[...] = gg[:sent]
    gg_ref[...] = gg[sent:]
    sent = gu_send_ref.shape[0]
    gu = dot(right_ref[...], up_low).astype(BF)
    gu_send_ref[...] = gu[:sent]
    gu_ref[...] = gu[sent:]
    width = hidden.shape[1]
    down_ref[pl.ds(step * width, width)] = dot_tn(hidden, low).astype(BF)
    part = dot(hidden, wd_ref[...])
    back = dot_nt(gate_low, w_gate) + dot_nt(up_low, w_up)

    @pl.when(step == 0)
    def _():
        part_ref[...] = part[:half]
        part_other_ref[...] = part[half:]
        back_ref[...] = back[:half]
        back_other_ref[...] = back[half:]

    @pl.when(step > 0)
    def _():
        part_ref[...] += part[:half]
        part_other_ref[...] += part[half:]
        back_ref[...] += back[:half]
        back_other_ref[...] += back[half:]

    pairs, lines_down, _ = gd_ref.shape
    for k in range(2):

        @pl.when((step == pl.num_programs(0) - 1) & (at_ref[3] == k))
        def _():
            for q in range(pairs):
                at = 2 * q * lines_down
                near, far = at + k * lines_down, at + (1 - k) * lines_down
                gd_ref[q] = down_ref[near : near + lines_down]
                gd_other_ref[q] = down_ref[far : far + lines_down]


def ffn_call(place, mine, other, low_mine, low_other, w_gate, w_up, w_down, chip_d, f_rows):
    tokens, model = 2 * mine.shape[0], mine.shape[1]
    width = w_gate[0].shape[-1]
    tile = 2 * TILE
    sent_l, sent_r = model // place.size["x"], model // place.size["y"]
    down = (width // (2 * f_rows), f_rows, model)
    rows = [sent_l, model - sent_l, sent_r, model - sent_r]
    return pl.pallas_call(
        functools.partial(ffn_kernel, place.sizes, chip_d, len(w_gate), len(w_up)),
        grid=(width // tile,),
        in_specs=[
            pl.BlockSpec(memory_space=pltpu.SMEM),
            full((tokens // 2, model)),
            full((tokens // 2, model)),
            full((tokens // 2, model)),
            full((tokens // 2, model)),
            *piece_specs(w_gate, chip_d, tile),
            *piece_specs(w_up, chip_d, tile),
            lines(tile, model),
        ],
        out_specs=[columns(n, tile) for n in rows]
        + [full(down)] * 2
        + [full((tokens // 2, model))] * 4,
        out_shape=[in_hbm((n, width), BF) for n in rows]
        + [shape_of(down, BF), in_hbm(down, BF)]
        + [shape_of((tokens // 2, model), F32), in_hbm((tokens // 2, model), F32)] * 2,
        scratch_shapes=[
            pltpu.VMEM((tokens, model), BF),
            pltpu.VMEM((tokens, model), BF),
            pltpu.VMEM((model, tokens), BF),
            pltpu.VMEM((model, tokens), BF),
            piece_scratch(place, w_gate, chip_d, tile),
            piece_scratch(place, w_up, chip_d, tile),
            pltpu.VMEM((width, model), BF),
        ],
        compiler_params=params(60),
        cost_estimate=LIGHT,
        name="feed_forward",
    )(place.where, mine, other, low_mine, low_other, *w_gate, *w_up, w_down)


def split_kernel(cuts, at_ref, whole_ref, *outs):
    for out, (low, high) in zip(outs, cuts):
        out[...] = whole_ref[:, low:high]


def split_call(place, whole, cuts):
    count, rows, width = whole.shape
    steps = 4
    step = count // (2 * steps)
    if any(n % 16 for cut in cuts for n in cut):
        half = lax.dynamic_slice_in_dim(whole, place.at["c"] * (count // 2), count // 2, 0)
        return [half[:, low:high].reshape(-1, width) for low, high in cuts]
    outs = pl.pallas_call(
        functools.partial(split_kernel, cuts),
        grid_spec=pltpu.PrefetchScalarGridSpec(
            num_scalar_prefetch=1,
            grid=(steps,),
            in_specs=[pl.BlockSpec((step, rows, width), lambda j, at: (at[3] * steps + j, 0, 0))],
            out_specs=[
                pl.BlockSpec((step, high - low, width), lambda j, at: (j, 0, 0))
                for low, high in cuts
            ],
        ),
        out_shape=[in_hbm((count // 2, high - low, width), BF) for low, high in cuts],
        compiler_params=params(58),
        cost_estimate=LIGHT,
        name="split",
    )(place.where, whole)
    return [out.reshape(-1, width) for out in outs]


def regroup_kernel(sizes, order_of, cuts, at_ref, mine_ref, got_ref, *outs):
    nz, ny, nx = sizes
    size = {"z": nz, "y": ny, "x": nx}
    spot = {"z": at_ref[0], "y": at_ref[1], "x": at_ref[2]}
    half = mine_ref.shape[0]
    for index, order in enumerate(order_of):
        send_ref, rest_ref = outs[2 * index], outs[2 * index + 1]
        span = slice(*cuts[index])
        for i0 in range(size[order[0]]):
            for i1 in range(size[order[1]]):
                for i2 in range(size[order[2]]):
                    place = {}
                    for axis, i in zip(order, (i0, i1, i2)):
                        n = size[axis]
                        place[axis] = lax.rem(spot[axis] + (n - 1 - i), n)
                    chip = (place["z"] * ny + place["y"]) * nx + place["x"]
                    here = lax.rem(chip, half)
                    own = lax.div(chip, half) == at_ref[3]
                    value = jnp.where(own, mine_ref[here][:, span], got_ref[here][:, span])
                    if i0 == 0:
                        send_ref[i1, i2] = value
                    else:
                        rest_ref[i0 - 1, i1, i2] = value


def regroup_call(place, mine, got, order_of, cuts):
    sizes = tuple(place.size[a] for a in "zyx")
    rows = mine.shape[1]
    shapes = []
    for order, (low, high) in zip(order_of, cuts):
        n0, n1, n2 = (place.size[a] for a in order)
        shapes.append((n1, n2, rows, high - low))
        shapes.append((n0 - 1, n1, n2, rows, high - low))
    whole = pl.BlockSpec(memory_space=pltpu.VMEM)
    outs = pl.pallas_call(
        functools.partial(regroup_kernel, sizes, order_of, cuts),
        in_specs=[pl.BlockSpec(memory_space=pltpu.SMEM), whole, whole],
        out_specs=[whole] * len(shapes),
        out_shape=[shape_of(shape, BF) for shape in shapes],
        compiler_params=params(24),
        cost_estimate=LIGHT,
        name="regroup",
    )(place.where, mine, got)
    return [
        [outs[2 * i]] + [outs[2 * i + 1][j] for j in range(shapes[2 * i + 1][0])]
        for i in range(len(order_of))
    ]


def decay_of(rpre, vec7, reset):
    recur = jax.nn.sigmoid(rpre)
    rate = vec7 * recur
    return recur, rate, jnp.exp(-rate) * (1.0 - reset)


def back_kernel(
    n_rows,
    group,
    mine_ref,
    other_ref,
    w_ref,
    bpre_ref,
    state_ref,
    rpre_ref,
    mixed_ref,
    vec_ref,
    mask_ref,
    right_ref,
    go_ref,
    gb_send_ref,
    gb_ref,
    gbl_ref,
    reach_ref,
    local_ref,
    ends_ref,
    low_ref,
    grad_ref,
):
    @pl.when(pl.program_id(0) == 0)
    def _():
        half = mine_ref.shape[0]
        low_ref[0:half] = mine_ref[...]
        low_ref[half:] = other_ref[...]

    low = low_ref[...]
    grad_ref[...] = dot_nt(low, w_ref[...])
    go_ref[...] = dot_tn(mixed_ref[...], low).astype(BF)
    half = w_ref.shape[0] // 2
    for h in range(2):
        cols = slice(h * half, (h + 1) * half)
        for r in range(n_rows):
            span = slice(r * group, (r + 1) * group)
            branch, slope = gelu_parts(bpre_ref[span, cols])
            grad = grad_ref[span, cols]
            gbl_ref[span, cols] = (grad * state_ref[span, cols] * slope).astype(BF)
            _, _, decay = decay_of(rpre_ref[span, cols], vec_ref[7:8, cols], mask_ref[span, 0:1])
            ahead = moved(decay, -1, 1.0)
            reach, local = scan_tile(ahead, grad * branch, -1)
            reach_ref[span, cols] = reach
            local_ref[span, cols] = local
            ends_ref[r : r + 1, cols] = decay[0:1] * reach[0:1]
            ends_ref[n_rows + r : n_rows + r + 1, cols] = decay[0:1] * local[0:1]
    sent = gb_send_ref.shape[0]
    gb = dot(right_ref[:, 0 : gbl_ref.shape[0]], gbl_ref[...]).astype(BF)
    gb_send_ref[...] = gb[:sent]
    gb_ref[...] = gb[sent:]


def back_call(place, mine, other, w_out, branch_pre, state, rpre, mixed, vec, masks, right, n_rows, group):
    model, length = right.shape
    tokens = state.shape[0]
    sent = model // place.size["y"]
    width = w_out.shape[0]
    return pl.pallas_call(
        functools.partial(back_kernel, n_rows, group),
        grid=(width // TILE,),
        in_specs=[
            full((tokens // 2, model)),
            full((tokens // 2, model)),
            lines(TILE, model),
            columns(tokens),
            columns(tokens),
            columns(tokens),
            columns(tokens),
            columns(16),
            full(masks.shape),
            full((model, length)),
        ],
        out_specs=[
            lines(TILE, model),
            columns(sent),
            columns(model - sent),
            columns(tokens),
            columns(tokens),
            columns(tokens),
            columns(2 * n_rows),
        ],
        out_shape=[
            shape_of((width, model), BF),
            in_hbm((sent, width), BF),
            in_hbm((model - sent, width), BF),
            shape_of((tokens, width), BF),
            shape_of((tokens, width), F32),
            shape_of((tokens, width), F32),
            shape_of((2 * n_rows, width), F32),
        ],
        scratch_shapes=[pltpu.VMEM((tokens, model), BF), pltpu.VMEM((tokens, TILE), F32)],
        compiler_params=params(32),
        cost_estimate=LIGHT,
        name="recurrence_back",
    )(mine, other, w_out, branch_pre, state, rpre, mixed, vec, masks, right)


def gates_kernel(
    n_rows,
    group,
    block,
    reach_ref,
    local_ref,
    leave_ref,
    state_ref,
    enter_ref,
    rpre_ref,
    ipre_ref,
    conv_ref,
    mixer_ref,
    vec_ref,
    mask_ref,
    gr_ref,
    gi_ref,
    left_ref,
    win_ref,
    wbr_ref,
    gbl_ref,
    gin_send_ref,
    gin_ref,
    ggr_ref,
    ggi_ref,
    gvec_ref,
    gfirst_ref,
    rlow_ref,
    ilow_ref,
    gconv_ref,
    ext_ref,
    spread_ref,
    gm_ref,
):
    step = pl.program_id(0)
    tokens = n_rows * group

    gvec_ref[...] = jnp.zeros_like(gvec_ref)
    for h in range(win_ref.shape[1] // block):
        cols = slice(h * block, (h + 1) * block)
        for r in range(n_rows):
            span = slice(r * group, (r + 1) * group)
            adjoint = local_ref[span, cols] + reach_ref[span, cols] * leave_ref[r : r + 1, cols]
            state = state_ref[span, cols]
            at = lax.broadcasted_iota(jnp.int32, state.shape, 0)
            before = jnp.where(at == 0, enter_ref[r : r + 1, cols], pltpu.roll(state, 1, 0))
            reset = mask_ref[span, 0:1]
            live = 1.0 - reset
            recur, rate, decay = decay_of(rpre_ref[span, cols], vec_ref[7:8, cols], reset)
            admit = jax.nn.sigmoid(ipre_ref[span, cols])
            full_decay = jnp.exp(-rate)
            root = jnp.sqrt(one_less_exp(2.0 * rate))
            scale = jnp.where(reset > 0.5, 1.0, root)
            conv = conv_ref[span, cols].astype(F32)
            direct = adjoint * scale
            gadmit = direct * conv
            gconv_ref[span, cols] = direct * admit
            gscale = adjoint * admit * conv
            glog = live * full_decay * (adjoint * before - gscale * full_decay / root)
            gvec_ref[7:8, cols] += jnp.sum(glog * recur, axis=0, keepdims=True)
            grecur = -(vec_ref[7:8, cols] * glog) * recur * (1.0 - recur)
            ginput = gadmit * admit * (1.0 - admit)
            rlow, ilow = grecur.astype(BF), ginput.astype(BF)
            rlow_ref[span, cols] = rlow
            ilow_ref[span, cols] = ilow
            gvec_ref[5:6, cols] += jnp.sum(rlow.astype(F32), axis=0, keepdims=True)
            gvec_ref[6:7, cols] += jnp.sum(ilow.astype(F32), axis=0, keepdims=True)
        rlow, ilow = rlow_ref[:, cols], ilow_ref[:, cols]
        low = conv_ref[:, cols]
        ggr_ref[cols] = dot_tn(low, rlow)
        ggi_ref[cols] = dot_tn(low, ilow)
        gconv_ref[:, cols] += dot_nt(rlow, gr_ref[cols]) + dot_nt(ilow, gi_ref[cols])
        for r in range(n_rows):
            span = slice(r * group, (r + 1) * group)
            head = slice(tokens + HALO * r, tokens + HALO * (r + 1))
            ext_ref[0:HALO] = mixer_ref[head, cols].astype(F32)
            ext_ref[HALO : HALO + group] = mixer_ref[span, cols].astype(F32)
            gconv = gconv_ref[span, cols]
            gvec_ref[4:5, cols] += jnp.sum(gconv, axis=0, keepdims=True)
            gvec_ref[0:1, cols] += jnp.sum(
                gconv * ext_ref[HALO : HALO + group], axis=0, keepdims=True
            )
            spread_ref[0:HALO] = jnp.zeros((HALO, block), F32)
            spread_ref[HALO : HALO + group] = vec_ref[0:1, cols] * gconv
            for k in range(1, 4):
                masked = gconv * mask_ref[span, k : k + 1]
                there = slice(HALO - k, HALO - k + group)
                gvec_ref[k : k + 1, cols] += jnp.sum(
                    masked * ext_ref[there], axis=0, keepdims=True
                )
                spread_ref[there] += vec_ref[k : k + 1, cols] * masked
            gm_ref[head, cols] = spread_ref[0:HALO].astype(BF)
            gm_ref[span, cols] = spread_ref[HALO : HALO + group].astype(BF)
    gm = gm_ref[...]
    sent = gin_send_ref.shape[0]
    gin = dot(left_ref[...], gm).astype(BF)
    gin_send_ref[...] = gin[:sent]
    gin_ref[...] = gin[sent:]
    part = dot_nt(gm, win_ref[...])
    part_branch = dot_nt(gbl_ref[...], wbr_ref[...])

    @pl.when(step == 0)
    def _():
        gfirst_ref[...] = part

    @pl.when(step > 0)
    def _():
        gfirst_ref[...] += part

    gfirst_ref[0:tokens] += part_branch


def gates_call(
    place, reach, local, leave, state, enter, rpre, ipre, conv, mixer, vec, masks, gate_r, gate_i, left, w_in, w_branch, gbl, n_rows, group
):
    model, length = left.shape
    sent = model // place.size["x"]
    tokens, width = state.shape
    block = gate_r.shape[1]
    tile = TILE
    return pl.pallas_call(
        functools.partial(gates_kernel, n_rows, group, block),
        grid=(width // tile,),
        in_specs=[
            columns(tokens),
            columns(tokens),
            columns(n_rows),
            columns(tokens),
            columns(n_rows),
            columns(tokens),
            columns(tokens),
            columns(tokens),
            columns(length),
            columns(16),
            full(masks.shape),
            lines(tile, block),
            lines(tile, block),
            full((model, length)),
            columns(model),
            columns(model),
            columns(tokens),
        ],
        out_specs=[
            columns(sent),
            columns(model - sent),
            lines(tile, block),
            lines(tile, block),
            columns(8),
            full((length, model)),
        ],
        out_shape=[
            in_hbm((sent, width), BF),
            in_hbm((model - sent, width), BF),
            shape_of((width, block), F32),
            shape_of((width, block), F32),
            shape_of((8, width), F32),
            shape_of((length, model), F32),
        ],
        scratch_shapes=[
            pltpu.VMEM((tokens, tile), BF),
            pltpu.VMEM((tokens, tile), BF),
            pltpu.VMEM((tokens, tile), F32),
            pltpu.VMEM((HALO + group, block), F32),
            pltpu.VMEM((HALO + group, block), F32),
            pltpu.VMEM((length, tile), BF),
        ],
        compiler_params=params(40),
        cost_estimate=LIGHT,
        name="recurrence_gates",
    )(reach, local, leave, state, enter, rpre, ipre, conv, mixer, vec, masks, gate_r, gate_i, left, w_in, w_branch, gbl)


def normed(values, gain):
    return values * lax.rsqrt(jnp.mean(values * values, axis=-1, keepdims=True) + EPS) * gain


def halves(value, place, dim):
    half = value.shape[dim] // 2
    mine = lax.dynamic_slice_in_dim(value, place.at["c"] * half, half, dim)
    other = lax.dynamic_slice_in_dim(value, (1 - place.at["c"]) * half, half, dim)
    return mine, other


def own_channels(place, value):
    mine, other = halves(value, place, 0)
    got = place.ring(other, "c", 1)
    pair = place.ordered(mine, got)
    both = jnp.stack(pair, axis=1)
    return both.reshape(-1, both.shape[-1])


def own_devices(place, value, rows):
    shaped = value.reshape(place.chips // 2, 2, rows, value.shape[-1])
    mine = lax.dynamic_index_in_dim(shaped, place.at["c"], 1, keepdims=False)
    other = lax.dynamic_index_in_dim(shaped, 1 - place.at["c"], 1, keepdims=False)
    got = place.ring(other, "c", 1)
    return jnp.concatenate(place.ordered(mine, got), axis=0)


def on_device(
    inputs,
    cotangent,
    segments,
    norm1_gain,
    input_proj,
    branch_proj,
    conv_weight,
    conv_bias,
    recur_gate,
    input_gate,
    recur_bias,
    input_bias,
    decay_param,
    output_proj,
    norm2_gain,
    mlp_gate,
    mlp_up,
    mlp_down,
):
    place = Place()
    core = place.at["c"]
    chips = place.chips
    rows_dev, group, model = inputs.shape
    n_rows = 2 * rows_dev
    tokens_dev = rows_dev * group
    tokens = 2 * tokens_dev
    d_rows, lru = input_proj.shape
    ffn = mlp_gate.shape[1]
    r_rows, block = recur_gate.shape
    f_rows = mlp_down.shape[0]
    lru_half, ffn_half = lru // 2, ffn // 2
    pair = lambda value: place.ring(value, "c", 1)

    order = Order(place)
    lead = (place.size["z"], place.size["y"], place.size["x"])

    wide = [halves(w, place, 1) for w in (input_proj, branch_proj, mlp_gate, mlp_up)]
    got_a = order.ring(jnp.concatenate([w[1] for w in wide[:2]], axis=1), "c")
    got_c = order.ring(jnp.concatenate([w[1] for w in wide[2:]], axis=1), "c")
    span = max(d_rows, r_rows)
    lines_one = [
        jnp.pad(v, (0, span - v.shape[0]))[None]
        for v in (norm1_gain, norm2_gain, conv_bias, recur_bias, input_bias, decay_param)
    ]
    taps = jnp.pad(conv_weight, ((0, 0), (0, span - r_rows)))
    vectors = jnp.concatenate(lines_one[:2] + [taps] + lines_one[2:], axis=0)
    small = Gather(order, vectors[None, None, None, None], "y", 1)
    ids_pair = order.ring(segments, "c")
    mine_a = jnp.concatenate([w[0] for w in wide[:2]], axis=1)
    mine_c = jnp.concatenate([w[0] for w in wide[2:]], axis=1)
    gates = jnp.concatenate([recur_gate, input_gate], axis=0)
    gate_lines = 2 * r_rows * block // lru
    gates = gates.reshape(-1, gate_lines, block).transpose(1, 0, 2).reshape(gate_lines, lru)
    order.must(gates, mine_a)
    small = Gather(order, small.done(), "x", 2)
    got_a = order.wait(got_a)
    rows_a = jnp.concatenate(place.ordered(mine_a, got_a), axis=0)
    group_a = jnp.concatenate([rows_a, gates], axis=0)[None, None, None]
    order.must(group_a)
    both_whole = jnp.concatenate([output_proj, mlp_down], axis=0)
    both_whole = lax.all_gather(both_whole, AXES, axis=0)
    small = Gather(order, small.done(), "c", 3)
    small = Gather(order, small.done(), "z", 0, direct=True)

    a_z = Gather(order, group_a, "z", 0, direct=True)
    grad_out = cotangent.reshape(tokens_dev, model)
    low = grad_out.astype(BF)
    low_other = order.ring(low, "c")
    ids_pair, got_c = order.wait(ids_pair, got_c)
    ids = jnp.concatenate([segments, ids_pair], axis=0)
    prior_ids = order.along(ids[:, group - 3 :], 1)
    gains, vec = small_call(
        place, small.done().reshape(2 * chips, -1, span), d_rows, r_rows
    )
    flat = inputs.reshape(tokens_dev, model)
    (first,) = norm_call([flat], gains, 0)
    first_other = order.ring(first, "c")
    group_c = jnp.concatenate(place.ordered(mine_c, got_c), axis=0)[None, None, None]
    first_other, low_other = order.wait(first_other, low_other)
    tail = jnp.concatenate(
        [v.reshape(rows_dev, group, model)[:, group - 3 :] for v in (first, first_other)], axis=0
    )
    halo = order.along(tail, 1)
    c_z = Gather(order, group_c, "z", 0, both=True)
    a_z = a_z.done()
    halo, prior_ids = order.wait(halo, prior_ids)

    a_left = Gather(order, a_z[..., :lru_half], "y", 1)
    a_right = Gather(order, a_z[..., lru_half:], "x", 2)
    a_left, a_right = a_left.done(), a_right.done()

    a_left = Gather(order, a_left, "x", 2)
    a_right = Gather(order, a_right, "y", 1)
    c_z.next()
    a_left.arrived()
    a_right.arrived()

    chip_d = 2 * d_rows
    packed = [g.whole([p[..., chip_d:, :] for p in g.pieces]) for g in (a_left, a_right)]
    packed = jnp.concatenate(packed, axis=-1)
    packed = packed.reshape(chips, gate_lines, -1, block)
    packed = packed.transpose(0, 2, 1, 3).reshape(chips, 2, r_rows, block)
    packed = jnp.concatenate([packed[:, 0], packed[:, 1]], axis=-1)
    gate_mine, gate_other = halves(packed, place, 0)
    gate_got = order.ring(gate_other, "c")
    c_z = c_z.done()
    c_left = Gather(order, c_z[..., :ffn_half], "y", 1)
    c_right = Gather(order, c_z[..., ffn_half:], "x", 2)
    halo = jnp.pad(halo, ((0, 0), (HALO - 3, 0), (0, 0))).reshape(n_rows * HALO, model)
    position = place.s * group + jnp.arange(group, dtype=jnp.int32)
    joined_ids = jnp.concatenate([prior_ids, ids], axis=1)
    marks = [(joined_ids[:, 2 : 2 + group] != ids) | (position == 0)[None, :]]
    for k in range(1, 4):
        marks.append(
            (joined_ids[:, 3 - k : 3 - k + group] == ids) & (position >= k)[None, :]
        )
    masks = jnp.stack(marks, axis=-1).astype(F32).reshape(tokens, 4)
    masks = jnp.pad(masks, ((0, 0), (0, 4)))
    gate_got = order.wait(gate_got)
    packed = jnp.stack(place.ordered(gate_mine, gate_got), axis=1).reshape(-1, 2 * block)
    gate_r, gate_i = packed[:, :block], packed[:, block:]
    first_ext, branch_pre, mixer, conv, rpre, ipre, through, local, ends, w_in, w_branch = forward_call(
        place, first, first_other, halo, a_left.weight(chip_d), a_right.weight(chip_d), vec, masks, gate_r, gate_i, n_rows, group, chip_d
    )
    enter = Carry(order, ends, 1)
    more = enter.next()
    c_left, c_right = c_left.done(), c_right.done()

    c_left = Gather(order, c_left, "x", 2)
    c_right = Gather(order, c_right, "y", 1)
    both_whole = order.wait(both_whole)
    w_out, w_down = split_call(
        place, both_whole, ((0, r_rows), (r_rows, r_rows + f_rows))
    )
    order.must(w_out, w_down)
    enter = enter.done() if more else enter.total[4:]
    state, mixed, part, part_other = mix_call(
        local, through, enter, branch_pre, w_out, n_rows, group
    )
    part_pair = order.ring(part_other, "c")
    first_l, first_r = turn_call(place, order.tie(first_ext), chip_d)
    order.must(first_l, first_r)
    w_gate, w_up = c_left.weight(chip_d), c_right.weight(chip_d)
    part_pair = order.wait(part_pair)
    second, middle = norm_call([flat, part, part_pair], gains, 1)
    second_other = order.ring(second, "c")
    second_other = order.wait(second_other)

    nz, ny, nx = lead

    def blocks_of(send, rest, axis, other):
        shape = (place.size[other], nz, chip_d, -1)
        rest = rest.reshape((place.size[axis] - 1,) + shape)
        return [send.reshape(shape)] + [rest[i] for i in range(rest.shape[0])]

    def joined(left, right):
        return [jnp.concatenate(p, axis=-1) for p in zip(left.done(nz), right.done(nz))]

    g_send, g_rest, u_send, u_rest, down_mine, down_other, part, part_other, back, back_other = ffn_call(
        place, second, second_other, low, low_other, w_gate, w_up, w_down, chip_d, f_rows
    )

    back_pair = order.ring(back_other, "c")
    g_left = Scatter(order, blocks_of(g_send, g_rest, "x", "y"), "x")
    g_right = Scatter(order, blocks_of(u_send, u_rest, "y", "x"), "y")
    down_got = order.ring(down_other, "c")
    back_pair = order.wait(back_pair)
    grad_middle, mid_low, grad_gain_two = norm_back_call(
        [back, back_pair], middle, gains, 1, grad_out, 1
    )
    mid_pair = order.ring(mid_low, "c")
    down_got = order.wait(down_got)
    (d_z,) = regroup_call(place, down_mine, down_got, ("zyx",), ((0, model),))
    d_z = Scatter(order, d_z, "z")
    mid_other = order.wait(mid_pair)
    g_out, b_send, b_rest, gbl, reach, local_back, ends_back = back_call(
        place, mid_low, mid_other, w_out, branch_pre, state, rpre, mixed, vec, masks, first_r, n_rows, group
    )
    d_z.take()
    leave = Carry(order, ends_back, -1)
    g_left.next()
    g_right.next()
    more = leave.next()

    g_left = Scatter(order, g_left.done(ny), "y")
    g_right = Scatter(order, g_right.done(nx), "x")
    leave = leave.done() if more else leave.total[4:]
    d_z.next()
    in_send, in_rest, g_gate_r, g_gate_i, g_vec, grad_first = gates_call(
        place, reach, local_back, leave, state, enter, rpre, ipre, conv, mixer, vec, masks, gate_r, gate_i, first_l, w_in, w_branch, gbl, n_rows, group
    )
    order.must(in_send)
    g_left.next()
    g_right.next()
    d_z.take()

    a_left = Scatter(order, blocks_of(in_send, in_rest, "x", "y"), "x")
    a_right = Scatter(order, blocks_of(b_send, b_rest, "y", "x"), "y")
    out_mine, out_other = pack_call(place, g_out, g_gate_r, g_gate_i, g_vec, vec, r_rows)
    out_got = order.ring(out_other, "c")
    out_got = order.wait(out_got)
    wide_r = out_mine.shape[-1]
    cut = (wide_r // (2 * block)) * block
    o_left, o_right = regroup_call(
        place, out_mine, out_got, ("xyz", "yxz"), ((0, cut), (cut, wide_r))
    )
    d_z.next()
    g_both = Scatter(order, joined(g_left, g_right), "z", both=True)
    order.must(o_left[0], o_right[0])
    a_left.next()
    a_right.next()

    a_left = Scatter(order, a_left.done(ny), "y")
    a_right = Scatter(order, a_right.done(nx), "x")
    o_left = Scatter(order, o_left, "x")
    o_right = Scatter(order, o_right, "y")
    d_z.take()
    g_both.next()
    spill = grad_first[tokens:].reshape(n_rows, HALO, model)[:, HALO - 3 :]
    spill = order.along(spill, -1)
    a_left.next()
    a_right.next()
    o_left.next()
    o_right.next()

    a_both = Scatter(order, joined(a_left, a_right), "z", both=True)
    o_left = Scatter(order, o_left.done(ny), "y")
    o_right = Scatter(order, o_right.done(nx), "x")
    spill = order.wait(spill)
    spill = jnp.pad(spill, ((0, 0), (group - 3, 0), (0, 0))).reshape(tokens, model)
    grad_first = grad_first[:tokens] + spill
    first_pair = order.ring(grad_first[tokens_dev:], "c")
    first_pair = order.wait(first_pair)
    grad_inputs, grad_gain_one = norm_back_call(
        [grad_first[:tokens_dev], first_pair], flat, gains, 0, grad_middle, 0
    )
    order.must(grad_inputs)
    d_x = Scatter(order, d_z.done(ny), "y")
    a_both.next()
    o_left.next()
    o_right.next()
    d_x.next()

    o_both = Scatter(order, joined(o_left, o_right), "z", both=True)
    d_y = Scatter(order, d_x.done(nx), "x")
    g_gains = jnp.concatenate([grad_gain_one, grad_gain_two], axis=0)
    g_gains = jnp.transpose(g_gains.reshape(2, chips, 2, d_rows), (1, 2, 0, 3))
    g_gains = g_gains.reshape(lead + (2, 2 * d_rows))
    g_gains = jnp.moveaxis(behind(place, "yxz", g_gains), 3, 0)
    gains_mine = lax.dynamic_index_in_dim(g_gains, core, 0, False)
    gains_got = order.ring(lax.dynamic_index_in_dim(g_gains, 1 - core, 0, False), "c")
    part_pair = order.ring(part_other, "c")

    def whole_columns(value):
        mine, other = halves(value, place, 0)
        return mine, order.ring(other, "c")

    gains_got, part_pair = order.wait(gains_got, part_pair)
    result = middle + (part + part_pair)
    order.must(result)
    g_gains = gains_mine + gains_got
    g_gains = Scatter(order, [g_gains[i] for i in range(ny)], "y", between=F32)
    a_both.next()
    sum_c = whole_columns(g_both.done(dtype=F32))
    g_gains = Scatter(order, g_gains.done(nx, F32), "x", between=F32)
    o_both.next()
    sum_down = d_y.done(dtype=F32)
    order.must(sum_down)
    g_gains = Scatter(order, g_gains.done(nz, F32), "z", direct=True, between=F32)
    low_c, high_c = place.ordered(sum_c[0], order.wait(sum_c[1]))
    grad_gate = jnp.concatenate([low_c[:, :ffn_half], high_c[:, :ffn_half]], axis=1)
    grad_up = jnp.concatenate([low_c[:, ffn_half:], high_c[:, ffn_half:]], axis=1)
    order.must(grad_gate, grad_up)
    sum_a = whole_columns(a_both.done(dtype=F32))
    o_both.next()
    low_a, high_a = place.ordered(sum_a[0], order.wait(sum_a[1]))
    grad_input_proj = jnp.concatenate([low_a[:, :lru_half], high_a[:, :lru_half]], axis=1)
    grad_branch_proj = jnp.concatenate([low_a[:, lru_half:], high_a[:, lru_half:]], axis=1)
    order.must(grad_input_proj, grad_branch_proj)
    own = o_both.done(dtype=F32)
    g_gains = g_gains.done(dtype=F32).reshape(2, d_rows)
    own_gates = own[:, model : model + 2 * block]
    own_vec = own[:, model + 2 * block : model + 2 * block + 8].T
    return (
        result.reshape(inputs.shape),
        grad_inputs.reshape(inputs.shape),
        g_gains[0],
        grad_input_proj,
        grad_branch_proj,
        own_vec[:4],
        own_vec[4],
        own_gates[:, :block],
        own_gates[:, block:],
        own_vec[5],
        own_vec[6],
        own_vec[7],
        own[:, :model],
        g_gains[1],
        grad_gate,
        grad_up,
        sum_down,
    )


def solution(mesh):
    seq, row = mesh.shape["seq"], mesh.shape["row"]
    ny = 1 << ((seq.bit_length() - 1) // 2)
    grid = Mesh(mesh.devices.reshape(seq // ny, ny, row // 2, 2), AXES)
    tokens, line, flat, taps = P(("x", "c"), ("z", "y"), None), P(AXES, None), P(AXES), P(None, AXES)
    in_specs = (
        tokens,
        tokens,
        P(("x", "c"), ("z", "y")),
        flat,
        line,
        line,
        taps,
        flat,
        line,
        line,
        flat,
        flat,
        flat,
        line,
        flat,
        line,
        line,
        line,
    )
    out_specs = (
        tokens,
        tokens,
        flat,
        line,
        line,
        taps,
        flat,
        line,
        line,
        flat,
        flat,
        flat,
        line,
        flat,
        line,
        line,
        line,
    )
    return jax.shard_map(
        on_device, mesh=grid, in_specs=in_specs, out_specs=out_specs, check_vma=False
    )
```

```python
import functools
import math

import jax
import jax.numpy as jnp
import numpy as np
from jax import lax
from jax.experimental import pallas as pl
from jax.experimental.pallas import tpu as pltpu
from jax.sharding import Mesh, PartitionSpec as P

EPS = 1e-06
BF = jnp.bfloat16
F32 = jnp.float32
AXES = ("z", "y", "x", "c")
MIB = 1 << 20
TILE = 256
HALO = 8
GELU_C = math.sqrt(2.0 / math.pi)


class Place:
    def __init__(self):
        self.size = {axis: lax.axis_size(axis) for axis in AXES}
        self.at = {axis: lax.axis_index(axis) for axis in AXES}
        nz, ny, nx, _ = self.size.values()
        self.seq, self.row = nz * ny, nx * 2
        self.s = self.at["z"] * ny + self.at["y"]
        self.stride = {"z": ny * self.row, "y": self.row, "x": 2, "c": 1}
        self.chips = nz * ny * nx
        self.sizes = (nz, ny, nx)
        self.where = jnp.stack([self.at[axis] for axis in AXES]).astype(jnp.int32)


    def ring(self, value, axis, shift):
        pairs = []
        for i in range(self.seq * self.row):
            at = (i // self.stride[axis]) % self.size[axis]
            to = (at + shift) % self.size[axis]
            pairs.append((i, i + (to - at) * self.stride[axis]))
        return lax.ppermute(value, AXES, pairs)

    def along(self, value, distance):
        pairs = []
        for s in range(self.seq):
            if 0 <= s + distance < self.seq:
                for r in range(self.row):
                    pairs.append((s * self.row + r, (s + distance) * self.row + r))
        return lax.ppermute(value, AXES, pairs)

    def ordered(self, mine, other):
        high = self.at["c"] != 0
        return jnp.where(high, other, mine), jnp.where(high, mine, other)


class Order:
    def __init__(self, place):
        self.place = place
        self.last = ()
        self.sent = ()

    def tie(self, value):
        if not self.last:
            return value
        return lax.optimization_barrier((value,) + self.last)[0]

    def must(self, *values):
        self.sent += values

    def ring(self, value, axis, shift=1):
        value = self.tie(value)
        self.sent += (value,)
        return self.place.ring(value, axis, shift)

    def along(self, value, distance):
        value = self.tie(value)
        self.sent += (value,)
        return self.place.along(value, distance)

    def wait(self, *values):
        n = len(values)
        held = values + self.last + self.sent
        if len(held) > n:
            values = lax.optimization_barrier(held)[:n]
        self.last = tuple(values)
        self.sent = ()
        return values[0] if n == 1 else values


class Gather:
    def __init__(self, order, value, axis, dim, direct=False, both=False):
        self.order, self.axis, self.dim = order, axis, dim
        self.n = order.place.size[axis]
        self.pieces = [value]
        self.direct = direct
        self.both = both and self.n == 4
        if self.both:
            self.flying = [order.ring(value, axis, 1), order.ring(value, axis, 3)]
            return
        shifts = range(1, self.n) if direct else range(1, min(2, self.n))
        self.flying = [order.ring(value, axis, k) for k in shifts]

    def next(self):
        if self.direct:
            if self.flying:
                got = self.order.wait(*self.flying)
                self.pieces += [got] if len(self.flying) == 1 else list(got)
            self.flying = []
            return
        if self.both:
            if len(self.flying) == 2:
                one, three = self.order.wait(*self.flying)
                self.pieces += [one, None, three]
                self.flying = [self.order.ring(one, self.axis)]
            elif self.flying:
                self.pieces[2] = self.order.wait(self.flying.pop())
            return
        got = self.order.wait(self.flying.pop())
        self.pieces.append(got)
        if len(self.pieces) < self.n:
            self.flying = [self.order.ring(got, self.axis)]

    def arrived(self):
        while len(self.pieces) < self.n or (self.both and self.flying):
            self.next()
        return self.pieces

    def done(self):
        return self.whole(self.arrived())

    def whole(self, pieces):
        at = self.order.place.at[self.axis]
        if self.n == 2:
            high = at != 0
            mine, other = pieces
            parts = [jnp.where(high, other, mine), jnp.where(high, mine, other)]
            return jnp.concatenate(parts, axis=self.dim)
        parts = [
            lax.select_n(lax.rem(at - j + self.n, self.n), *pieces) for j in range(self.n)
        ]
        return jnp.concatenate(parts, axis=self.dim)

    def weight(self, rows):
        if rows % 16 == 0:
            return self.arrived()
        whole = self.done()[..., :rows, :]
        return [whole.reshape(-1, whole.shape[-1])]


class Scatter:
    def __init__(self, order, blocks, axis, direct=False, between=BF, both=False):
        self.order, self.axis, self.blocks = order, axis, list(blocks)
        self.n = order.place.size[axis]
        self.both = both and self.n == 4
        self.direct, self.between = direct, between
        self.hop = 0
        self.held = False
        if self.both:
            self.flying = [order.ring(self.blocks[1], axis, 3), order.ring(self.blocks[2], axis, 1)]
        elif direct:
            self.flying = [
                order.ring(self.blocks[i], axis, self.n - 1 - i) for i in range(self.n - 1)
            ]
        elif self.n > 1:
            self.flying = order.ring(self.blocks[0], axis)

    def next(self):
        if self.both:
            if self.hop == 0:
                far, near = self.order.wait(*self.flying)
                total = far.astype(F32) + self.blocks[0].astype(F32)
                self.got = [near]
                self.flying = self.order.ring(total.astype(self.between), self.axis, 3)
                self.hop = 1
            elif self.hop == 1:
                self.got.append(self.order.wait(self.flying))
                self.hop = self.n - 1
            return
        if self.direct:
            if self.n > 1:
                got = self.order.wait(*self.flying)
                self.got = [got] if self.n == 2 else list(got)
            self.hop = self.n - 1
            return
        if not self.held:
            self.take()
        self.held = False
        if self.hop < self.n - 1:
            total = self.got[0].astype(F32) + self.blocks[self.hop].astype(F32)
            self.flying = self.order.ring(total.astype(self.between), self.axis)

    def take(self):
        self.got = [self.order.wait(self.flying)]
        self.hop += 1
        self.held = True

    def done(self, parts=0, dtype=BF):
        if self.held:
            self.next()
        while self.hop < self.n - 1:
            self.next()
        terms = [self.blocks[-1]] + (self.got if self.n > 1 else [])

        def total(pick):
            values = [pick(t).astype(F32) for t in terms]
            return functools.reduce(jnp.add, values).astype(dtype)

        if not parts:
            return total(lambda t: t)
        return [total(lambda t, i=i: t[i]) for i in range(parts)]


def behind(place, order_of_axes, value):
    for dim, axis in enumerate(("z", "y", "x")):
        n, at = place.size[axis], place.at[axis]
        picks = [
            lax.dynamic_index_in_dim(value, lax.rem(at - i - 1 + 2 * n, n), dim)
            for i in range(n)
        ]
        value = jnp.concatenate(picks, axis=dim)
    dims = ["zyx".index(axis) for axis in order_of_axes]
    return jnp.transpose(value, tuple(dims) + tuple(range(3, value.ndim)))


def sources(place, order_of_axes, rows):
    lead = tuple(place.size[a] for a in "zyx")
    at = jnp.arange(math.prod(lead) * rows, dtype=jnp.int32).reshape(lead + (rows,))
    return behind(place, order_of_axes, at).reshape(-1)


def compose(earlier, later):
    return jnp.concatenate(
        [earlier[:4] * later[:4], later[:4] * earlier[4:] + later[4:]], axis=0
    )


class Carry:
    def __init__(self, order, end_map, sign, most=3):
        self.order, self.sign, self.most = order, sign, most
        self.n = order.place.seq
        self.unit = jnp.concatenate(
            [jnp.ones_like(end_map[:4]), jnp.zeros_like(end_map[4:])], axis=0
        )
        self.total = None
        self.reach = 0
        self.send(end_map, 1)

    def send(self, value, width):
        self.shifts = []
        distance = max(self.reach, 1)
        while distance < self.n and len(self.shifts) < self.most:
            self.shifts.append(distance)
            distance += width
        self.width = width
        self.flying = [self.order.along(value, self.sign * d) for d in self.shifts]

    def next(self):
        got = self.order.wait(*self.flying)
        got = [got] if len(self.flying) == 1 else list(got)
        s, n = self.order.place.s, self.n
        for value, d in zip(got, self.shifts):
            inside = (s >= d) if self.sign > 0 else (s < n - d)
            part = jnp.where(inside, value, self.unit)
            self.total = part if self.total is None else compose(part, self.total)
        self.reach += self.width * len(self.shifts)
        if self.reach < self.n - 1:
            self.send(self.total, self.reach)
            return True
        return False

    def done(self):
        while self.next():
            pass
        return self.total[4:]


def dot(a, b):
    return jnp.dot(a, b, preferred_element_type=F32)


def dot_nt(a, b):
    return lax.dot_general(a, b, (((1,), (1,)), ((), ())), preferred_element_type=F32)


def dot_tn(a, b):
    return lax.dot_general(a, b, (((0,), (0,)), ((), ())), preferred_element_type=F32)


def moved(value, distance, fill):
    n = value.shape[0]
    size = abs(distance)
    edge = jnp.full((size,) + value.shape[1:], fill, value.dtype)
    if size % 8 == 0:
        if distance > 0:
            return jnp.concatenate([edge, value[: n - size]], axis=0)
        return jnp.concatenate([value[size:], edge], axis=0)
    at = lax.broadcasted_iota(jnp.int32, value.shape, 0)
    turned = pltpu.roll(value, distance % n, 0)
    inside = at >= size if distance > 0 else at < n - size
    return jnp.where(inside, turned, fill)


def scan_tile(decay, drive, sign):
    n = decay.shape[0]
    distance = 1
    while distance < n:
        drive = decay * moved(drive, sign * distance, 0.0) + drive
        decay = decay * moved(decay, sign * distance, 1.0)
        distance *= 2
    return decay, drive


def one_less_exp(u):
    term = jnp.full_like(u, 1.0 / 3628800.0)
    for k in (362880, 40320, 5040, 720, 120, 24, 6, 2):
        term = 1.0 / k - u * term
    small = u * (1.0 - u * term)
    return jnp.where(u < 0.8, small, 1.0 - jnp.exp(-u))


def log2(n):
    return n.bit_length() - 1


def source_rows(order, sizes, at_ref, rows, first, count):
    spot = {"z": at_ref[0], "y": at_ref[1], "x": at_ref[2]}
    size = dict(zip("zyx", sizes))
    line = first + lax.broadcasted_iota(jnp.int32, (count, 1), 0)
    inside = line & (rows - 1)
    line = line >> log2(rows)
    where = {}
    for axis in reversed(order):
        n = size[axis]
        where[axis] = (spot[axis] + (n - 1) - (line & (n - 1))) & (n - 1)
        line = line >> log2(n)
    chip = (where["z"] * size["y"] + where["y"]) * size["x"] + where["x"]
    return chip * rows + inside


def turn_rows(order, sizes, at_ref, value, rows, out_ref):
    total = value.shape[1]
    step = min(total, 256)
    for first in range(0, total, step):
        source = source_rows(order, sizes, at_ref, rows, first, step)
        lane = lax.broadcasted_iota(jnp.int32, (step, total), 1)
        pick = jnp.where(source == lane, 1.0, 0.0).astype(BF)
        out_ref[first : first + step] = dot_nt(pick, value).astype(BF)


def gelu_parts(value):
    square = value * value
    t = jnp.tanh(GELU_C * value * (1.0 + 0.044715 * square))
    half = 0.5 * (1.0 + t)
    slope = half + 0.5 * value * (1.0 - t * t) * GELU_C * (1.0 + 3.0 * 0.044715 * square)
    return value * half, slope


def full(shape):
    return pl.BlockSpec(shape, lambda j: (0,) * len(shape))


def columns(rows, width=TILE):
    return pl.BlockSpec((rows, width), lambda j: (0, j))


def lines(rows, width):
    return pl.BlockSpec((rows, width), lambda j: (j, 0))


def in_hbm(shape, dtype):
    return pltpu.HBM(shape, dtype)


def piece_specs(pieces, rows, tile=TILE):
    if len(pieces) == 1:
        return [columns(pieces[0].shape[0], tile)]
    block = pieces[0].shape[:3] + (rows, tile)
    return [pl.BlockSpec(block, lambda j: (0, 0, 0, 0, j)) for _ in pieces]


def piece_scratch(place, pieces, rows, tile=TILE):
    if len(pieces) == 1:
        return pltpu.VMEM((16, 128), BF)
    return pltpu.VMEM(place.sizes + (rows, tile), BF)


def from_pieces(at, dim, refs, out_ref):
    n = len(refs)
    if n == 1:
        return refs[0][...]
    for k, ref in enumerate(refs):
        where = pl.ds((at - k + n) & (n - 1), 1)
        out_ref[(slice(None),) * dim + (where,)] = ref[...]
    whole = out_ref[...]
    return whole.reshape(-1, whole.shape[-1])


def shape_of(shape, dtype):
    return jax.ShapeDtypeStruct(shape, dtype)


def params(limit):
    return pltpu.CompilerParams(vmem_limit_bytes=limit * MIB)


LIGHT = pl.CostEstimate(flops=1, bytes_accessed=1, transcendentals=0)


def turn_kernel(sizes, rows, at_ref, first_ref, left_ref, right_ref):
    turn_rows("xyz", sizes, at_ref, first_ref[...], rows, left_ref)
    turn_rows("yxz", sizes, at_ref, first_ref[...], rows, right_ref)


def turn_call(place, first, rows):
    length, model = first.shape
    whole = pl.BlockSpec(memory_space=pltpu.VMEM)
    return pl.pallas_call(
        functools.partial(turn_kernel, place.sizes, rows),
        in_specs=[pl.BlockSpec(memory_space=pltpu.SMEM), whole],
        out_specs=[whole] * 2,
        out_shape=[shape_of((model, length), BF)] * 2,
        compiler_params=params(24),
        cost_estimate=LIGHT,
        name="turn",
    )(place.where, first)


def small_kernel(d_rows, r_rows, at_ref, small_ref, qd_ref, md_ref, qr_ref, mr_ref, gain_ref, vec_ref):
    def spread(row, q_ref, m_ref):
        value = dot(small_ref[:, row, :], q_ref[...])
        return jnp.sum(value * m_ref[...], axis=0, keepdims=True)

    for k in range(2):
        gain_ref[k : k + 1] = spread(k, qd_ref, md_ref)
    half = vec_ref.shape[1]
    for k in range(8):
        value = spread(2 + k, qr_ref, mr_ref)
        value = jnp.where(at_ref[3] == 0, value[:, :half], value[:, half:])
        if k == 7:
            soft = jnp.maximum(value, 0.0) + jnp.log1p(jnp.exp(-jnp.abs(value)))
            vec_ref[8:9] = -8.0 * jax.nn.sigmoid(value)
            value = 8.0 * soft
        vec_ref[k : k + 1] = value


def small_call(place, small, d_rows, r_rows):
    devices, _, span = small.shape
    operands = []
    for rows in (d_rows, r_rows):
        lane = np.arange(devices * rows)
        operands.append(jnp.asarray(lane[None] % rows == np.arange(span)[:, None], BF))
        operands.append(jnp.asarray(lane[None] // rows == np.arange(devices)[:, None], F32))
    whole = pl.BlockSpec(memory_space=pltpu.VMEM)
    return pl.pallas_call(
        functools.partial(small_kernel, d_rows, r_rows),
        in_specs=[pl.BlockSpec(memory_space=pltpu.SMEM)] + [whole] * 5,
        out_specs=[whole] * 2,
        out_shape=[shape_of((2, devices * d_rows), F32), shape_of((16, devices * r_rows // 2), F32)],
        compiler_params=params(24),
        cost_estimate=LIGHT,
        name="small_weights",
    )(place.where, small, *operands)


def norm_kernel(n_terms, row, *refs):
    terms, gain_ref, outs = refs[:n_terms], refs[n_terms], refs[n_terms + 1 :]
    value = functools.reduce(jnp.add, [t[...] for t in terms])
    scale = lax.rsqrt(jnp.mean(value * value, axis=-1, keepdims=True) + EPS)
    outs[0][...] = (value * scale * gain_ref[row : row + 1]).astype(BF)
    if n_terms > 1:
        outs[1][...] = value


def norm_call(terms, gains, row):
    tokens, model = terms[0].shape
    step = tokens // 4
    block = pl.BlockSpec((step, model), lambda j: (j, 0))
    shapes = [in_hbm((tokens, model), BF), shape_of((tokens, model), F32)]
    shapes = shapes[: 1 if len(terms) == 1 else 2]
    return pl.pallas_call(
        functools.partial(norm_kernel, len(terms), row),
        grid=(4,),
        in_specs=[block] * len(terms) + [full(gains.shape)],
        out_specs=[block] * len(shapes),
        out_shape=shapes,
        compiler_params=params(16),
        cost_estimate=LIGHT,
        name="norm",
    )(*terms, gains)


def norm_back_kernel(n_terms, row, low, *refs):
    terms = refs[:n_terms]
    value_ref, gain_ref, add_ref, out_ref = refs[n_terms : n_terms + 4]
    gain_out = refs[-1]
    grad = functools.reduce(jnp.add, [t[...] for t in terms])
    value = value_ref[...]
    scale = lax.rsqrt(jnp.mean(value * value, axis=-1, keepdims=True) + EPS)
    unit = value * scale
    inner = grad * gain_ref[row : row + 1]
    total = add_ref[...] + scale * (inner - unit * jnp.mean(inner * unit, axis=-1, keepdims=True))
    out_ref[...] = total
    if low:
        refs[n_terms + 4][...] = total.astype(BF)
    part = jnp.sum(grad * unit, axis=0, keepdims=True)

    @pl.when(pl.program_id(0) == 0)
    def _():
        gain_out[...] = part

    @pl.when(pl.program_id(0) > 0)
    def _():
        gain_out[...] += part


def norm_back_call(terms, value, gains, row, add, low):
    tokens, model = value.shape
    step = tokens // 4
    block = pl.BlockSpec((step, model), lambda j: (j, 0))
    shapes = [shape_of((tokens, model), F32)] + [in_hbm((tokens, model), BF)] * low
    return pl.pallas_call(
        functools.partial(norm_back_kernel, len(terms), row, low),
        grid=(4,),
        in_specs=[block] * len(terms) + [block, full(gains.shape), block],
        out_specs=[block] * len(shapes) + [full((1, model))],
        out_shape=shapes + [shape_of((1, model), F32)],
        compiler_params=params(16),
        cost_estimate=LIGHT,
        name="norm_back",
    )(*terms, value, gains, add)


def pack_kernel(at_ref, go_ref, gr_ref, gi_ref, gvec_ref, vec_ref, mine_ref, other_ref):
    pairs, rows, _ = mine_ref.shape
    model, block = go_ref.shape[1], gr_ref.shape[1]
    line = lax.broadcasted_iota(jnp.int32, gvec_ref.shape, 0)
    gvec = jnp.where(line == 7, gvec_ref[...] * vec_ref[8:9], gvec_ref[...]).astype(BF)
    slot = lax.broadcasted_iota(jnp.int32, (8, block), 0)
    lane = lax.broadcasted_iota(jnp.int32, (8, block), 1)
    turned = dot_tn(gvec, jnp.where(slot == lane, 1.0, 0.0).astype(BF)).astype(BF)
    gr, gi = gr_ref[...].astype(BF), gi_ref[...].astype(BF)
    for k in range(2):

        @pl.when(at_ref[3] == k)
        def _():
            for q in range(pairs):
                for ref, which in ((mine_ref, k), (other_ref, 1 - k)):
                    span = slice((2 * q + which) * rows, (2 * q + which + 1) * rows)
                    ref[q, :, 0:model] = go_ref[span]
                    ref[q, :, model : model + block] = gr[span]
                    ref[q, :, model + block : model + 2 * block] = gi[span]
                    ref[q, :, model + 2 * block :] = turned[span]


def pack_call(place, g_out, g_gate_r, g_gate_i, g_vec, vec, rows):
    width, model = g_out.shape
    block = g_gate_r.shape[1]
    shape = (width // (2 * rows), rows, model + 3 * block)
    whole = pl.BlockSpec(memory_space=pltpu.VMEM)
    return pl.pallas_call(
        pack_kernel,
        in_specs=[pl.BlockSpec(memory_space=pltpu.SMEM)] + [whole] * 5,
        out_specs=[whole] * 2,
        out_shape=[shape_of(shape, BF), shape_of(shape, BF)],
        compiler_params=params(24),
        cost_estimate=LIGHT,
        name="pack",
    )(place.where, g_out, g_gate_r, g_gate_i, g_vec, vec)


def forward_kernel(
    n_rows,
    group,
    block,
    n_in,
    n_branch,
    at_ref,
    mine_ref,
    other_ref,
    halo_ref,
    *refs,
):
    w_refs, wb_refs, refs = refs[:n_in], refs[n_in : n_in + n_branch], refs[n_in + n_branch :]
    vec_ref, mask_ref, gr_ref, gi_ref, first_ref, bpre_ref, mixer_ref, conv_ref = refs[:8]
    rpre_ref, ipre_ref, through_ref, local_ref, ends_ref, w_ref, wb_ref = refs[8:15]
    ext_ref, in_ref, branch_ref = refs[15:]
    half = mine_ref.shape[0]
    w_ref[...] = from_pieces(at_ref[2], 2, w_refs, in_ref)
    wb_ref[...] = from_pieces(at_ref[1], 1, wb_refs, branch_ref)

    @pl.when(pl.program_id(0) == 0)
    def _():
        first_ref[0:half] = mine_ref[...]
        first_ref[half : 2 * half] = other_ref[...]
        first_ref[2 * half :] = halo_ref[...]

    mixer = dot(first_ref[...], w_ref[...]).astype(BF)
    bpre_ref[...] = dot(first_ref[0 : 2 * half], wb_ref[...])
    mixer_ref[...] = mixer
    wide = mixer.astype(F32)
    tokens = n_rows * group
    for r in range(n_rows):
        ext_ref[r, 0:HALO] = wide[tokens + HALO * r : tokens + HALO * (r + 1)]
        ext_ref[r, HALO : HALO + group] = wide[r * group : (r + 1) * group]
    for r in range(n_rows):
        span = slice(r * group, (r + 1) * group)
        conv = vec_ref[4:5] + vec_ref[0:1] * ext_ref[r, HALO : HALO + group]
        for k in range(1, 4):
            conv += (
                vec_ref[k : k + 1]
                * ext_ref[r, HALO - k : HALO - k + group]
                * mask_ref[span, k : k + 1]
            )
        conv_ref[span] = conv.astype(BF)
    for h in range(w_ref.shape[1] // block):
        cols = slice(h * block, (h + 1) * block)
        low = conv_ref[:, cols]
        rpre_ref[:, cols] = dot(low, gr_ref[cols]) + vec_ref[5:6, cols]
        ipre_ref[:, cols] = dot(low, gi_ref[cols]) + vec_ref[6:7, cols]
        for r in range(n_rows):
            span = slice(r * group, (r + 1) * group)
            recur = jax.nn.sigmoid(rpre_ref[span, cols])
            admit = jax.nn.sigmoid(ipre_ref[span, cols])
            rate = vec_ref[7:8, cols] * recur
            reset = mask_ref[span, 0:1]
            decay = jnp.exp(-rate) * (1.0 - reset)
            scale = jnp.where(reset > 0.5, 1.0, jnp.sqrt(one_less_exp(2.0 * rate)))
            drive = scale * admit * conv_ref[span, cols].astype(F32)
            decay, drive = scan_tile(decay, drive, 1)
            through_ref[span, cols] = decay
            local_ref[span, cols] = drive
            ends_ref[r : r + 1, cols] = decay[group - 1 : group]
            ends_ref[n_rows + r : n_rows + r + 1, cols] = drive[group - 1 : group]


def forward_call(place, mine, other, halo, w_in, w_branch, vec, masks, gate_r, gate_i, n_rows, group, chip_d):
    model = mine.shape[1]
    length = 2 * mine.shape[0] + halo.shape[0]
    width, block = w_in[0].shape[-1], gate_r.shape[1]
    tokens = n_rows * group
    tile = TILE
    return pl.pallas_call(
        functools.partial(
            forward_kernel, n_rows, group, block, len(w_in), len(w_branch)
        ),
        grid=(width // tile,),
        in_specs=[
            pl.BlockSpec(memory_space=pltpu.SMEM),
            full(mine.shape),
            full(mine.shape),
            full(halo.shape),
            *piece_specs(w_in, chip_d),
            *piece_specs(w_branch, chip_d),
            columns(16),
            full(masks.shape),
            lines(tile, block),
            lines(tile, block),
        ],
        out_specs=[full((length, model)), columns(tokens), columns(length)]
        + [columns(tokens)] * 5
        + [columns(2 * n_rows), columns(model), columns(model)],
        out_shape=[
            in_hbm((length, model), BF),
            in_hbm((tokens, width), F32),
            in_hbm((length, width), BF),
            in_hbm((tokens, width), BF),
            in_hbm((tokens, width), F32),
            in_hbm((tokens, width), F32),
            in_hbm((tokens, width), F32),
            in_hbm((tokens, width), F32),
            in_hbm((2 * n_rows, width), F32),
            in_hbm((model, width), BF),
            in_hbm((model, width), BF),
        ],
        scratch_shapes=[
            pltpu.VMEM((n_rows, HALO + group, tile), F32),
            piece_scratch(place, w_in, chip_d),
            piece_scratch(place, w_branch, chip_d),
        ],
        compiler_params=params(24),
        cost_estimate=LIGHT,
        name="recurrence_forward",
    )(place.where, mine, other, halo, *w_in, *w_branch, vec, masks, gate_r, gate_i)


def mix_kernel(
    n_rows, group, local_ref, through_ref, enter_ref, bpre_ref, w_ref, state_ref, mixed_ref, part_ref, part_other_ref
):
    for r in range(n_rows):
        span = slice(r * group, (r + 1) * group)
        state = local_ref[span] + through_ref[span] * enter_ref[r : r + 1]
        state_ref[span] = state
        branch, _ = gelu_parts(bpre_ref[span])
        mixed_ref[span] = (state * branch).astype(BF)
    part = dot(mixed_ref[...], w_ref[...])
    half = part_ref.shape[0]

    @pl.when(pl.program_id(0) == 0)
    def _():
        part_ref[...] = part[:half]
        part_other_ref[...] = part[half:]

    @pl.when(pl.program_id(0) > 0)
    def _():
        part_ref[...] += part[:half]
        part_other_ref[...] += part[half:]


def mix_call(local, through, enter, branch_pre, w_out, n_rows, group):
    tokens, width = local.shape
    model = w_out.shape[1]
    return pl.pallas_call(
        functools.partial(mix_kernel, n_rows, group),
        grid=(width // TILE,),
        in_specs=[
            columns(tokens),
            columns(tokens),
            columns(n_rows),
            columns(tokens),
            lines(TILE, model),
        ],
        out_specs=[columns(tokens), columns(tokens)] + [full((tokens // 2, model))] * 2,
        out_shape=[
            in_hbm((tokens, width), F32),
            in_hbm((tokens, width), BF),
            shape_of((tokens // 2, model), F32),
            in_hbm((tokens // 2, model), F32),
        ],
        compiler_params=params(58),
        cost_estimate=LIGHT,
        name="mix",
    )(local, through, enter, branch_pre, w_out)


def ffn_kernel(
    sizes,
    rows,
    n_gate,
    n_up,
    at_ref,
    mine_ref,
    other_ref,
    low_mine_ref,
    low_other_ref,
    *refs,
):
    wg_refs, wu_refs, refs = refs[:n_gate], refs[n_gate : n_gate + n_up], refs[n_gate + n_up :]
    wd_ref, gg_send_ref, gg_ref, gu_send_ref, gu_ref, gd_ref, gd_other_ref = refs[:7]
    part_ref, part_other_ref, back_ref, back_other_ref = refs[7:11]
    second_ref, low_ref, left_ref, right_ref, gate_ref, up_ref, down_ref = refs[11:]
    step = pl.program_id(0)
    half = mine_ref.shape[0]

    @pl.when(step == 0)
    def _():
        second_ref[0:half] = mine_ref[...]
        second_ref[half:] = other_ref[...]
        low_ref[0:half] = low_mine_ref[...]
        low_ref[half:] = low_other_ref[...]
        turn_rows("xyz", sizes, at_ref, second_ref[...], rows, left_ref)
        turn_rows("yxz", sizes, at_ref, second_ref[...], rows, right_ref)

    second, low = second_ref[...], low_ref[...]
    w_gate = from_pieces(at_ref[2], 2, wg_refs, gate_ref)
    w_up = from_pieces(at_ref[1], 1, wu_refs, up_ref)
    gate = dot(second, w_gate)
    up = dot(second, w_up)
    grad = dot_nt(low, wd_ref[...])
    active, slope = gelu_parts(gate)
    hidden = (active * up).astype(BF)
    gate_low = (grad * up * slope).astype(BF)
    up_low = (grad * active).astype(BF)
    sent = gg_send_ref.shape[0]
    gg = dot(left_ref[...], gate_low).astype(BF)
    gg_send_ref[...] = gg[:sent]
    gg_ref[...] = gg[sent:]
    sent = gu_send_ref.shape[0]
    gu = dot(right_ref[...], up_low).astype(BF)
    gu_send_ref[...] = gu[:sent]
    gu_ref[...] = gu[sent:]
    width = hidden.shape[1]
    down_ref[pl.ds(step * width, width)] = dot_tn(hidden, low).astype(BF)
    part = dot(hidden, wd_ref[...])
    back = dot_nt(gate_low, w_gate) + dot_nt(up_low, w_up)

    @pl.when(step == 0)
    def _():
        part_ref[...] = part[:half]
        part_other_ref[...] = part[half:]
        back_ref[...] = back[:half]
        back_other_ref[...] = back[half:]

    @pl.when(step > 0)
    def _():
        part_ref[...] += part[:half]
        part_other_ref[...] += part[half:]
        back_ref[...] += back[:half]
        back_other_ref[...] += back[half:]

    pairs, lines_down, _ = gd_ref.shape
    for k in range(2):

        @pl.when((step == pl.num_programs(0) - 1) & (at_ref[3] == k))
        def _():
            for q in range(pairs):
                at = 2 * q * lines_down
                near, far = at + k * lines_down, at + (1 - k) * lines_down
                gd_ref[q] = down_ref[near : near + lines_down]
                gd_other_ref[q] = down_ref[far : far + lines_down]


def ffn_call(place, mine, other, low_mine, low_other, w_gate, w_up, w_down, chip_d, f_rows):
    tokens, model = 2 * mine.shape[0], mine.shape[1]
    width = w_gate[0].shape[-1]
    tile = 2 * TILE
    sent_l, sent_r = model // place.size["x"], model // place.size["y"]
    down = (width // (2 * f_rows), f_rows, model)
    rows = [sent_l, model - sent_l, sent_r, model - sent_r]
    return pl.pallas_call(
        functools.partial(ffn_kernel, place.sizes, chip_d, len(w_gate), len(w_up)),
        grid=(width // tile,),
        in_specs=[
            pl.BlockSpec(memory_space=pltpu.SMEM),
            full((tokens // 2, model)),
            full((tokens // 2, model)),
            full((tokens // 2, model)),
            full((tokens // 2, model)),
            *piece_specs(w_gate, chip_d, tile),
            *piece_specs(w_up, chip_d, tile),
            lines(tile, model),
        ],
        out_specs=[columns(n, tile) for n in rows]
        + [full(down)] * 2
        + [full((tokens // 2, model))] * 4,
        out_shape=[in_hbm((n, width), BF) for n in rows]
        + [shape_of(down, BF), in_hbm(down, BF)]
        + [shape_of((tokens // 2, model), F32), in_hbm((tokens // 2, model), F32)] * 2,
        scratch_shapes=[
            pltpu.VMEM((tokens, model), BF),
            pltpu.VMEM((tokens, model), BF),
            pltpu.VMEM((model, tokens), BF),
            pltpu.VMEM((model, tokens), BF),
            piece_scratch(place, w_gate, chip_d, tile),
            piece_scratch(place, w_up, chip_d, tile),
            pltpu.VMEM((width, model), BF),
        ],
        compiler_params=params(60),
        cost_estimate=LIGHT,
        name="feed_forward",
    )(place.where, mine, other, low_mine, low_other, *w_gate, *w_up, w_down)


def split_kernel(cuts, at_ref, whole_ref, *outs):
    for out, (low, high) in zip(outs, cuts):
        out[...] = whole_ref[:, low:high]


def split_call(place, whole, cuts):
    count, rows, width = whole.shape
    steps = 4
    step = count // (2 * steps)
    if any(n % 16 for cut in cuts for n in cut):
        half = lax.dynamic_slice_in_dim(whole, place.at["c"] * (count // 2), count // 2, 0)
        return [half[:, low:high].reshape(-1, width) for low, high in cuts]
    outs = pl.pallas_call(
        functools.partial(split_kernel, cuts),
        grid_spec=pltpu.PrefetchScalarGridSpec(
            num_scalar_prefetch=1,
            grid=(steps,),
            in_specs=[pl.BlockSpec((step, rows, width), lambda j, at: (at[3] * steps + j, 0, 0))],
            out_specs=[
                pl.BlockSpec((step, high - low, width), lambda j, at: (j, 0, 0))
                for low, high in cuts
            ],
        ),
        out_shape=[in_hbm((count // 2, high - low, width), BF) for low, high in cuts],
        compiler_params=params(58),
        cost_estimate=LIGHT,
        name="split",
    )(place.where, whole)
    return [out.reshape(-1, width) for out in outs]


def regroup_kernel(sizes, order_of, cuts, at_ref, mine_ref, got_ref, *outs):
    nz, ny, nx = sizes
    size = {"z": nz, "y": ny, "x": nx}
    spot = {"z": at_ref[0], "y": at_ref[1], "x": at_ref[2]}
    half = mine_ref.shape[0]
    for index, order in enumerate(order_of):
        send_ref, rest_ref = outs[2 * index], outs[2 * index + 1]
        span = slice(*cuts[index])
        for i0 in range(size[order[0]]):
            for i1 in range(size[order[1]]):
                for i2 in range(size[order[2]]):
                    place = {}
                    for axis, i in zip(order, (i0, i1, i2)):
                        n = size[axis]
                        place[axis] = lax.rem(spot[axis] + (n - 1 - i), n)
                    chip = (place["z"] * ny + place["y"]) * nx + place["x"]
                    here = lax.rem(chip, half)
                    own = lax.div(chip, half) == at_ref[3]
                    value = jnp.where(own, mine_ref[here][:, span], got_ref[here][:, span])
                    if i0 == 0:
                        send_ref[i1, i2] = value
                    else:
                        rest_ref[i0 - 1, i1, i2] = value


def regroup_call(place, mine, got, order_of, cuts):
    sizes = tuple(place.size[a] for a in "zyx")
    rows = mine.shape[1]
    shapes = []
    for order, (low, high) in zip(order_of, cuts):
        n0, n1, n2 = (place.size[a] for a in order)
        shapes.append((n1, n2, rows, high - low))
        shapes.append((n0 - 1, n1, n2, rows, high - low))
    whole = pl.BlockSpec(memory_space=pltpu.VMEM)
    outs = pl.pallas_call(
        functools.partial(regroup_kernel, sizes, order_of, cuts),
        in_specs=[pl.BlockSpec(memory_space=pltpu.SMEM), whole, whole],
        out_specs=[whole] * len(shapes),
        out_shape=[shape_of(shape, BF) for shape in shapes],
        compiler_params=params(24),
        cost_estimate=LIGHT,
        name="regroup",
    )(place.where, mine, got)
    return [
        [outs[2 * i]] + [outs[2 * i + 1][j] for j in range(shapes[2 * i + 1][0])]
        for i in range(len(order_of))
    ]


def decay_of(rpre, vec7, reset):
    recur = jax.nn.sigmoid(rpre)
    rate = vec7 * recur
    return recur, rate, jnp.exp(-rate) * (1.0 - reset)


def back_kernel(
    n_rows,
    group,
    mine_ref,
    other_ref,
    w_ref,
    bpre_ref,
    state_ref,
    rpre_ref,
    mixed_ref,
    vec_ref,
    mask_ref,
    right_ref,
    go_ref,
    gb_send_ref,
    gb_ref,
    gbl_ref,
    reach_ref,
    local_ref,
    ends_ref,
    low_ref,
    grad_ref,
):
    @pl.when(pl.program_id(0) == 0)
    def _():
        half = mine_ref.shape[0]
        low_ref[0:half] = mine_ref[...]
        low_ref[half:] = other_ref[...]

    low = low_ref[...]
    grad_ref[...] = dot_nt(low, w_ref[...])
    go_ref[...] = dot_tn(mixed_ref[...], low).astype(BF)
    half = w_ref.shape[0] // 2
    for h in range(2):
        cols = slice(h * half, (h + 1) * half)
        for r in range(n_rows):
            span = slice(r * group, (r + 1) * group)
            branch, slope = gelu_parts(bpre_ref[span, cols])
            grad = grad_ref[span, cols]
            gbl_ref[span, cols] = (grad * state_ref[span, cols] * slope).astype(BF)
            _, _, decay = decay_of(rpre_ref[span, cols], vec_ref[7:8, cols], mask_ref[span, 0:1])
            ahead = moved(decay, -1, 1.0)
            reach, local = scan_tile(ahead, grad * branch, -1)
            reach_ref[span, cols] = reach
            local_ref[span, cols] = local
            ends_ref[r : r + 1, cols] = decay[0:1] * reach[0:1]
            ends_ref[n_rows + r : n_rows + r + 1, cols] = decay[0:1] * local[0:1]
    sent = gb_send_ref.shape[0]
    gb = dot(right_ref[:, 0 : gbl_ref.shape[0]], gbl_ref[...]).astype(BF)
    gb_send_ref[...] = gb[:sent]
    gb_ref[...] = gb[sent:]


def back_call(place, mine, other, w_out, branch_pre, state, rpre, mixed, vec, masks, right, n_rows, group):
    model, length = right.shape
    tokens = state.shape[0]
    sent = model // place.size["y"]
    width = w_out.shape[0]
    return pl.pallas_call(
        functools.partial(back_kernel, n_rows, group),
        grid=(width // TILE,),
        in_specs=[
            full((tokens // 2, model)),
            full((tokens // 2, model)),
            lines(TILE, model),
            columns(tokens),
            columns(tokens),
            columns(tokens),
            columns(tokens),
            columns(16),
            full(masks.shape),
            full((model, length)),
        ],
        out_specs=[
            lines(TILE, model),
            columns(sent),
            columns(model - sent),
            columns(tokens),
            columns(tokens),
            columns(tokens),
            columns(2 * n_rows),
        ],
        out_shape=[
            shape_of((width, model), BF),
            in_hbm((sent, width), BF),
            in_hbm((model - sent, width), BF),
            shape_of((tokens, width), BF),
            shape_of((tokens, width), F32),
            shape_of((tokens, width), F32),
            shape_of((2 * n_rows, width), F32),
        ],
        scratch_shapes=[pltpu.VMEM((tokens, model), BF), pltpu.VMEM((tokens, TILE), F32)],
        compiler_params=params(32),
        cost_estimate=LIGHT,
        name="recurrence_back",
    )(mine, other, w_out, branch_pre, state, rpre, mixed, vec, masks, right)


def gates_kernel(
    n_rows,
    group,
    block,
    reach_ref,
    local_ref,
    leave_ref,
    state_ref,
    enter_ref,
    rpre_ref,
    ipre_ref,
    conv_ref,
    mixer_ref,
    vec_ref,
    mask_ref,
    gr_ref,
    gi_ref,
    left_ref,
    gin_send_ref,
    gin_ref,
    ggr_ref,
    ggi_ref,
    gvec_ref,
    gm_ref,
    rlow_ref,
    ilow_ref,
    gconv_ref,
    ext_ref,
    spread_ref,
):
    tokens = n_rows * group

    gvec_ref[...] = jnp.zeros_like(gvec_ref)
    for h in range(conv_ref.shape[1] // block):
        cols = slice(h * block, (h + 1) * block)
        for r in range(n_rows):
            span = slice(r * group, (r + 1) * group)
            adjoint = local_ref[span, cols] + reach_ref[span, cols] * leave_ref[r : r + 1, cols]
            state = state_ref[span, cols]
            at = lax.broadcasted_iota(jnp.int32, state.shape, 0)
            before = jnp.where(at == 0, enter_ref[r : r + 1, cols], pltpu.roll(state, 1, 0))
            reset = mask_ref[span, 0:1]
            live = 1.0 - reset
            recur, rate, decay = decay_of(rpre_ref[span, cols], vec_ref[7:8, cols], reset)
            admit = jax.nn.sigmoid(ipre_ref[span, cols])
            full_decay = jnp.exp(-rate)
            root = jnp.sqrt(one_less_exp(2.0 * rate))
            scale = jnp.where(reset > 0.5, 1.0, root)
            conv = conv_ref[span, cols].astype(F32)
            direct = adjoint * scale
            gadmit = direct * conv
            gconv_ref[span, cols] = direct * admit
            gscale = adjoint * admit * conv
            glog = live * full_decay * (adjoint * before - gscale * full_decay / root)
            gvec_ref[7:8, cols] += jnp.sum(glog * recur, axis=0, keepdims=True)
            grecur = -(vec_ref[7:8, cols] * glog) * recur * (1.0 - recur)
            ginput = gadmit * admit * (1.0 - admit)
            rlow, ilow = grecur.astype(BF), ginput.astype(BF)
            rlow_ref[span, cols] = rlow
            ilow_ref[span, cols] = ilow
            gvec_ref[5:6, cols] += jnp.sum(rlow.astype(F32), axis=0, keepdims=True)
            gvec_ref[6:7, cols] += jnp.sum(ilow.astype(F32), axis=0, keepdims=True)
        rlow, ilow = rlow_ref[:, cols], ilow_ref[:, cols]
        low = conv_ref[:, cols]
        ggr_ref[cols] = dot_tn(low, rlow)
        ggi_ref[cols] = dot_tn(low, ilow)
        gconv_ref[:, cols] += dot_nt(rlow, gr_ref[cols]) + dot_nt(ilow, gi_ref[cols])
        for r in range(n_rows):
            span = slice(r * group, (r + 1) * group)
            head = slice(tokens + HALO * r, tokens + HALO * (r + 1))
            ext_ref[0:HALO] = mixer_ref[head, cols].astype(F32)
            ext_ref[HALO : HALO + group] = mixer_ref[span, cols].astype(F32)
            gconv = gconv_ref[span, cols]
            gvec_ref[4:5, cols] += jnp.sum(gconv, axis=0, keepdims=True)
            gvec_ref[0:1, cols] += jnp.sum(
                gconv * ext_ref[HALO : HALO + group], axis=0, keepdims=True
            )
            spread_ref[0:HALO] = jnp.zeros((HALO, block), F32)
            spread_ref[HALO : HALO + group] = vec_ref[0:1, cols] * gconv
            for k in range(1, 4):
                masked = gconv * mask_ref[span, k : k + 1]
                there = slice(HALO - k, HALO - k + group)
                gvec_ref[k : k + 1, cols] += jnp.sum(
                    masked * ext_ref[there], axis=0, keepdims=True
                )
                spread_ref[there] += vec_ref[k : k + 1, cols] * masked
            gm_ref[head, cols] = spread_ref[0:HALO].astype(BF)
            gm_ref[span, cols] = spread_ref[HALO : HALO + group].astype(BF)
    gm = gm_ref[...]
    sent = gin_send_ref.shape[0]
    gin = dot(left_ref[...], gm).astype(BF)
    gin_send_ref[...] = gin[:sent]
    gin_ref[...] = gin[sent:]


def first_kernel(gm_ref, gbl_ref, win_ref, wbr_ref, gfirst_ref):
    step = pl.program_id(0)
    tokens = gbl_ref.shape[0]
    gm = gm_ref[...]
    part = dot_nt(gm, win_ref[...])
    part_branch = dot_nt(gbl_ref[...], wbr_ref[...])

    @pl.when(step == 0)
    def _():
        gfirst_ref[...] = part

    @pl.when(step > 0)
    def _():
        gfirst_ref[...] += part

    gfirst_ref[0:tokens] += part_branch


def gates_call(
    place, reach, local, leave, state, enter, rpre, ipre, conv, mixer, vec, masks, gate_r, gate_i, left, n_rows, group
):
    model, length = left.shape
    sent = model // place.size["x"]
    tokens, width = state.shape
    block = gate_r.shape[1]
    tile = TILE
    return pl.pallas_call(
        functools.partial(gates_kernel, n_rows, group, block),
        grid=(width // tile,),
        in_specs=[
            columns(tokens),
            columns(tokens),
            columns(n_rows),
            columns(tokens),
            columns(n_rows),
            columns(tokens),
            columns(tokens),
            columns(tokens),
            columns(length),
            columns(16),
            full(masks.shape),
            lines(tile, block),
            lines(tile, block),
            full((model, length)),
        ],
        out_specs=[
            columns(sent),
            columns(model - sent),
            lines(tile, block),
            lines(tile, block),
            columns(8),
            columns(length),
        ],
        out_shape=[
            in_hbm((sent, width), BF),
            in_hbm((model - sent, width), BF),
            shape_of((width, block), F32),
            shape_of((width, block), F32),
            shape_of((8, width), F32),
            in_hbm((length, width), BF),
        ],
        scratch_shapes=[
            pltpu.VMEM((tokens, tile), BF),
            pltpu.VMEM((tokens, tile), BF),
            pltpu.VMEM((tokens, tile), F32),
            pltpu.VMEM((HALO + group, block), F32),
            pltpu.VMEM((HALO + group, block), F32),
        ],
        compiler_params=params(40),
        cost_estimate=LIGHT,
        name="recurrence_gates",
    )(reach, local, leave, state, enter, rpre, ipre, conv, mixer, vec, masks, gate_r, gate_i, left)


def first_call(gm, gbl, w_in, w_branch):
    length, width = gm.shape
    model = w_in.shape[0]
    return pl.pallas_call(
        first_kernel,
        grid=(width // TILE,),
        in_specs=[columns(length), columns(gbl.shape[0]), columns(model), columns(model)],
        out_specs=full((length, model)),
        out_shape=shape_of((length, model), F32),
        compiler_params=params(24),
        cost_estimate=LIGHT,
        name="first_gradient",
    )(gm, gbl, w_in, w_branch)


def normed(values, gain):
    return values * lax.rsqrt(jnp.mean(values * values, axis=-1, keepdims=True) + EPS) * gain


def halves(value, place, dim):
    half = value.shape[dim] // 2
    mine = lax.dynamic_slice_in_dim(value, place.at["c"] * half, half, dim)
    other = lax.dynamic_slice_in_dim(value, (1 - place.at["c"]) * half, half, dim)
    return mine, other


def own_channels(place, value):
    mine, other = halves(value, place, 0)
    got = place.ring(other, "c", 1)
    pair = place.ordered(mine, got)
    both = jnp.stack(pair, axis=1)
    return both.reshape(-1, both.shape[-1])


def own_devices(place, value, rows):
    shaped = value.reshape(place.chips // 2, 2, rows, value.shape[-1])
    mine = lax.dynamic_index_in_dim(shaped, place.at["c"], 1, keepdims=False)
    other = lax.dynamic_index_in_dim(shaped, 1 - place.at["c"], 1, keepdims=False)
    got = place.ring(other, "c", 1)
    return jnp.concatenate(place.ordered(mine, got), axis=0)


def on_device(
    inputs,
    cotangent,
    segments,
    norm1_gain,
    input_proj,
    branch_proj,
    conv_weight,
    conv_bias,
    recur_gate,
    input_gate,
    recur_bias,
    input_bias,
    decay_param,
    output_proj,
    norm2_gain,
    mlp_gate,
    mlp_up,
    mlp_down,
):
    place = Place()
    core = place.at["c"]
    chips = place.chips
    rows_dev, group, model = inputs.shape
    n_rows = 2 * rows_dev
    tokens_dev = rows_dev * group
    tokens = 2 * tokens_dev
    d_rows, lru = input_proj.shape
    ffn = mlp_gate.shape[1]
    r_rows, block = recur_gate.shape
    f_rows = mlp_down.shape[0]
    lru_half, ffn_half = lru // 2, ffn // 2
    pair = lambda value: place.ring(value, "c", 1)

    order = Order(place)
    lead = (place.size["z"], place.size["y"], place.size["x"])

    wide = [halves(w, place, 1) for w in (input_proj, branch_proj, mlp_gate, mlp_up)]
    got_a = order.ring(jnp.concatenate([w[1] for w in wide[:2]], axis=1), "c")
    got_c = order.ring(jnp.concatenate([w[1] for w in wide[2:]], axis=1), "c")
    span = max(d_rows, r_rows)
    lines_one = [
        jnp.pad(v, (0, span - v.shape[0]))[None]
        for v in (norm1_gain, norm2_gain, conv_bias, recur_bias, input_bias, decay_param)
    ]
    taps = jnp.pad(conv_weight, ((0, 0), (0, span - r_rows)))
    vectors = jnp.concatenate(lines_one[:2] + [taps] + lines_one[2:], axis=0)
    small = Gather(order, vectors[None, None, None, None], "y", 1)
    ids_pair = order.ring(segments, "c")
    mine_a = jnp.concatenate([w[0] for w in wide[:2]], axis=1)
    mine_c = jnp.concatenate([w[0] for w in wide[2:]], axis=1)
    gates = jnp.concatenate([recur_gate, input_gate], axis=0)
    gate_lines = 2 * r_rows * block // lru
    gates = gates.reshape(-1, gate_lines, block).transpose(1, 0, 2).reshape(gate_lines, lru)
    order.must(gates, mine_a)
    small = Gather(order, small.done(), "x", 2)
    got_a = order.wait(got_a)
    rows_a = jnp.concatenate(place.ordered(mine_a, got_a), axis=0)
    group_a = jnp.concatenate([rows_a, gates], axis=0)[None, None, None]
    order.must(group_a)
    both_whole = jnp.concatenate([output_proj, mlp_down], axis=0)
    both_whole = lax.all_gather(both_whole, AXES, axis=0)
    small = Gather(order, small.done(), "c", 3)
    small = Gather(order, small.done(), "z", 0, direct=True)

    a_z = Gather(order, group_a, "z", 0, direct=True)
    grad_out = cotangent.reshape(tokens_dev, model)
    low = grad_out.astype(BF)
    low_other = order.ring(low, "c")
    ids_pair, got_c = order.wait(ids_pair, got_c)
    ids = jnp.concatenate([segments, ids_pair], axis=0)
    prior_ids = order.along(ids[:, group - 3 :], 1)
    gains, vec = small_call(
        place, small.done().reshape(2 * chips, -1, span), d_rows, r_rows
    )
    flat = inputs.reshape(tokens_dev, model)
    (first,) = norm_call([flat], gains, 0)
    first_other = order.ring(first, "c")
    group_c = jnp.concatenate(place.ordered(mine_c, got_c), axis=0)[None, None, None]
    first_other, low_other = order.wait(first_other, low_other)
    tail = jnp.concatenate(
        [v.reshape(rows_dev, group, model)[:, group - 3 :] for v in (first, first_other)], axis=0
    )
    halo = order.along(tail, 1)
    c_z = Gather(order, group_c, "z", 0, both=True)
    a_z = a_z.done()
    halo, prior_ids = order.wait(halo, prior_ids)

    a_left = Gather(order, a_z[..., :lru_half], "y", 1)
    a_right = Gather(order, a_z[..., lru_half:], "x", 2)
    a_left, a_right = a_left.done(), a_right.done()

    a_left = Gather(order, a_left, "x", 2)
    a_right = Gather(order, a_right, "y", 1)
    c_z.next()
    a_left.arrived()
    a_right.arrived()

    chip_d = 2 * d_rows
    packed = [g.whole([p[..., chip_d:, :] for p in g.pieces]) for g in (a_left, a_right)]
    packed = jnp.concatenate(packed, axis=-1)
    packed = packed.reshape(chips, gate_lines, -1, block)
    packed = packed.transpose(0, 2, 1, 3).reshape(chips, 2, r_rows, block)
    packed = jnp.concatenate([packed[:, 0], packed[:, 1]], axis=-1)
    gate_mine, gate_other = halves(packed, place, 0)
    gate_got = order.ring(gate_other, "c")
    c_z = c_z.done()
    c_left = Gather(order, c_z[..., :ffn_half], "y", 1)
    c_right = Gather(order, c_z[..., ffn_half:], "x", 2)
    halo = jnp.pad(halo, ((0, 0), (HALO - 3, 0), (0, 0))).reshape(n_rows * HALO, model)
    position = place.s * group + jnp.arange(group, dtype=jnp.int32)
    joined_ids = jnp.concatenate([prior_ids, ids], axis=1)
    marks = [(joined_ids[:, 2 : 2 + group] != ids) | (position == 0)[None, :]]
    for k in range(1, 4):
        marks.append(
            (joined_ids[:, 3 - k : 3 - k + group] == ids) & (position >= k)[None, :]
        )
    masks = jnp.stack(marks, axis=-1).astype(F32).reshape(tokens, 4)
    masks = jnp.pad(masks, ((0, 0), (0, 4)))
    gate_got = order.wait(gate_got)
    packed = jnp.stack(place.ordered(gate_mine, gate_got), axis=1).reshape(-1, 2 * block)
    gate_r, gate_i = packed[:, :block], packed[:, block:]
    first_ext, branch_pre, mixer, conv, rpre, ipre, through, local, ends, w_in, w_branch = forward_call(
        place, first, first_other, halo, a_left.weight(chip_d), a_right.weight(chip_d), vec, masks, gate_r, gate_i, n_rows, group, chip_d
    )
    enter = Carry(order, ends, 1)
    more = enter.next()
    c_left, c_right = c_left.done(), c_right.done()

    c_left = Gather(order, c_left, "x", 2)
    c_right = Gather(order, c_right, "y", 1)
    both_whole = order.wait(both_whole)
    w_out, w_down = split_call(
        place, both_whole, ((0, r_rows), (r_rows, r_rows + f_rows))
    )
    order.must(w_out, w_down)
    enter = enter.done() if more else enter.total[4:]
    state, mixed, part, part_other = mix_call(
        local, through, enter, branch_pre, w_out, n_rows, group
    )
    part_pair = order.ring(part_other, "c")
    first_l, first_r = turn_call(place, order.tie(first_ext), chip_d)
    order.must(first_l, first_r)
    w_gate, w_up = c_left.weight(chip_d), c_right.weight(chip_d)
    part_pair = order.wait(part_pair)
    second, middle = norm_call([flat, part, part_pair], gains, 1)
    second_other = order.ring(second, "c")
    second_other = order.wait(second_other)

    nz, ny, nx = lead

    def blocks_of(send, rest, axis, other):
        shape = (place.size[other], nz, chip_d, -1)
        rest = rest.reshape((place.size[axis] - 1,) + shape)
        return [send.reshape(shape)] + [rest[i] for i in range(rest.shape[0])]

    def joined(left, right):
        return [jnp.concatenate(p, axis=-1) for p in zip(left.done(nz), right.done(nz))]

    g_send, g_rest, u_send, u_rest, down_mine, down_other, part, part_other, back, back_other = ffn_call(
        place, second, second_other, low, low_other, w_gate, w_up, w_down, chip_d, f_rows
    )

    back_pair = order.ring(back_other, "c")
    g_left = Scatter(order, blocks_of(g_send, g_rest, "x", "y"), "x")
    g_right = Scatter(order, blocks_of(u_send, u_rest, "y", "x"), "y")
    down_got = order.ring(down_other, "c")
    back_pair = order.wait(back_pair)
    grad_middle, mid_low, grad_gain_two = norm_back_call(
        [back, back_pair], middle, gains, 1, grad_out, 1
    )
    mid_pair = order.ring(mid_low, "c")
    down_got = order.wait(down_got)
    (d_z,) = regroup_call(place, down_mine, down_got, ("zyx",), ((0, model),))
    d_z = Scatter(order, d_z, "z")
    mid_other = order.wait(mid_pair)
    g_out, b_send, b_rest, gbl, reach, local_back, ends_back = back_call(
        place, mid_low, mid_other, w_out, branch_pre, state, rpre, mixed, vec, masks, first_r, n_rows, group
    )
    d_z.take()
    leave = Carry(order, ends_back, -1)
    g_left.next()
    g_right.next()
    more = leave.next()

    g_left = Scatter(order, g_left.done(ny), "y")
    g_right = Scatter(order, g_right.done(nx), "x")
    leave = leave.done() if more else leave.total[4:]
    d_z.next()
    in_send, in_rest, g_gate_r, g_gate_i, g_vec, gm = gates_call(
        place, reach, local_back, leave, state, enter, rpre, ipre, conv, mixer, vec, masks, gate_r, gate_i, first_l, n_rows, group
    )
    order.must(in_send)
    g_left.next()
    g_right.next()

    a_left = Scatter(order, blocks_of(in_send, in_rest, "x", "y"), "x")
    a_right = Scatter(order, blocks_of(b_send, b_rest, "y", "x"), "y")
    d_z.take()
    out_mine, out_other = pack_call(place, g_out, g_gate_r, g_gate_i, g_vec, vec, r_rows)
    out_got = order.ring(out_other, "c")
    out_got = order.wait(out_got)
    wide_r = out_mine.shape[-1]
    cut = (wide_r // (2 * block)) * block
    o_left, o_right = regroup_call(
        place, out_mine, out_got, ("xyz", "yxz"), ((0, cut), (cut, wide_r))
    )
    d_z.next()
    grad_first = first_call(order.tie(gm), gbl, w_in, w_branch)
    order.must(grad_first)
    g_both = Scatter(order, joined(g_left, g_right), "z")
    order.must(o_left[0], o_right[0])
    a_left.next()
    a_right.next()

    a_left = Scatter(order, a_left.done(ny), "y")
    a_right = Scatter(order, a_right.done(nx), "x")
    o_left = Scatter(order, o_left, "x")
    o_right = Scatter(order, o_right, "y")
    d_z.take()
    g_both.next()
    spill = grad_first[tokens:].reshape(n_rows, HALO, model)[:, HALO - 3 :]
    spill = order.along(spill, -1)
    a_left.next()
    a_right.next()
    o_left.next()
    o_right.next()

    a_both = Scatter(order, joined(a_left, a_right), "z", both=True)
    o_left = Scatter(order, o_left.done(ny), "y")
    o_right = Scatter(order, o_right.done(nx), "x")
    spill = order.wait(spill)
    spill = jnp.pad(spill, ((0, 0), (group - 3, 0), (0, 0))).reshape(tokens, model)
    grad_first = grad_first[:tokens] + spill
    first_pair = order.ring(grad_first[tokens_dev:], "c")
    first_pair = order.wait(first_pair)
    grad_inputs, grad_gain_one = norm_back_call(
        [grad_first[:tokens_dev], first_pair], flat, gains, 0, grad_middle, 0
    )
    order.must(grad_inputs)
    g_both.next()
    d_x = Scatter(order, d_z.done(ny), "y")
    a_both.next()
    o_left.next()
    o_right.next()
    d_x.next()

    o_both = Scatter(order, joined(o_left, o_right), "z", both=True)
    d_y = Scatter(order, d_x.done(nx), "x")
    g_gains = jnp.concatenate([grad_gain_one, grad_gain_two], axis=0)
    g_gains = jnp.transpose(g_gains.reshape(2, chips, 2, d_rows), (1, 2, 0, 3))
    g_gains = g_gains.reshape(lead + (2, 2 * d_rows))
    g_gains = jnp.moveaxis(behind(place, "yxz", g_gains), 3, 0)
    gains_mine = lax.dynamic_index_in_dim(g_gains, core, 0, False)
    gains_got = order.ring(lax.dynamic_index_in_dim(g_gains, 1 - core, 0, False), "c")
    part_pair = order.ring(part_other, "c")

    def whole_columns(value):
        mine, other = halves(value, place, 0)
        return mine, order.ring(other, "c")

    gains_got, part_pair = order.wait(gains_got, part_pair)
    result = middle + (part + part_pair)
    order.must(result)
    g_gains = gains_mine + gains_got
    g_gains = Scatter(order, [g_gains[i] for i in range(ny)], "y", between=F32)
    a_both.next()
    sum_c = whole_columns(g_both.done(dtype=F32))
    g_gains = Scatter(order, g_gains.done(nx, F32), "x", between=F32)
    o_both.next()
    sum_down = d_y.done(dtype=F32)
    order.must(sum_down)
    g_gains = Scatter(order, g_gains.done(nz, F32), "z", direct=True, between=F32)
    low_c, high_c = place.ordered(sum_c[0], order.wait(sum_c[1]))
    grad_gate = jnp.concatenate([low_c[:, :ffn_half], high_c[:, :ffn_half]], axis=1)
    grad_up = jnp.concatenate([low_c[:, ffn_half:], high_c[:, ffn_half:]], axis=1)
    order.must(grad_gate, grad_up)
    sum_a = whole_columns(a_both.done(dtype=F32))
    o_both.next()
    low_a, high_a = place.ordered(sum_a[0], order.wait(sum_a[1]))
    grad_input_proj = jnp.concatenate([low_a[:, :lru_half], high_a[:, :lru_half]], axis=1)
    grad_branch_proj = jnp.concatenate([low_a[:, lru_half:], high_a[:, lru_half:]], axis=1)
    order.must(grad_input_proj, grad_branch_proj)
    own = o_both.done(dtype=F32)
    g_gains = g_gains.done(dtype=F32).reshape(2, d_rows)
    own_gates = own[:, model : model + 2 * block]
    own_vec = own[:, model + 2 * block : model + 2 * block + 8].T
    return (
        result.reshape(inputs.shape),
        grad_inputs.reshape(inputs.shape),
        g_gains[0],
        grad_input_proj,
        grad_branch_proj,
        own_vec[:4],
        own_vec[4],
        own_gates[:, :block],
        own_gates[:, block:],
        own_vec[5],
        own_vec[6],
        own_vec[7],
        own[:, :model],
        g_gains[1],
        grad_gate,
        grad_up,
        sum_down,
    )


def solution(mesh):
    seq, row = mesh.shape["seq"], mesh.shape["row"]
    ny = 1 << ((seq.bit_length() - 1) // 2)
    grid = Mesh(mesh.devices.reshape(seq // ny, ny, row // 2, 2), AXES)
    tokens, line, flat, taps = P(("x", "c"), ("z", "y"), None), P(AXES, None), P(AXES), P(None, AXES)
    in_specs = (
        tokens,
        tokens,
        P(("x", "c"), ("z", "y")),
        flat,
        line,
        line,
        taps,
        flat,
        line,
        line,
        flat,
        flat,
        flat,
        line,
        flat,
        line,
        line,
        line,
    )
    out_specs = (
        tokens,
        tokens,
        flat,
        line,
        line,
        taps,
        flat,
        line,
        line,
        flat,
        flat,
        flat,
        line,
        flat,
        line,
        line,
        line,
    )
    return jax.shard_map(
        on_device, mesh=grid, in_specs=in_specs, out_specs=out_specs, check_vma=False
    )
```

```python
import functools
import math

import jax
import jax.numpy as jnp
import numpy as np
from jax import lax
from jax.experimental import pallas as pl
from jax.experimental.pallas import tpu as pltpu
from jax.sharding import Mesh, PartitionSpec as P

EPS = 1e-06
BF = jnp.bfloat16
F32 = jnp.float32
AXES = ("z", "y", "x", "c")
MIB = 1 << 20
TILE = 256
HALO = 8
GELU_C = math.sqrt(2.0 / math.pi)


class Place:
    def __init__(self):
        self.size = {axis: lax.axis_size(axis) for axis in AXES}
        self.at = {axis: lax.axis_index(axis) for axis in AXES}
        nz, ny, nx, _ = self.size.values()
        self.seq, self.row = nz * ny, nx * 2
        self.s = self.at["z"] * ny + self.at["y"]
        self.stride = {"z": ny * self.row, "y": self.row, "x": 2, "c": 1}
        self.chips = nz * ny * nx
        self.sizes = (nz, ny, nx)
        self.where = jnp.stack([self.at[axis] for axis in AXES]).astype(jnp.int32)


    def ring(self, value, axis, shift):
        pairs = []
        for i in range(self.seq * self.row):
            at = (i // self.stride[axis]) % self.size[axis]
            to = (at + shift) % self.size[axis]
            pairs.append((i, i + (to - at) * self.stride[axis]))
        return lax.ppermute(value, AXES, pairs)

    def along(self, value, distance):
        pairs = []
        for s in range(self.seq):
            if 0 <= s + distance < self.seq:
                for r in range(self.row):
                    pairs.append((s * self.row + r, (s + distance) * self.row + r))
        return lax.ppermute(value, AXES, pairs)

    def ordered(self, mine, other):
        high = self.at["c"] != 0
        return jnp.where(high, other, mine), jnp.where(high, mine, other)


class Order:
    def __init__(self, place):
        self.place = place
        self.last = ()
        self.sent = ()

    def tie(self, value):
        if not self.last:
            return value
        return lax.optimization_barrier((value,) + self.last)[0]

    def must(self, *values):
        self.sent += values

    def ring(self, value, axis, shift=1):
        value = self.tie(value)
        self.sent += (value,)
        return self.place.ring(value, axis, shift)

    def along(self, value, distance):
        value = self.tie(value)
        self.sent += (value,)
        return self.place.along(value, distance)

    def wait(self, *values):
        n = len(values)
        held = values + self.last + self.sent
        if len(held) > n:
            values = lax.optimization_barrier(held)[:n]
        self.last = tuple(values)
        self.sent = ()
        return values[0] if n == 1 else values


class Gather:
    def __init__(self, order, value, axis, dim, direct=False, both=False):
        self.order, self.axis, self.dim = order, axis, dim
        self.n = order.place.size[axis]
        self.pieces = [value]
        self.direct = direct
        self.both = both and self.n == 4
        if self.both:
            self.flying = [order.ring(value, axis, 1), order.ring(value, axis, 3)]
            return
        shifts = range(1, self.n) if direct else range(1, min(2, self.n))
        self.flying = [order.ring(value, axis, k) for k in shifts]

    def next(self):
        if self.direct:
            if self.flying:
                got = self.order.wait(*self.flying)
                self.pieces += [got] if len(self.flying) == 1 else list(got)
            self.flying = []
            return
        if self.both:
            if len(self.flying) == 2:
                one, three = self.order.wait(*self.flying)
                self.pieces += [one, None, three]
                self.flying = [self.order.ring(one, self.axis)]
            elif self.flying:
                self.pieces[2] = self.order.wait(self.flying.pop())
            return
        got = self.order.wait(self.flying.pop())
        self.pieces.append(got)
        if len(self.pieces) < self.n:
            self.flying = [self.order.ring(got, self.axis)]

    def arrived(self):
        while len(self.pieces) < self.n or (self.both and self.flying):
            self.next()
        return self.pieces

    def done(self):
        return self.whole(self.arrived())

    def whole(self, pieces):
        at = self.order.place.at[self.axis]
        if self.n == 2:
            high = at != 0
            mine, other = pieces
            parts = [jnp.where(high, other, mine), jnp.where(high, mine, other)]
            return jnp.concatenate(parts, axis=self.dim)
        parts = [
            lax.select_n(lax.rem(at - j + self.n, self.n), *pieces) for j in range(self.n)
        ]
        return jnp.concatenate(parts, axis=self.dim)

    def weight(self, rows):
        if rows % 16 == 0:
            return self.arrived()
        whole = self.done()[..., :rows, :]
        return [whole.reshape(-1, whole.shape[-1])]


class Scatter:
    def __init__(self, order, blocks, axis, direct=False, between=BF, both=False):
        self.order, self.axis, self.blocks = order, axis, list(blocks)
        self.n = order.place.size[axis]
        self.both = both and self.n == 4
        self.direct, self.between = direct, between
        self.hop = 0
        self.held = False
        if self.both:
            self.flying = [order.ring(self.blocks[1], axis, 3), order.ring(self.blocks[2], axis, 1)]
        elif direct:
            self.flying = [
                order.ring(self.blocks[i], axis, self.n - 1 - i) for i in range(self.n - 1)
            ]
        elif self.n > 1:
            self.flying = order.ring(self.blocks[0], axis)

    def next(self):
        if self.both:
            if self.hop == 0:
                far, near = self.order.wait(*self.flying)
                total = far.astype(F32) + self.blocks[0].astype(F32)
                self.got = [near]
                self.flying = self.order.ring(total.astype(self.between), self.axis, 3)
                self.hop = 1
            elif self.hop == 1:
                self.got.append(self.order.wait(self.flying))
                self.hop = self.n - 1
            return
        if self.direct:
            if self.n > 1:
                got = self.order.wait(*self.flying)
                self.got = [got] if self.n == 2 else list(got)
            self.hop = self.n - 1
            return
        if not self.held:
            self.take()
        self.held = False
        if self.hop < self.n - 1:
            total = self.got[0].astype(F32) + self.blocks[self.hop].astype(F32)
            self.flying = self.order.ring(total.astype(self.between), self.axis)

    def take(self):
        self.got = [self.order.wait(self.flying)]
        self.hop += 1
        self.held = True

    def done(self, parts=0, dtype=BF):
        if self.held:
            self.next()
        while self.hop < self.n - 1:
            self.next()
        terms = [self.blocks[-1]] + (self.got if self.n > 1 else [])

        def total(pick):
            values = [pick(t).astype(F32) for t in terms]
            return functools.reduce(jnp.add, values).astype(dtype)

        if not parts:
            return total(lambda t: t)
        return [total(lambda t, i=i: t[i]) for i in range(parts)]


def behind(place, order_of_axes, value):
    for dim, axis in enumerate(("z", "y", "x")):
        n, at = place.size[axis], place.at[axis]
        picks = [
            lax.dynamic_index_in_dim(value, lax.rem(at - i - 1 + 2 * n, n), dim)
            for i in range(n)
        ]
        value = jnp.concatenate(picks, axis=dim)
    dims = ["zyx".index(axis) for axis in order_of_axes]
    return jnp.transpose(value, tuple(dims) + tuple(range(3, value.ndim)))


def sources(place, order_of_axes, rows):
    lead = tuple(place.size[a] for a in "zyx")
    at = jnp.arange(math.prod(lead) * rows, dtype=jnp.int32).reshape(lead + (rows,))
    return behind(place, order_of_axes, at).reshape(-1)


def compose(earlier, later):
    return jnp.concatenate(
        [earlier[:4] * later[:4], later[:4] * earlier[4:] + later[4:]], axis=0
    )


class Carry:
    def __init__(self, order, end_map, sign, most=3):
        self.order, self.sign, self.most = order, sign, most
        self.n = order.place.seq
        self.unit = jnp.concatenate(
            [jnp.ones_like(end_map[:4]), jnp.zeros_like(end_map[4:])], axis=0
        )
        self.total = None
        self.reach = 0
        self.send(end_map, 1)

    def send(self, value, width):
        self.shifts = []
        distance = max(self.reach, 1)
        while distance < self.n and len(self.shifts) < self.most:
            self.shifts.append(distance)
            distance += width
        self.width = width
        self.flying = [self.order.along(value, self.sign * d) for d in self.shifts]

    def next(self):
        got = self.order.wait(*self.flying)
        got = [got] if len(self.flying) == 1 else list(got)
        s, n = self.order.place.s, self.n
        for value, d in zip(got, self.shifts):
            inside = (s >= d) if self.sign > 0 else (s < n - d)
            part = jnp.where(inside, value, self.unit)
            self.total = part if self.total is None else compose(part, self.total)
        self.reach += self.width * len(self.shifts)
        if self.reach < self.n - 1:
            self.send(self.total, self.reach)
            return True
        return False

    def done(self):
        while self.next():
            pass
        return self.total[4:]


def dot(a, b):
    return jnp.dot(a, b, preferred_element_type=F32)


def dot_nt(a, b):
    return lax.dot_general(a, b, (((1,), (1,)), ((), ())), preferred_element_type=F32)


def dot_tn(a, b):
    return lax.dot_general(a, b, (((0,), (0,)), ((), ())), preferred_element_type=F32)


def moved(value, distance, fill):
    n = value.shape[0]
    size = abs(distance)
    edge = jnp.full((size,) + value.shape[1:], fill, value.dtype)
    if size % 8 == 0:
        if distance > 0:
            return jnp.concatenate([edge, value[: n - size]], axis=0)
        return jnp.concatenate([value[size:], edge], axis=0)
    at = lax.broadcasted_iota(jnp.int32, value.shape, 0)
    turned = pltpu.roll(value, distance % n, 0)
    inside = at >= size if distance > 0 else at < n - size
    return jnp.where(inside, turned, fill)


def scan_tile(decay, drive, sign):
    n = decay.shape[0]
    distance = 1
    while distance < n:
        drive = decay * moved(drive, sign * distance, 0.0) + drive
        decay = decay * moved(decay, sign * distance, 1.0)
        distance *= 2
    return decay, drive


def one_less_exp(u):
    term = jnp.full_like(u, 1.0 / 3628800.0)
    for k in (362880, 40320, 5040, 720, 120, 24, 6, 2):
        term = 1.0 / k - u * term
    small = u * (1.0 - u * term)
    return jnp.where(u < 0.8, small, 1.0 - jnp.exp(-u))


def log2(n):
    return n.bit_length() - 1


def source_rows(order, sizes, at_ref, rows, first, count):
    spot = {"z": at_ref[0], "y": at_ref[1], "x": at_ref[2]}
    size = dict(zip("zyx", sizes))
    line = first + lax.broadcasted_iota(jnp.int32, (count, 1), 0)
    inside = line & (rows - 1)
    line = line >> log2(rows)
    where = {}
    for axis in reversed(order):
        n = size[axis]
        where[axis] = (spot[axis] + (n - 1) - (line & (n - 1))) & (n - 1)
        line = line >> log2(n)
    chip = (where["z"] * size["y"] + where["y"]) * size["x"] + where["x"]
    return chip * rows + inside


def turn_rows(order, sizes, at_ref, value, rows, out_ref):
    total = value.shape[1]
    step = min(total, 256)
    for first in range(0, total, step):
        source = source_rows(order, sizes, at_ref, rows, first, step)
        lane = lax.broadcasted_iota(jnp.int32, (step, total), 1)
        pick = jnp.where(source == lane, 1.0, 0.0).astype(BF)
        out_ref[first : first + step] = dot_nt(pick, value).astype(BF)


def gelu_parts(value):
    square = value * value
    t = jnp.tanh(GELU_C * value * (1.0 + 0.044715 * square))
    half = 0.5 * (1.0 + t)
    slope = half + 0.5 * value * (1.0 - t * t) * GELU_C * (1.0 + 3.0 * 0.044715 * square)
    return value * half, slope


def full(shape):
    return pl.BlockSpec(shape, lambda j: (0,) * len(shape))


def columns(rows, width=TILE):
    return pl.BlockSpec((rows, width), lambda j: (0, j))


def lines(rows, width):
    return pl.BlockSpec((rows, width), lambda j: (j, 0))


def in_hbm(shape, dtype):
    return pltpu.HBM(shape, dtype)


def piece_specs(pieces, rows, tile=TILE):
    if len(pieces) == 1:
        return [columns(pieces[0].shape[0], tile)]
    block = pieces[0].shape[:3] + (rows, tile)
    return [pl.BlockSpec(block, lambda j: (0, 0, 0, 0, j)) for _ in pieces]


def piece_scratch(place, pieces, rows, tile=TILE):
    if len(pieces) == 1:
        return pltpu.VMEM((16, 128), BF)
    return pltpu.VMEM(place.sizes + (rows, tile), BF)


def from_pieces(at, dim, refs, out_ref):
    n = len(refs)
    if n == 1:
        return refs[0][...]
    for k, ref in enumerate(refs):
        where = pl.ds((at - k + n) & (n - 1), 1)
        out_ref[(slice(None),) * dim + (where,)] = ref[...]
    whole = out_ref[...]
    return whole.reshape(-1, whole.shape[-1])


def shape_of(shape, dtype):
    return jax.ShapeDtypeStruct(shape, dtype)


def params(limit):
    return pltpu.CompilerParams(vmem_limit_bytes=limit * MIB)


LIGHT = pl.CostEstimate(flops=1, bytes_accessed=1, transcendentals=0)


def turn_kernel(sizes, rows, at_ref, first_ref, left_ref, right_ref):
    turn_rows("xyz", sizes, at_ref, first_ref[...], rows, left_ref)
    turn_rows("yxz", sizes, at_ref, first_ref[...], rows, right_ref)


def turn_call(place, first, rows):
    length, model = first.shape
    whole = pl.BlockSpec(memory_space=pltpu.VMEM)
    return pl.pallas_call(
        functools.partial(turn_kernel, place.sizes, rows),
        in_specs=[pl.BlockSpec(memory_space=pltpu.SMEM), whole],
        out_specs=[whole] * 2,
        out_shape=[shape_of((model, length), BF)] * 2,
        compiler_params=params(24),
        cost_estimate=LIGHT,
        name="turn",
    )(place.where, first)


def small_kernel(d_rows, r_rows, at_ref, small_ref, qd_ref, md_ref, qr_ref, mr_ref, gain_ref, vec_ref):
    def spread(row, q_ref, m_ref):
        value = dot(small_ref[:, row, :], q_ref[...])
        return jnp.sum(value * m_ref[...], axis=0, keepdims=True)

    for k in range(2):
        gain_ref[k : k + 1] = spread(k, qd_ref, md_ref)
    half = vec_ref.shape[1]
    for k in range(8):
        value = spread(2 + k, qr_ref, mr_ref)
        value = jnp.where(at_ref[3] == 0, value[:, :half], value[:, half:])
        if k == 7:
            soft = jnp.maximum(value, 0.0) + jnp.log1p(jnp.exp(-jnp.abs(value)))
            vec_ref[8:9] = -8.0 * jax.nn.sigmoid(value)
            value = 8.0 * soft
        vec_ref[k : k + 1] = value


def small_call(place, small, d_rows, r_rows):
    devices, _, span = small.shape
    operands = []
    for rows in (d_rows, r_rows):
        lane = np.arange(devices * rows)
        operands.append(jnp.asarray(lane[None] % rows == np.arange(span)[:, None], BF))
        operands.append(jnp.asarray(lane[None] // rows == np.arange(devices)[:, None], F32))
    whole = pl.BlockSpec(memory_space=pltpu.VMEM)
    return pl.pallas_call(
        functools.partial(small_kernel, d_rows, r_rows),
        in_specs=[pl.BlockSpec(memory_space=pltpu.SMEM)] + [whole] * 5,
        out_specs=[whole] * 2,
        out_shape=[shape_of((2, devices * d_rows), F32), shape_of((16, devices * r_rows // 2), F32)],
        compiler_params=params(24),
        cost_estimate=LIGHT,
        name="small_weights",
    )(place.where, small, *operands)


def norm_kernel(n_terms, row, *refs):
    terms, gain_ref, outs = refs[:n_terms], refs[n_terms], refs[n_terms + 1 :]
    value = functools.reduce(jnp.add, [t[...] for t in terms])
    scale = lax.rsqrt(jnp.mean(value * value, axis=-1, keepdims=True) + EPS)
    outs[0][...] = (value * scale * gain_ref[row : row + 1]).astype(BF)
    if n_terms > 1:
        outs[1][...] = value


def norm_call(terms, gains, row):
    tokens, model = terms[0].shape
    step = tokens // 4
    block = pl.BlockSpec((step, model), lambda j: (j, 0))
    shapes = [in_hbm((tokens, model), BF), shape_of((tokens, model), F32)]
    shapes = shapes[: 1 if len(terms) == 1 else 2]
    return pl.pallas_call(
        functools.partial(norm_kernel, len(terms), row),
        grid=(4,),
        in_specs=[block] * len(terms) + [full(gains.shape)],
        out_specs=[block] * len(shapes),
        out_shape=shapes,
        compiler_params=params(16),
        cost_estimate=LIGHT,
        name="norm",
    )(*terms, gains)


def norm_back_kernel(n_terms, row, low, *refs):
    terms = refs[:n_terms]
    value_ref, gain_ref, add_ref, out_ref = refs[n_terms : n_terms + 4]
    gain_out = refs[-1]
    grad = functools.reduce(jnp.add, [t[...] for t in terms])
    value = value_ref[...]
    scale = lax.rsqrt(jnp.mean(value * value, axis=-1, keepdims=True) + EPS)
    unit = value * scale
    inner = grad * gain_ref[row : row + 1]
    total = add_ref[...] + scale * (inner - unit * jnp.mean(inner * unit, axis=-1, keepdims=True))
    out_ref[...] = total
    if low:
        refs[n_terms + 4][...] = total.astype(BF)
    part = jnp.sum(grad * unit, axis=0, keepdims=True)

    @pl.when(pl.program_id(0) == 0)
    def _():
        gain_out[...] = part

    @pl.when(pl.program_id(0) > 0)
    def _():
        gain_out[...] += part


def norm_back_call(terms, value, gains, row, add, low):
    tokens, model = value.shape
    step = tokens // 4
    block = pl.BlockSpec((step, model), lambda j: (j, 0))
    shapes = [shape_of((tokens, model), F32)] + [in_hbm((tokens, model), BF)] * low
    return pl.pallas_call(
        functools.partial(norm_back_kernel, len(terms), row, low),
        grid=(4,),
        in_specs=[block] * len(terms) + [block, full(gains.shape), block],
        out_specs=[block] * len(shapes) + [full((1, model))],
        out_shape=shapes + [shape_of((1, model), F32)],
        compiler_params=params(16),
        cost_estimate=LIGHT,
        name="norm_back",
    )(*terms, value, gains, add)


def pack_kernel(at_ref, go_ref, gr_ref, gi_ref, gvec_ref, vec_ref, mine_ref, other_ref):
    pairs, rows, _ = mine_ref.shape
    model, block = go_ref.shape[1], gr_ref.shape[1]
    line = lax.broadcasted_iota(jnp.int32, gvec_ref.shape, 0)
    gvec = jnp.where(line == 7, gvec_ref[...] * vec_ref[8:9], gvec_ref[...]).astype(BF)
    slot = lax.broadcasted_iota(jnp.int32, (8, block), 0)
    lane = lax.broadcasted_iota(jnp.int32, (8, block), 1)
    turned = dot_tn(gvec, jnp.where(slot == lane, 1.0, 0.0).astype(BF)).astype(BF)
    gr, gi = gr_ref[...].astype(BF), gi_ref[...].astype(BF)
    for k in range(2):

        @pl.when(at_ref[3] == k)
        def _():
            for q in range(pairs):
                for ref, which in ((mine_ref, k), (other_ref, 1 - k)):
                    span = slice((2 * q + which) * rows, (2 * q + which + 1) * rows)
                    ref[q, :, 0:model] = go_ref[span]
                    ref[q, :, model : model + block] = gr[span]
                    ref[q, :, model + block : model + 2 * block] = gi[span]
                    ref[q, :, model + 2 * block :] = turned[span]


def pack_call(place, g_out, g_gate_r, g_gate_i, g_vec, vec, rows):
    width, model = g_out.shape
    block = g_gate_r.shape[1]
    shape = (width // (2 * rows), rows, model + 3 * block)
    whole = pl.BlockSpec(memory_space=pltpu.VMEM)
    return pl.pallas_call(
        pack_kernel,
        in_specs=[pl.BlockSpec(memory_space=pltpu.SMEM)] + [whole] * 5,
        out_specs=[whole] * 2,
        out_shape=[shape_of(shape, BF), shape_of(shape, BF)],
        compiler_params=params(24),
        cost_estimate=LIGHT,
        name="pack",
    )(place.where, g_out, g_gate_r, g_gate_i, g_vec, vec)


def forward_kernel(
    n_rows,
    group,
    block,
    n_in,
    n_branch,
    at_ref,
    mine_ref,
    other_ref,
    halo_ref,
    *refs,
):
    w_refs, wb_refs, refs = refs[:n_in], refs[n_in : n_in + n_branch], refs[n_in + n_branch :]
    vec_ref, mask_ref, gr_ref, gi_ref, first_ref, bpre_ref, mixer_ref, conv_ref = refs[:8]
    rpre_ref, ipre_ref, through_ref, local_ref, ends_ref, w_ref, wb_ref = refs[8:15]
    ext_ref, in_ref, branch_ref = refs[15:]
    half = mine_ref.shape[0]
    w_ref[...] = from_pieces(at_ref[2], 2, w_refs, in_ref)
    wb_ref[...] = from_pieces(at_ref[1], 1, wb_refs, branch_ref)

    @pl.when(pl.program_id(0) == 0)
    def _():
        first_ref[0:half] = mine_ref[...]
        first_ref[half : 2 * half] = other_ref[...]
        first_ref[2 * half :] = halo_ref[...]

    mixer = dot(first_ref[...], w_ref[...]).astype(BF)
    bpre_ref[...] = dot(first_ref[0 : 2 * half], wb_ref[...])
    mixer_ref[...] = mixer
    wide = mixer.astype(F32)
    tokens = n_rows * group
    for r in range(n_rows):
        ext_ref[r, 0:HALO] = wide[tokens + HALO * r : tokens + HALO * (r + 1)]
        ext_ref[r, HALO : HALO + group] = wide[r * group : (r + 1) * group]
    for r in range(n_rows):
        span = slice(r * group, (r + 1) * group)
        conv = vec_ref[4:5] + vec_ref[0:1] * ext_ref[r, HALO : HALO + group]
        for k in range(1, 4):
            conv += (
                vec_ref[k : k + 1]
                * ext_ref[r, HALO - k : HALO - k + group]
                * mask_ref[span, k : k + 1]
            )
        conv_ref[span] = conv.astype(BF)
    for h in range(w_ref.shape[1] // block):
        cols = slice(h * block, (h + 1) * block)
        low = conv_ref[:, cols]
        rpre_ref[:, cols] = dot(low, gr_ref[cols]) + vec_ref[5:6, cols]
        ipre_ref[:, cols] = dot(low, gi_ref[cols]) + vec_ref[6:7, cols]
        for r in range(n_rows):
            span = slice(r * group, (r + 1) * group)
            recur = jax.nn.sigmoid(rpre_ref[span, cols])
            admit = jax.nn.sigmoid(ipre_ref[span, cols])
            rate = vec_ref[7:8, cols] * recur
            reset = mask_ref[span, 0:1]
            decay = jnp.exp(-rate) * (1.0 - reset)
            scale = jnp.where(reset > 0.5, 1.0, jnp.sqrt(one_less_exp(2.0 * rate)))
            drive = scale * admit * conv_ref[span, cols].astype(F32)
            decay, drive = scan_tile(decay, drive, 1)
            through_ref[span, cols] = decay
            local_ref[span, cols] = drive
            ends_ref[r : r + 1, cols] = decay[group - 1 : group]
            ends_ref[n_rows + r : n_rows + r + 1, cols] = drive[group - 1 : group]


def forward_call(place, mine, other, halo, w_in, w_branch, vec, masks, gate_r, gate_i, n_rows, group, chip_d):
    model = mine.shape[1]
    length = 2 * mine.shape[0] + halo.shape[0]
    width, block = w_in[0].shape[-1], gate_r.shape[1]
    tokens = n_rows * group
    tile = TILE
    return pl.pallas_call(
        functools.partial(
            forward_kernel, n_rows, group, block, len(w_in), len(w_branch)
        ),
        grid=(width // tile,),
        in_specs=[
            pl.BlockSpec(memory_space=pltpu.SMEM),
            full(mine.shape),
            full(mine.shape),
            full(halo.shape),
            *piece_specs(w_in, chip_d),
            *piece_specs(w_branch, chip_d),
            columns(16),
            full(masks.shape),
            lines(tile, block),
            lines(tile, block),
        ],
        out_specs=[full((length, model)), columns(tokens), columns(length)]
        + [columns(tokens)] * 5
        + [columns(2 * n_rows), columns(model), columns(model)],
        out_shape=[
            in_hbm((length, model), BF),
            in_hbm((tokens, width), F32),
            in_hbm((length, width), BF),
            in_hbm((tokens, width), BF),
            in_hbm((tokens, width), F32),
            in_hbm((tokens, width), F32),
            in_hbm((tokens, width), F32),
            in_hbm((tokens, width), F32),
            in_hbm((2 * n_rows, width), F32),
            in_hbm((model, width), BF),
            in_hbm((model, width), BF),
        ],
        scratch_shapes=[
            pltpu.VMEM((n_rows, HALO + group, tile), F32),
            piece_scratch(place, w_in, chip_d),
            piece_scratch(place, w_branch, chip_d),
        ],
        compiler_params=params(24),
        cost_estimate=LIGHT,
        name="recurrence_forward",
    )(place.where, mine, other, halo, *w_in, *w_branch, vec, masks, gate_r, gate_i)


def mix_kernel(
    n_rows, group, local_ref, through_ref, enter_ref, bpre_ref, w_ref, state_ref, mixed_ref, part_ref, part_other_ref
):
    for r in range(n_rows):
        span = slice(r * group, (r + 1) * group)
        state = local_ref[span] + through_ref[span] * enter_ref[r : r + 1]
        state_ref[span] = state
        branch, _ = gelu_parts(bpre_ref[span])
        mixed_ref[span] = (state * branch).astype(BF)
    part = dot(mixed_ref[...], w_ref[...])
    half = part_ref.shape[0]

    @pl.when(pl.program_id(0) == 0)
    def _():
        part_ref[...] = part[:half]
        part_other_ref[...] = part[half:]

    @pl.when(pl.program_id(0) > 0)
    def _():
        part_ref[...] += part[:half]
        part_other_ref[...] += part[half:]


def mix_call(local, through, enter, branch_pre, w_out, n_rows, group):
    tokens, width = local.shape
    model = w_out.shape[1]
    return pl.pallas_call(
        functools.partial(mix_kernel, n_rows, group),
        grid=(width // TILE,),
        in_specs=[
            columns(tokens),
            columns(tokens),
            columns(n_rows),
            columns(tokens),
            lines(TILE, model),
        ],
        out_specs=[columns(tokens), columns(tokens)] + [full((tokens // 2, model))] * 2,
        out_shape=[
            in_hbm((tokens, width), F32),
            in_hbm((tokens, width), BF),
            shape_of((tokens // 2, model), F32),
            in_hbm((tokens // 2, model), F32),
        ],
        compiler_params=params(58),
        cost_estimate=LIGHT,
        name="mix",
    )(local, through, enter, branch_pre, w_out)


def part_kernel(hidden_ref, wd_ref, part_ref, part_other_ref):
    step = pl.program_id(0)
    half = part_ref.shape[0]
    part = dot(hidden_ref[...], wd_ref[...])

    @pl.when(step == 0)
    def _():
        part_ref[...] = part[:half]
        part_other_ref[...] = part[half:]

    @pl.when(step > 0)
    def _():
        part_ref[...] += part[:half]
        part_other_ref[...] += part[half:]


def part_call(hidden, w_down):
    tokens, width = hidden.shape
    model = w_down.shape[1]
    tile = 2 * TILE
    return pl.pallas_call(
        part_kernel,
        grid=(width // tile,),
        in_specs=[columns(tokens, tile), lines(tile, model)],
        out_specs=[full((tokens // 2, model))] * 2,
        out_shape=[in_hbm((tokens // 2, model), F32)] * 2,
        compiler_params=params(24),
        cost_estimate=LIGHT,
        name="feed_forward_out",
    )(hidden, w_down)


def ffn_kernel(
    sizes,
    rows,
    n_gate,
    n_up,
    at_ref,
    mine_ref,
    other_ref,
    low_mine_ref,
    low_other_ref,
    *refs,
):
    wg_refs, wu_refs, refs = refs[:n_gate], refs[n_gate : n_gate + n_up], refs[n_gate + n_up :]
    wd_ref, gg_send_ref, gg_ref, gu_send_ref, gu_ref, gd_ref, gd_other_ref = refs[:7]
    hidden_ref, back_ref, back_other_ref = refs[7:10]
    second_ref, low_ref, left_ref, right_ref, gate_ref, up_ref, down_ref = refs[10:]
    step = pl.program_id(0)
    half = mine_ref.shape[0]

    @pl.when(step == 0)
    def _():
        second_ref[0:half] = mine_ref[...]
        second_ref[half:] = other_ref[...]
        low_ref[0:half] = low_mine_ref[...]
        low_ref[half:] = low_other_ref[...]
        turn_rows("xyz", sizes, at_ref, second_ref[...], rows, left_ref)
        turn_rows("yxz", sizes, at_ref, second_ref[...], rows, right_ref)

    second, low = second_ref[...], low_ref[...]
    w_gate = from_pieces(at_ref[2], 2, wg_refs, gate_ref)
    w_up = from_pieces(at_ref[1], 1, wu_refs, up_ref)
    gate = dot(second, w_gate)
    up = dot(second, w_up)
    grad = dot_nt(low, wd_ref[...])
    active, slope = gelu_parts(gate)
    hidden = (active * up).astype(BF)
    gate_low = (grad * up * slope).astype(BF)
    up_low = (grad * active).astype(BF)
    sent = gg_send_ref.shape[0]
    gg = dot(left_ref[...], gate_low).astype(BF)
    gg_send_ref[...] = gg[:sent]
    gg_ref[...] = gg[sent:]
    sent = gu_send_ref.shape[0]
    gu = dot(right_ref[...], up_low).astype(BF)
    gu_send_ref[...] = gu[:sent]
    gu_ref[...] = gu[sent:]
    width = hidden.shape[1]
    down_ref[pl.ds(step * width, width)] = dot_tn(hidden, low).astype(BF)
    hidden_ref[...] = hidden
    back = dot_nt(gate_low, w_gate) + dot_nt(up_low, w_up)

    @pl.when(step == 0)
    def _():
        back_ref[...] = back[:half]
        back_other_ref[...] = back[half:]

    @pl.when(step > 0)
    def _():
        back_ref[...] += back[:half]
        back_other_ref[...] += back[half:]

    pairs, lines_down, _ = gd_ref.shape
    for k in range(2):

        @pl.when((step == pl.num_programs(0) - 1) & (at_ref[3] == k))
        def _():
            for q in range(pairs):
                at = 2 * q * lines_down
                near, far = at + k * lines_down, at + (1 - k) * lines_down
                gd_ref[q] = down_ref[near : near + lines_down]
                gd_other_ref[q] = down_ref[far : far + lines_down]


def ffn_call(place, mine, other, low_mine, low_other, w_gate, w_up, w_down, chip_d, f_rows):
    tokens, model = 2 * mine.shape[0], mine.shape[1]
    width = w_gate[0].shape[-1]
    tile = 2 * TILE
    sent_l, sent_r = model // place.size["x"], model // place.size["y"]
    down = (width // (2 * f_rows), f_rows, model)
    rows = [sent_l, model - sent_l, sent_r, model - sent_r]
    return pl.pallas_call(
        functools.partial(ffn_kernel, place.sizes, chip_d, len(w_gate), len(w_up)),
        grid=(width // tile,),
        in_specs=[
            pl.BlockSpec(memory_space=pltpu.SMEM),
            full((tokens // 2, model)),
            full((tokens // 2, model)),
            full((tokens // 2, model)),
            full((tokens // 2, model)),
            *piece_specs(w_gate, chip_d, tile),
            *piece_specs(w_up, chip_d, tile),
            lines(tile, model),
        ],
        out_specs=[columns(n, tile) for n in rows]
        + [full(down)] * 2
        + [columns(tokens, tile)]
        + [full((tokens // 2, model))] * 2,
        out_shape=[in_hbm((n, width), BF) for n in rows]
        + [shape_of(down, BF), in_hbm(down, BF)]
        + [in_hbm((tokens, width), BF)]
        + [shape_of((tokens // 2, model), F32), in_hbm((tokens // 2, model), F32)],
        scratch_shapes=[
            pltpu.VMEM((tokens, model), BF),
            pltpu.VMEM((tokens, model), BF),
            pltpu.VMEM((model, tokens), BF),
            pltpu.VMEM((model, tokens), BF),
            piece_scratch(place, w_gate, chip_d, tile),
            piece_scratch(place, w_up, chip_d, tile),
            pltpu.VMEM((width, model), BF),
        ],
        compiler_params=params(60),
        cost_estimate=LIGHT,
        name="feed_forward",
    )(place.where, mine, other, low_mine, low_other, *w_gate, *w_up, w_down)


def split_kernel(cuts, at_ref, whole_ref, *outs):
    for out, (low, high) in zip(outs, cuts):
        out[...] = whole_ref[:, low:high]


def split_call(place, whole, cuts):
    count, rows, width = whole.shape
    steps = 4
    step = count // (2 * steps)
    if any(n % 16 for cut in cuts for n in cut):
        half = lax.dynamic_slice_in_dim(whole, place.at["c"] * (count // 2), count // 2, 0)
        return [half[:, low:high].reshape(-1, width) for low, high in cuts]
    outs = pl.pallas_call(
        functools.partial(split_kernel, cuts),
        grid_spec=pltpu.PrefetchScalarGridSpec(
            num_scalar_prefetch=1,
            grid=(steps,),
            in_specs=[pl.BlockSpec((step, rows, width), lambda j, at: (at[3] * steps + j, 0, 0))],
            out_specs=[
                pl.BlockSpec((step, high - low, width), lambda j, at: (j, 0, 0))
                for low, high in cuts
            ],
        ),
        out_shape=[in_hbm((count // 2, high - low, width), BF) for low, high in cuts],
        compiler_params=params(58),
        cost_estimate=LIGHT,
        name="split",
    )(place.where, whole)
    return [out.reshape(-1, width) for out in outs]


def regroup_kernel(sizes, order_of, cuts, at_ref, mine_ref, got_ref, *outs):
    nz, ny, nx = sizes
    size = {"z": nz, "y": ny, "x": nx}
    spot = {"z": at_ref[0], "y": at_ref[1], "x": at_ref[2]}
    half = mine_ref.shape[0]
    for index, order in enumerate(order_of):
        send_ref, rest_ref = outs[2 * index], outs[2 * index + 1]
        span = slice(*cuts[index])
        for i0 in range(size[order[0]]):
            for i1 in range(size[order[1]]):
                for i2 in range(size[order[2]]):
                    place = {}
                    for axis, i in zip(order, (i0, i1, i2)):
                        n = size[axis]
                        place[axis] = lax.rem(spot[axis] + (n - 1 - i), n)
                    chip = (place["z"] * ny + place["y"]) * nx + place["x"]
                    here = lax.rem(chip, half)
                    own = lax.div(chip, half) == at_ref[3]
                    value = jnp.where(own, mine_ref[here][:, span], got_ref[here][:, span])
                    if i0 == 0:
                        send_ref[i1, i2] = value
                    else:
                        rest_ref[i0 - 1, i1, i2] = value


def regroup_call(place, mine, got, order_of, cuts):
    sizes = tuple(place.size[a] for a in "zyx")
    rows = mine.shape[1]
    shapes = []
    for order, (low, high) in zip(order_of, cuts):
        n0, n1, n2 = (place.size[a] for a in order)
        shapes.append((n1, n2, rows, high - low))
        shapes.append((n0 - 1, n1, n2, rows, high - low))
    whole = pl.BlockSpec(memory_space=pltpu.VMEM)
    outs = pl.pallas_call(
        functools.partial(regroup_kernel, sizes, order_of, cuts),
        in_specs=[pl.BlockSpec(memory_space=pltpu.SMEM), whole, whole],
        out_specs=[whole] * len(shapes),
        out_shape=[shape_of(shape, BF) for shape in shapes],
        compiler_params=params(24),
        cost_estimate=LIGHT,
        name="regroup",
    )(place.where, mine, got)
    return [
        [outs[2 * i]] + [outs[2 * i + 1][j] for j in range(shapes[2 * i + 1][0])]
        for i in range(len(order_of))
    ]


def decay_of(rpre, vec7, reset):
    recur = jax.nn.sigmoid(rpre)
    rate = vec7 * recur
    return recur, rate, jnp.exp(-rate) * (1.0 - reset)


def back_kernel(
    n_rows,
    group,
    mine_ref,
    other_ref,
    w_ref,
    bpre_ref,
    state_ref,
    rpre_ref,
    mixed_ref,
    vec_ref,
    mask_ref,
    right_ref,
    go_ref,
    gb_send_ref,
    gb_ref,
    gbl_ref,
    reach_ref,
    local_ref,
    ends_ref,
    low_ref,
    grad_ref,
):
    @pl.when(pl.program_id(0) == 0)
    def _():
        half = mine_ref.shape[0]
        low_ref[0:half] = mine_ref[...]
        low_ref[half:] = other_ref[...]

    low = low_ref[...]
    grad_ref[...] = dot_nt(low, w_ref[...])
    go_ref[...] = dot_tn(mixed_ref[...], low).astype(BF)
    half = w_ref.shape[0] // 2
    for h in range(2):
        cols = slice(h * half, (h + 1) * half)
        for r in range(n_rows):
            span = slice(r * group, (r + 1) * group)
            branch, slope = gelu_parts(bpre_ref[span, cols])
            grad = grad_ref[span, cols]
            gbl_ref[span, cols] = (grad * state_ref[span, cols] * slope).astype(BF)
            _, _, decay = decay_of(rpre_ref[span, cols], vec_ref[7:8, cols], mask_ref[span, 0:1])
            ahead = moved(decay, -1, 1.0)
            reach, local = scan_tile(ahead, grad * branch, -1)
            reach_ref[span, cols] = reach
            local_ref[span, cols] = local
            ends_ref[r : r + 1, cols] = decay[0:1] * reach[0:1]
            ends_ref[n_rows + r : n_rows + r + 1, cols] = decay[0:1] * local[0:1]
    sent = gb_send_ref.shape[0]
    gb = dot(right_ref[:, 0 : gbl_ref.shape[0]], gbl_ref[...]).astype(BF)
    gb_send_ref[...] = gb[:sent]
    gb_ref[...] = gb[sent:]


def back_call(place, mine, other, w_out, branch_pre, state, rpre, mixed, vec, masks, right, n_rows, group):
    model, length = right.shape
    tokens = state.shape[0]
    sent = model // place.size["y"]
    width = w_out.shape[0]
    return pl.pallas_call(
        functools.partial(back_kernel, n_rows, group),
        grid=(width // TILE,),
        in_specs=[
            full((tokens // 2, model)),
            full((tokens // 2, model)),
            lines(TILE, model),
            columns(tokens),
            columns(tokens),
            columns(tokens),
            columns(tokens),
            columns(16),
            full(masks.shape),
            full((model, length)),
        ],
        out_specs=[
            lines(TILE, model),
            columns(sent),
            columns(model - sent),
            columns(tokens),
            columns(tokens),
            columns(tokens),
            columns(2 * n_rows),
        ],
        out_shape=[
            shape_of((width, model), BF),
            in_hbm((sent, width), BF),
            in_hbm((model - sent, width), BF),
            shape_of((tokens, width), BF),
            shape_of((tokens, width), F32),
            shape_of((tokens, width), F32),
            shape_of((2 * n_rows, width), F32),
        ],
        scratch_shapes=[pltpu.VMEM((tokens, model), BF), pltpu.VMEM((tokens, TILE), F32)],
        compiler_params=params(32),
        cost_estimate=LIGHT,
        name="recurrence_back",
    )(mine, other, w_out, branch_pre, state, rpre, mixed, vec, masks, right)


def gates_kernel(
    n_rows,
    group,
    block,
    reach_ref,
    local_ref,
    leave_ref,
    state_ref,
    enter_ref,
    rpre_ref,
    ipre_ref,
    conv_ref,
    mixer_ref,
    vec_ref,
    mask_ref,
    gr_ref,
    gi_ref,
    left_ref,
    gin_send_ref,
    gin_ref,
    ggr_ref,
    ggi_ref,
    gvec_ref,
    gm_ref,
    rlow_ref,
    ilow_ref,
    gconv_ref,
    ext_ref,
    spread_ref,
):
    tokens = n_rows * group

    gvec_ref[...] = jnp.zeros_like(gvec_ref)
    for h in range(conv_ref.shape[1] // block):
        cols = slice(h * block, (h + 1) * block)
        for r in range(n_rows):
            span = slice(r * group, (r + 1) * group)
            adjoint = local_ref[span, cols] + reach_ref[span, cols] * leave_ref[r : r + 1, cols]
            state = state_ref[span, cols]
            at = lax.broadcasted_iota(jnp.int32, state.shape, 0)
            before = jnp.where(at == 0, enter_ref[r : r + 1, cols], pltpu.roll(state, 1, 0))
            reset = mask_ref[span, 0:1]
            live = 1.0 - reset
            recur, rate, decay = decay_of(rpre_ref[span, cols], vec_ref[7:8, cols], reset)
            admit = jax.nn.sigmoid(ipre_ref[span, cols])
            full_decay = jnp.exp(-rate)
            root = jnp.sqrt(one_less_exp(2.0 * rate))
            scale = jnp.where(reset > 0.5, 1.0, root)
            conv = conv_ref[span, cols].astype(F32)
            direct = adjoint * scale
            gadmit = direct * conv
            gconv_ref[span, cols] = direct * admit
            gscale = adjoint * admit * conv
            glog = live * full_decay * (adjoint * before - gscale * full_decay / root)
            gvec_ref[7:8, cols] += jnp.sum(glog * recur, axis=0, keepdims=True)
            grecur = -(vec_ref[7:8, cols] * glog) * recur * (1.0 - recur)
            ginput = gadmit * admit * (1.0 - admit)
            rlow, ilow = grecur.astype(BF), ginput.astype(BF)
            rlow_ref[span, cols] = rlow
            ilow_ref[span, cols] = ilow
            gvec_ref[5:6, cols] += jnp.sum(rlow.astype(F32), axis=0, keepdims=True)
            gvec_ref[6:7, cols] += jnp.sum(ilow.astype(F32), axis=0, keepdims=True)
        rlow, ilow = rlow_ref[:, cols], ilow_ref[:, cols]
        low = conv_ref[:, cols]
        ggr_ref[cols] = dot_tn(low, rlow)
        ggi_ref[cols] = dot_tn(low, ilow)
        gconv_ref[:, cols] += dot_nt(rlow, gr_ref[cols]) + dot_nt(ilow, gi_ref[cols])
        for r in range(n_rows):
            span = slice(r * group, (r + 1) * group)
            head = slice(tokens + HALO * r, tokens + HALO * (r + 1))
            ext_ref[0:HALO] = mixer_ref[head, cols].astype(F32)
            ext_ref[HALO : HALO + group] = mixer_ref[span, cols].astype(F32)
            gconv = gconv_ref[span, cols]
            gvec_ref[4:5, cols] += jnp.sum(gconv, axis=0, keepdims=True)
            gvec_ref[0:1, cols] += jnp.sum(
                gconv * ext_ref[HALO : HALO + group], axis=0, keepdims=True
            )
            spread_ref[0:HALO] = jnp.zeros((HALO, block), F32)
            spread_ref[HALO : HALO + group] = vec_ref[0:1, cols] * gconv
            for k in range(1, 4):
                masked = gconv * mask_ref[span, k : k + 1]
                there = slice(HALO - k, HALO - k + group)
                gvec_ref[k : k + 1, cols] += jnp.sum(
                    masked * ext_ref[there], axis=0, keepdims=True
                )
                spread_ref[there] += vec_ref[k : k + 1, cols] * masked
            gm_ref[head, cols] = spread_ref[0:HALO].astype(BF)
            gm_ref[span, cols] = spread_ref[HALO : HALO + group].astype(BF)
    gm = gm_ref[...]
    sent = gin_send_ref.shape[0]
    gin = dot(left_ref[...], gm).astype(BF)
    gin_send_ref[...] = gin[:sent]
    gin_ref[...] = gin[sent:]


def first_kernel(gm_ref, gbl_ref, win_ref, wbr_ref, gfirst_ref):
    step = pl.program_id(0)
    tokens = gbl_ref.shape[0]
    gm = gm_ref[...]
    part = dot_nt(gm, win_ref[...])
    part_branch = dot_nt(gbl_ref[...], wbr_ref[...])

    @pl.when(step == 0)
    def _():
        gfirst_ref[...] = part

    @pl.when(step > 0)
    def _():
        gfirst_ref[...] += part

    gfirst_ref[0:tokens] += part_branch


def gates_call(
    place, reach, local, leave, state, enter, rpre, ipre, conv, mixer, vec, masks, gate_r, gate_i, left, n_rows, group
):
    model, length = left.shape
    sent = model // place.size["x"]
    tokens, width = state.shape
    block = gate_r.shape[1]
    tile = TILE
    return pl.pallas_call(
        functools.partial(gates_kernel, n_rows, group, block),
        grid=(width // tile,),
        in_specs=[
            columns(tokens),
            columns(tokens),
            columns(n_rows),
            columns(tokens),
            columns(n_rows),
            columns(tokens),
            columns(tokens),
            columns(tokens),
            columns(length),
            columns(16),
            full(masks.shape),
            lines(tile, block),
            lines(tile, block),
            full((model, length)),
        ],
        out_specs=[
            columns(sent),
            columns(model - sent),
            lines(tile, block),
            lines(tile, block),
            columns(8),
            columns(length),
        ],
        out_shape=[
            in_hbm((sent, width), BF),
            in_hbm((model - sent, width), BF),
            shape_of((width, block), F32),
            shape_of((width, block), F32),
            shape_of((8, width), F32),
            in_hbm((length, width), BF),
        ],
        scratch_shapes=[
            pltpu.VMEM((tokens, tile), BF),
            pltpu.VMEM((tokens, tile), BF),
            pltpu.VMEM((tokens, tile), F32),
            pltpu.VMEM((HALO + group, block), F32),
            pltpu.VMEM((HALO + group, block), F32),
        ],
        compiler_params=params(40),
        cost_estimate=LIGHT,
        name="recurrence_gates",
    )(reach, local, leave, state, enter, rpre, ipre, conv, mixer, vec, masks, gate_r, gate_i, left)


def first_call(gm, gbl, w_in, w_branch):
    length, width = gm.shape
    model = w_in.shape[0]
    return pl.pallas_call(
        first_kernel,
        grid=(width // TILE,),
        in_specs=[columns(length), columns(gbl.shape[0]), columns(model), columns(model)],
        out_specs=full((length, model)),
        out_shape=shape_of((length, model), F32),
        compiler_params=params(24),
        cost_estimate=LIGHT,
        name="first_gradient",
    )(gm, gbl, w_in, w_branch)


def normed(values, gain):
    return values * lax.rsqrt(jnp.mean(values * values, axis=-1, keepdims=True) + EPS) * gain


def halves(value, place, dim):
    half = value.shape[dim] // 2
    mine = lax.dynamic_slice_in_dim(value, place.at["c"] * half, half, dim)
    other = lax.dynamic_slice_in_dim(value, (1 - place.at["c"]) * half, half, dim)
    return mine, other


def own_channels(place, value):
    mine, other = halves(value, place, 0)
    got = place.ring(other, "c", 1)
    pair = place.ordered(mine, got)
    both = jnp.stack(pair, axis=1)
    return both.reshape(-1, both.shape[-1])


def own_devices(place, value, rows):
    shaped = value.reshape(place.chips // 2, 2, rows, value.shape[-1])
    mine = lax.dynamic_index_in_dim(shaped, place.at["c"], 1, keepdims=False)
    other = lax.dynamic_index_in_dim(shaped, 1 - place.at["c"], 1, keepdims=False)
    got = place.ring(other, "c", 1)
    return jnp.concatenate(place.ordered(mine, got), axis=0)


def on_device(
    inputs,
    cotangent,
    segments,
    norm1_gain,
    input_proj,
    branch_proj,
    conv_weight,
    conv_bias,
    recur_gate,
    input_gate,
    recur_bias,
    input_bias,
    decay_param,
    output_proj,
    norm2_gain,
    mlp_gate,
    mlp_up,
    mlp_down,
):
    place = Place()
    core = place.at["c"]
    chips = place.chips
    rows_dev, group, model = inputs.shape
    n_rows = 2 * rows_dev
    tokens_dev = rows_dev * group
    tokens = 2 * tokens_dev
    d_rows, lru = input_proj.shape
    ffn = mlp_gate.shape[1]
    r_rows, block = recur_gate.shape
    f_rows = mlp_down.shape[0]
    lru_half, ffn_half = lru // 2, ffn // 2
    pair = lambda value: place.ring(value, "c", 1)

    order = Order(place)
    lead = (place.size["z"], place.size["y"], place.size["x"])

    wide = [halves(w, place, 1) for w in (input_proj, branch_proj, mlp_gate, mlp_up)]
    got_a = order.ring(jnp.concatenate([w[1] for w in wide[:2]], axis=1), "c")
    got_c = order.ring(jnp.concatenate([w[1] for w in wide[2:]], axis=1), "c")
    span = max(d_rows, r_rows)
    lines_one = [
        jnp.pad(v, (0, span - v.shape[0]))[None]
        for v in (norm1_gain, norm2_gain, conv_bias, recur_bias, input_bias, decay_param)
    ]
    taps = jnp.pad(conv_weight, ((0, 0), (0, span - r_rows)))
    vectors = jnp.concatenate(lines_one[:2] + [taps] + lines_one[2:], axis=0)
    small = Gather(order, vectors[None, None, None, None], "y", 1)
    ids_pair = order.ring(segments, "c")
    mine_a = jnp.concatenate([w[0] for w in wide[:2]], axis=1)
    mine_c = jnp.concatenate([w[0] for w in wide[2:]], axis=1)
    gates = jnp.concatenate([recur_gate, input_gate], axis=0)
    gate_lines = 2 * r_rows * block // lru
    gates = gates.reshape(-1, gate_lines, block).transpose(1, 0, 2).reshape(gate_lines, lru)
    order.must(gates, mine_a)
    small = Gather(order, small.done(), "x", 2)
    got_a = order.wait(got_a)
    rows_a = jnp.concatenate(place.ordered(mine_a, got_a), axis=0)
    group_a = jnp.concatenate([rows_a, gates], axis=0)[None, None, None]
    order.must(group_a)
    both_whole = jnp.concatenate([output_proj, mlp_down], axis=0)
    both_whole = lax.all_gather(both_whole, AXES, axis=0)
    small = Gather(order, small.done(), "c", 3)
    small = Gather(order, small.done(), "z", 0, direct=True)

    a_z = Gather(order, group_a, "z", 0, direct=True)
    grad_out = cotangent.reshape(tokens_dev, model)
    low = grad_out.astype(BF)
    low_other = order.ring(low, "c")
    ids_pair, got_c = order.wait(ids_pair, got_c)
    ids = jnp.concatenate([segments, ids_pair], axis=0)
    prior_ids = order.along(ids[:, group - 3 :], 1)
    gains, vec = small_call(
        place, small.done().reshape(2 * chips, -1, span), d_rows, r_rows
    )
    flat = inputs.reshape(tokens_dev, model)
    (first,) = norm_call([flat], gains, 0)
    first_other = order.ring(first, "c")
    group_c = jnp.concatenate(place.ordered(mine_c, got_c), axis=0)[None, None, None]
    first_other, low_other = order.wait(first_other, low_other)
    tail = jnp.concatenate(
        [v.reshape(rows_dev, group, model)[:, group - 3 :] for v in (first, first_other)], axis=0
    )
    halo = order.along(tail, 1)
    c_z = Gather(order, group_c, "z", 0, both=True)
    a_z = a_z.done()
    halo, prior_ids = order.wait(halo, prior_ids)

    a_left = Gather(order, a_z[..., :lru_half], "y", 1)
    a_right = Gather(order, a_z[..., lru_half:], "x", 2)
    a_left, a_right = a_left.done(), a_right.done()

    a_left = Gather(order, a_left, "x", 2)
    a_right = Gather(order, a_right, "y", 1)
    c_z.next()
    a_left.arrived()
    a_right.arrived()

    chip_d = 2 * d_rows
    packed = [g.whole([p[..., chip_d:, :] for p in g.pieces]) for g in (a_left, a_right)]
    packed = jnp.concatenate(packed, axis=-1)
    packed = packed.reshape(chips, gate_lines, -1, block)
    packed = packed.transpose(0, 2, 1, 3).reshape(chips, 2, r_rows, block)
    packed = jnp.concatenate([packed[:, 0], packed[:, 1]], axis=-1)
    gate_mine, gate_other = halves(packed, place, 0)
    gate_got = order.ring(gate_other, "c")
    c_z = c_z.done()
    c_left = Gather(order, c_z[..., :ffn_half], "y", 1)
    c_right = Gather(order, c_z[..., ffn_half:], "x", 2)
    halo = jnp.pad(halo, ((0, 0), (HALO - 3, 0), (0, 0))).reshape(n_rows * HALO, model)
    position = place.s * group + jnp.arange(group, dtype=jnp.int32)
    joined_ids = jnp.concatenate([prior_ids, ids], axis=1)
    marks = [(joined_ids[:, 2 : 2 + group] != ids) | (position == 0)[None, :]]
    for k in range(1, 4):
        marks.append(
            (joined_ids[:, 3 - k : 3 - k + group] == ids) & (position >= k)[None, :]
        )
    masks = jnp.stack(marks, axis=-1).astype(F32).reshape(tokens, 4)
    masks = jnp.pad(masks, ((0, 0), (0, 4)))
    gate_got = order.wait(gate_got)
    packed = jnp.stack(place.ordered(gate_mine, gate_got), axis=1).reshape(-1, 2 * block)
    gate_r, gate_i = packed[:, :block], packed[:, block:]
    first_ext, branch_pre, mixer, conv, rpre, ipre, through, local, ends, w_in, w_branch = forward_call(
        place, first, first_other, halo, a_left.weight(chip_d), a_right.weight(chip_d), vec, masks, gate_r, gate_i, n_rows, group, chip_d
    )
    enter = Carry(order, ends, 1)
    more = enter.next()
    c_left, c_right = c_left.done(), c_right.done()

    c_left = Gather(order, c_left, "x", 2)
    c_right = Gather(order, c_right, "y", 1)
    both_whole = order.wait(both_whole)
    w_out, w_down = split_call(
        place, both_whole, ((0, r_rows), (r_rows, r_rows + f_rows))
    )
    order.must(w_out, w_down)
    enter = enter.done() if more else enter.total[4:]
    state, mixed, part, part_other = mix_call(
        local, through, enter, branch_pre, w_out, n_rows, group
    )
    part_pair = order.ring(part_other, "c")
    first_l, first_r = turn_call(place, order.tie(first_ext), chip_d)
    order.must(first_l, first_r)
    w_gate, w_up = c_left.weight(chip_d), c_right.weight(chip_d)
    part_pair = order.wait(part_pair)
    second, middle = norm_call([flat, part, part_pair], gains, 1)
    second_other = order.ring(second, "c")
    second_other = order.wait(second_other)

    nz, ny, nx = lead

    def blocks_of(send, rest, axis, other):
        shape = (place.size[other], nz, chip_d, -1)
        rest = rest.reshape((place.size[axis] - 1,) + shape)
        return [send.reshape(shape)] + [rest[i] for i in range(rest.shape[0])]

    def joined(left, right):
        return [jnp.concatenate(p, axis=-1) for p in zip(left.done(nz), right.done(nz))]

    g_send, g_rest, u_send, u_rest, down_mine, down_other, hidden, back, back_other = ffn_call(
        place, second, second_other, low, low_other, w_gate, w_up, w_down, chip_d, f_rows
    )

    back_pair = order.ring(back_other, "c")
    g_left = Scatter(order, blocks_of(g_send, g_rest, "x", "y"), "x")
    g_right = Scatter(order, blocks_of(u_send, u_rest, "y", "x"), "y")
    down_got = order.ring(down_other, "c")
    back_pair = order.wait(back_pair)
    grad_middle, mid_low, grad_gain_two = norm_back_call(
        [back, back_pair], middle, gains, 1, grad_out, 1
    )
    mid_pair = order.ring(mid_low, "c")
    down_got = order.wait(down_got)
    (d_z,) = regroup_call(place, down_mine, down_got, ("zyx",), ((0, model),))
    d_z = Scatter(order, d_z, "z")
    mid_other = order.wait(mid_pair)
    g_out, b_send, b_rest, gbl, reach, local_back, ends_back = back_call(
        place, mid_low, mid_other, w_out, branch_pre, state, rpre, mixed, vec, masks, first_r, n_rows, group
    )
    part, part_other = part_call(order.tie(hidden), w_down)
    order.must(part)
    d_z.take()
    leave = Carry(order, ends_back, -1)
    g_left.next()
    g_right.next()
    more = leave.next()

    g_left = Scatter(order, g_left.done(ny), "y")
    g_right = Scatter(order, g_right.done(nx), "x")
    leave = leave.done() if more else leave.total[4:]
    d_z.next()
    in_send, in_rest, g_gate_r, g_gate_i, g_vec, gm = gates_call(
        place, reach, local_back, leave, state, enter, rpre, ipre, conv, mixer, vec, masks, gate_r, gate_i, first_l, n_rows, group
    )
    order.must(in_send)
    g_left.next()
    g_right.next()

    a_left = Scatter(order, blocks_of(in_send, in_rest, "x", "y"), "x")
    a_right = Scatter(order, blocks_of(b_send, b_rest, "y", "x"), "y")
    d_z.take()
    out_mine, out_other = pack_call(place, g_out, g_gate_r, g_gate_i, g_vec, vec, r_rows)
    out_got = order.ring(out_other, "c")
    out_got = order.wait(out_got)
    wide_r = out_mine.shape[-1]
    cut = (wide_r // (2 * block)) * block
    o_left, o_right = regroup_call(
        place, out_mine, out_got, ("xyz", "yxz"), ((0, cut), (cut, wide_r))
    )
    d_z.next()
    grad_first = first_call(order.tie(gm), gbl, w_in, w_branch)
    order.must(grad_first)
    g_both = Scatter(order, joined(g_left, g_right), "z")
    order.must(o_left[0], o_right[0])
    a_left.next()
    a_right.next()

    a_left = Scatter(order, a_left.done(ny), "y")
    a_right = Scatter(order, a_right.done(nx), "x")
    o_left = Scatter(order, o_left, "x")
    o_right = Scatter(order, o_right, "y")
    d_z.take()
    g_both.next()
    spill = grad_first[tokens:].reshape(n_rows, HALO, model)[:, HALO - 3 :]
    spill = order.along(spill, -1)
    a_left.next()
    a_right.next()
    o_left.next()
    o_right.next()

    a_both = Scatter(order, joined(a_left, a_right), "z", both=True)
    o_left = Scatter(order, o_left.done(ny), "y")
    o_right = Scatter(order, o_right.done(nx), "x")
    spill = order.wait(spill)
    spill = jnp.pad(spill, ((0, 0), (group - 3, 0), (0, 0))).reshape(tokens, model)
    grad_first = grad_first[:tokens] + spill
    first_pair = order.ring(grad_first[tokens_dev:], "c")
    first_pair = order.wait(first_pair)
    grad_inputs, grad_gain_one = norm_back_call(
        [grad_first[:tokens_dev], first_pair], flat, gains, 0, grad_middle, 0
    )
    order.must(grad_inputs)
    g_both.next()
    d_x = Scatter(order, d_z.done(ny), "y")
    a_both.next()
    o_left.next()
    o_right.next()
    d_x.next()

    o_both = Scatter(order, joined(o_left, o_right), "z", both=True)
    d_y = Scatter(order, d_x.done(nx), "x")
    g_gains = jnp.concatenate([grad_gain_one, grad_gain_two], axis=0)
    g_gains = jnp.transpose(g_gains.reshape(2, chips, 2, d_rows), (1, 2, 0, 3))
    g_gains = g_gains.reshape(lead + (2, 2 * d_rows))
    g_gains = jnp.moveaxis(behind(place, "yxz", g_gains), 3, 0)
    gains_mine = lax.dynamic_index_in_dim(g_gains, core, 0, False)
    gains_got = order.ring(lax.dynamic_index_in_dim(g_gains, 1 - core, 0, False), "c")
    part_pair = order.ring(part_other, "c")

    def whole_columns(value):
        mine, other = halves(value, place, 0)
        return mine, order.ring(other, "c")

    gains_got, part_pair = order.wait(gains_got, part_pair)
    result = middle + (part + part_pair)
    order.must(result)
    g_gains = gains_mine + gains_got
    g_gains = Scatter(order, [g_gains[i] for i in range(ny)], "y", between=F32)
    a_both.next()
    sum_c = whole_columns(g_both.done(dtype=F32))
    g_gains = Scatter(order, g_gains.done(nx, F32), "x", between=F32)
    o_both.next()
    sum_down = d_y.done(dtype=F32)
    order.must(sum_down)
    g_gains = Scatter(order, g_gains.done(nz, F32), "z", direct=True, between=F32)
    low_c, high_c = place.ordered(sum_c[0], order.wait(sum_c[1]))
    grad_gate = jnp.concatenate([low_c[:, :ffn_half], high_c[:, :ffn_half]], axis=1)
    grad_up = jnp.concatenate([low_c[:, ffn_half:], high_c[:, ffn_half:]], axis=1)
    order.must(grad_gate, grad_up)
    sum_a = whole_columns(a_both.done(dtype=F32))
    o_both.next()
    low_a, high_a = place.ordered(sum_a[0], order.wait(sum_a[1]))
    grad_input_proj = jnp.concatenate([low_a[:, :lru_half], high_a[:, :lru_half]], axis=1)
    grad_branch_proj = jnp.concatenate([low_a[:, lru_half:], high_a[:, lru_half:]], axis=1)
    order.must(grad_input_proj, grad_branch_proj)
    own = o_both.done(dtype=F32)
    g_gains = g_gains.done(dtype=F32).reshape(2, d_rows)
    own_gates = own[:, model : model + 2 * block]
    own_vec = own[:, model + 2 * block : model + 2 * block + 8].T
    return (
        result.reshape(inputs.shape),
        grad_inputs.reshape(inputs.shape),
        g_gains[0],
        grad_input_proj,
        grad_branch_proj,
        own_vec[:4],
        own_vec[4],
        own_gates[:, :block],
        own_gates[:, block:],
        own_vec[5],
        own_vec[6],
        own_vec[7],
        own[:, :model],
        g_gains[1],
        grad_gate,
        grad_up,
        sum_down,
    )


def solution(mesh):
    seq, row = mesh.shape["seq"], mesh.shape["row"]
    ny = 1 << ((seq.bit_length() - 1) // 2)
    grid = Mesh(mesh.devices.reshape(seq // ny, ny, row // 2, 2), AXES)
    tokens, line, flat, taps = P(("x", "c"), ("z", "y"), None), P(AXES, None), P(AXES), P(None, AXES)
    in_specs = (
        tokens,
        tokens,
        P(("x", "c"), ("z", "y")),
        flat,
        line,
        line,
        taps,
        flat,
        line,
        line,
        flat,
        flat,
        flat,
        line,
        flat,
        line,
        line,
        line,
    )
    out_specs = (
        tokens,
        tokens,
        flat,
        line,
        line,
        taps,
        flat,
        line,
        line,
        flat,
        flat,
        flat,
        line,
        flat,
        line,
        line,
        line,
    )
    return jax.shard_map(
        on_device, mesh=grid, in_specs=in_specs, out_specs=out_specs, check_vma=False
    )
```
